128 devices in a mesh: fsdp: 8 (over y, z_hi), ctx: 16 (over x, z_lo, core).
Axes of the slice: x: 4, y: 4, z: 4 (z_hi: 2, z_lo: 2; z = z_hi * 2 + z_lo), core: 2. Of those that a mesh axis runs over, the one named last changes fastest.
Arguments:
- tokens: bfloat16 [16384, 2048], P(('fsdp', 'ctx')), may hold values from -6 to 6
- out_grad: bfloat16 [16384, 2048], P(('fsdp', 'ctx')), may hold values from -6 to 6
- seq_lengths: int32 [8, 2], P('fsdp'), may hold values from 1 to 1792, as said below
- span_order: int32 [32], replicated, may hold values from 0 to 31, as said below
- attn_in: float32 [2048, 2560], P(('fsdp', 'ctx')), may hold values from -0.125 to 0.125
- attn_out: float32 [2048, 2048], P(('fsdp', 'ctx')), may hold values from -1.5 to 1.5
- gate_up: float32 [2048, 11264], P(('fsdp', 'ctx')), may hold values from -0.125 to 0.125
- down_proj: float32 [5632, 2048], P(('fsdp', 'ctx')), may hold values from -0.078125 to 0.078125
- norm_gains: float32 [2, 2048], P(None, ('fsdp', 'ctx')), may hold values from 0.5 to 1.5
- first_attn_in: float32 [2048, 2560], P(('fsdp', 'ctx')), may hold values from -128 to 128
- second_attn_in: float32 [2048, 2560], P(('fsdp', 'ctx')), may hold values from 983.04 to 6553.6
- first_attn_out: float32 [2048, 2048], P(('fsdp', 'ctx')), may hold values from -6 to 6
- second_attn_out: float32 [2048, 2048], P(('fsdp', 'ctx')), may hold values from 12.288 to 81.92
- first_gate_up: float32 [2048, 11264], P(('fsdp', 'ctx')), may hold values from -24 to 24
- second_gate_up: float32 [2048, 11264], P(('fsdp', 'ctx')), may hold values from 44.2368 to 294.912
- first_down_proj: float32 [5632, 2048], P(('fsdp', 'ctx')), may hold values from -48 to 48
- second_down_proj: float32 [5632, 2048], P(('fsdp', 'ctx')), may hold values from 180.224 to 1179.648
- first_norm_gains: float32 [2, 2048], P(None, ('fsdp', 'ctx')), may hold values from -80 to 80
- second_norm_gains: float32 [2, 2048], P(None, ('fsdp', 'ctx')), may hold values from 491.52 to 3276.8
Outputs:
- block_out: bfloat16 [16384, 2048], P(('fsdp', 'ctx'))
- in_grad: bfloat16 [16384, 2048], P(('fsdp', 'ctx'))
- first_attn_in_next: float32 [2048, 2560], P(('fsdp', 'ctx'))
- second_attn_in_next: float32 [2048, 2560], P(('fsdp', 'ctx'))
- attn_in_next: float32 [2048, 2560], P(('fsdp', 'ctx'))
- first_attn_out_next: float32 [2048, 2048], P(('fsdp', 'ctx'))
- second_attn_out_next: float32 [2048, 2048], P(('fsdp', 'ctx'))
- attn_out_next: float32 [2048, 2048], P(('fsdp', 'ctx'))
- first_gate_up_next: float32 [2048, 11264], P(('fsdp', 'ctx'))
- second_gate_up_next: float32 [2048, 11264], P(('fsdp', 'ctx'))
- gate_up_next: float32 [2048, 11264], P(('fsdp', 'ctx'))
- first_down_proj_next: float32 [5632, 2048], P(('fsdp', 'ctx'))
- second_down_proj_next: float32 [5632, 2048], P(('fsdp', 'ctx'))
- down_proj_next: float32 [5632, 2048], P(('fsdp', 'ctx'))
- first_norm_gains_next: float32 [2, 2048], P(None, ('fsdp', 'ctx'))
- second_norm_gains_next: float32 [2, 2048], P(None, ('fsdp', 'ctx'))
- norm_gains_next: float32 [2, 2048], P(None, ('fsdp', 'ctx'))
The draws below stay inside these ranges and needn't reach their ends.
Inputs may be any that keep to these rules, and one draw needn't show every extreme that they name: `seq_lengths`: row g lists the lengths of the 2 sequences of group g, laid end to end from position 0; the first is at least 1024 and in some group exactly 1792; a group's lengths sum to at most 2048, slots after them are unused. `span_order`: entry 2 c is a block from 0 to 15 and entry 2 c + 1 a block from 16 to 31; every block appears once. Block b holds positions b * 64 up to (b + 1) * 64 - 1.
All inputs are finite; a program needn't handle non-finite values.
Results may differ from the reference program's by a relative error of at most 0.035.
Values may be sent and summed in bfloat16 or wider, within the bound.
No kernel may reach another device: no remote copies, remote signals or barrier semaphores. Data moves between devices by JAX's collectives and lax.ppermute only.
A program may use at most 448 MiB of HBM per device.

```python
import math
import jax
import jax.numpy as jnp
from jax import lax

D = 2048
FF = 5632
HEADS = 32
KV_HEADS = 4
HEAD_DIM = 64
TOK_DEV = 128
SEQS = 2
STEP = 10
QDIM = 2048
KVDIM = 256
QKV = 2560
SLOTS = 2048
GROUPS = 8
SPANS = 32
TOKENS = 16384


def draw_seq_lengths(key, part):
    key = jax.random.fold_in(key, 11)
    key_cut, key_pick, key_fill = jax.random.split(key, 3)
    shortfall = jax.random.randint(key_cut, (GROUPS,), SLOTS // 8, SLOTS // 2 + 1)
    chosen = jax.random.randint(key_pick, (), 0, GROUPS)
    shortfall = jnp.where(jnp.arange(GROUPS) == chosen, SLOTS // 8, shortfall)
    longest = SLOTS - shortfall
    filler = jax.random.randint(key_fill, (GROUPS,), 0, 1 << 20)
    second = 1 + filler % shortfall
    return jnp.stack([longest, second], axis=1).astype(jnp.int32)


def draw_span_order(key, part):
    key = jax.random.fold_in(key, 23)
    key_early, key_late = jax.random.split(key)
    early_half = jax.random.permutation(key_early, SPANS // 2)
    late_half = jax.random.permutation(key_late, SPANS // 2) + SPANS // 2
    return jnp.stack([early_half, late_half], axis=1).reshape(SPANS).astype(jnp.int32)


def steps_of(stream_key, dims, cuts, least, high):
    loudness = 1.0
    for dim, parts in cuts:
        steps = jax.random.uniform(jax.random.fold_in(jax.random.fold_in(stream_key, 6), dim), (parts,), jnp.float32, least / len(cuts), high / len(cuts))
        loudness = loudness * jnp.repeat(jnp.exp(steps), dims[dim] // parts).reshape((-1,) + (1,) * (len(dims) - 1 - dim))
    return loudness


def scatter_about(key, dims, width, reach, cuts=(), kind=jnp.bfloat16):
    gain = steps_of(key, dims, cuts, -0.22, 0.18) if cuts else 1.0
    entries = jax.random.normal(key, dims, jnp.float32) * width * gain
    return jnp.minimum(jnp.maximum(entries, -reach), reach).astype(kind)


def setup_inputs(seed: int = 0) -> dict:
    splits = jax.random.split(jax.random.key(seed), 20)
    tokens = scatter_about(splits[0], (TOKENS, D), 1.0, 6.0, ((0, 128),))
    out_grad = scatter_about(splits[1], (TOKENS, D), 1.0, 6.0, ((0, 128),))
    seq_lengths = draw_seq_lengths(jax.random.fold_in(splits[19], 71), 0)
    span_order = draw_span_order(jax.random.fold_in(splits[19], 71), 0)
    attn_in = scatter_about(splits[4], (D, QKV), D ** -0.5, 0.125, ((0, 128),), jnp.float32)
    attn_out = scatter_about(splits[5], (QDIM, D), (QDIM // 128) ** -0.5, 1.5, ((0, 128),), jnp.float32)
    gate_up = scatter_about(splits[6], (D, 2 * FF), D ** -0.5, 0.125, ((0, 128),), jnp.float32)
    down_proj = scatter_about(splits[7], (FF, D), FF ** -0.5, 0.078125, ((0, 128),), jnp.float32)
    norm_gains = jnp.clip(1.0 + 0.1 * jax.random.normal(splits[8], (2, D), jnp.float32), 0.5, 1.5)
    first_attn_in = scatter_about(splits[9], (D, QKV), (0.16 * TOKENS ** 0.5), 128.0, ((0, 128),), jnp.float32)
    second_attn_in = jnp.clip(jnp.exp(math.log(6553.6) - 1.89712 * jax.random.uniform(splits[10], (D, QKV), jnp.float32) ** steps_of(splits[10], (D, QKV), ((0, 128),), -0.2, 0.2)), 983.04, 6553.6)
    first_attn_out = scatter_about(splits[11], (QDIM, D), (0.017 * TOKENS ** 0.5), 6.0, ((0, 128),), jnp.float32)
    second_attn_out = jnp.clip(jnp.exp(math.log(81.92) - 1.89712 * jax.random.uniform(splits[12], (QDIM, D), jnp.float32) ** steps_of(splits[12], (QDIM, D), ((0, 128),), -0.2, 0.2)), 12.288, 81.92)
    first_gate_up = scatter_about(splits[13], (D, 2 * FF), (0.033 * TOKENS ** 0.5), 24.0, ((0, 128),), jnp.float32)
    second_gate_up = jnp.clip(jnp.exp(math.log(294.912) - 1.8971199 * jax.random.uniform(splits[14], (D, 2 * FF), jnp.float32) ** steps_of(splits[14], (D, 2 * FF), ((0, 128),), -0.2, 0.2)), 44.2368, 294.912)
    first_down_proj = scatter_about(splits[15], (FF, D), (0.066 * TOKENS ** 0.5), 48.0, ((0, 128),), jnp.float32)
    second_down_proj = jnp.clip(jnp.exp(math.log(1179.648) - 1.8787708 * jax.random.uniform(splits[16], (FF, D), jnp.float32) ** steps_of(splits[16], (FF, D), ((0, 128),), -0.2, 0.2)), 180.224, 1179.648)
    first_norm_gains = scatter_about(splits[17], (2, D), (0.11 * TOKENS ** 0.5), 80.0, ((1, 128),), jnp.float32)
    second_norm_gains = jnp.clip(jnp.exp(math.log(3276.8) - 1.89712 * jax.random.uniform(splits[18], (2, D), jnp.float32) ** steps_of(splits[18], (2, D), ((1, 128),), -0.2, 0.2)), 491.52, 3276.8)
    return {"tokens": tokens, "out_grad": out_grad, "seq_lengths": seq_lengths, "span_order": span_order, "attn_in": attn_in, "attn_out": attn_out, "gate_up": gate_up, "down_proj": down_proj, "norm_gains": norm_gains, "first_attn_in": first_attn_in, "second_attn_in": second_attn_in, "first_attn_out": first_attn_out, "second_attn_out": second_attn_out, "first_gate_up": first_gate_up, "second_gate_up": second_gate_up, "first_down_proj": first_down_proj, "second_down_proj": second_down_proj, "first_norm_gains": first_norm_gains, "second_norm_gains": second_norm_gains}


@jax.custom_vjp
def low(v):
    return lax.optimization_barrier(v.astype(jnp.bfloat16)).astype(jnp.float32)

@jax.custom_vjp
def low_back(v):
    return v

def low_keep(v):
    return (low(v), None)

def low_pass(kept, grad):
    return (grad,)

def back_keep(v):
    return (v, None)

def back_low(kept, grad):
    return (low(grad),)
low.defvjp(low_keep, low_pass)
low_back.defvjp(back_keep, back_low)
norm_eps = 1e-05
beta_one = 0.9
beta_two = 0.95
adam_eps = 1e-08
big_negative = -1e+30
step_rates = (0.15, 0.3, 0.06, 0.04, 2.0)
decay_rates = (0.1, 0.1, 0.1, 0.1, 0.0)
highest = lax.Precision.HIGHEST

def slot_positions(slot_index, span_order, tok_rows):
    half_rows = tok_rows // 2
    holder = slot_index // tok_rows
    within = slot_index % tok_rows
    column = (2 * holder + within // half_rows).astype(jnp.int32)
    onehot_table = (column[:, None] == jnp.arange(span_order.shape[0], dtype=jnp.int32)[None, :]).astype(jnp.int32)
    span_ids = lax.optimization_barrier(jnp.sum(onehot_table * span_order[None, :], axis=1)).astype(jnp.int32)
    return (span_ids * half_rows + within % half_rows).astype(jnp.int32)

def doc_numbers(positions, lengths):
    bounds = jnp.cumsum(lengths).astype(jnp.int32)
    return lax.optimization_barrier(jnp.sum((positions[:, None] >= bounds[None, :]).astype(jnp.int32), axis=1)).astype(jnp.int32)

def attend_block(query_block, query_pos, query_doc, key_heads, value_heads, key_pos, key_doc):
    score_scale = HEAD_DIM ** (-0.5)
    scores = jnp.einsum('qhgd,khd->hgqk', query_block, key_heads, precision=highest) * score_scale
    scores = low_back(scores)
    allowed = (key_doc[None, :] == query_doc[:, None]) & (key_pos[None, :] <= query_pos[:, None]) & (query_doc[:, None] < SEQS)
    masked = jnp.where(allowed, scores, big_negative)
    row_peak = lax.optimization_barrier(jnp.max(masked, axis=-1, keepdims=True))
    raised = jnp.where(allowed, jnp.exp(masked - row_peak), 0.0)
    row_total = lax.optimization_barrier(jnp.sum(raised, axis=-1, keepdims=True))
    row_total = jnp.where((query_doc < SEQS)[:, None], row_total, 1.0)
    attn_probs = low(raised / row_total)
    return jnp.einsum('hgqk,khd->qhgd', attn_probs, value_heads, precision=highest)

def forward(inputs, w_qkv, w_out, w_gu, w_down, gain_pair, positions, doc_ids):
    w_qkv = low(w_qkv)
    w_out = low(w_out)
    w_gu = low(w_gu)
    w_down = low(w_down)
    gain_pair = low(gain_pair)
    group_size = HEADS // KV_HEADS
    scale_one = lax.rsqrt(lax.optimization_barrier(jnp.mean(inputs * inputs, axis=-1, keepdims=True)) + norm_eps)
    normed_one = low(inputs * scale_one * gain_pair[0])
    projected = low(low_back(jnp.dot(normed_one, w_qkv, precision=highest)))
    queries = projected[:, :QDIM].reshape(GROUPS, SLOTS, KV_HEADS, group_size, HEAD_DIM)
    key_all = projected[:, QDIM:QDIM + KVDIM].reshape(GROUPS, SLOTS, KV_HEADS, HEAD_DIM)
    value_all = projected[:, QDIM + KVDIM:].reshape(GROUPS, SLOTS, KV_HEADS, HEAD_DIM)
    block_rows = math.gcd(SLOTS, 512)

    def one_group(group_item):
        query_group, key_group, value_group, pos_group, doc_group = group_item

        def one_block(block_item):
            query_block, query_pos, query_doc = block_item
            return attend_block(query_block, query_pos, query_doc, key_group, value_group, pos_group, doc_group)
        blocks = lax.map(jax.checkpoint(one_block), (query_group.reshape(SLOTS // block_rows, block_rows, KV_HEADS, group_size, HEAD_DIM), pos_group.reshape(SLOTS // block_rows, block_rows), doc_group.reshape(SLOTS // block_rows, block_rows)))
        return blocks.reshape(SLOTS, QDIM)
    attended = lax.map(one_group, (queries, key_all, value_all, positions, doc_ids)).reshape(TOKENS, QDIM)
    attended = low(low_back(attended))
    hidden_one = inputs + low_back(jnp.dot(attended, w_out, precision=highest))
    scale_two = lax.rsqrt(lax.optimization_barrier(jnp.mean(hidden_one * hidden_one, axis=-1, keepdims=True)) + norm_eps)
    normed_two = low(hidden_one * scale_two * gain_pair[1])
    gate_up_val = low_back(jnp.dot(normed_two, w_gu, precision=highest))
    gate_part = gate_up_val[:, :FF]
    up_part = gate_up_val[:, FF:]
    activated = low(jax.nn.silu(gate_part) * up_part)
    return hidden_one + low_back(jnp.dot(activated, w_down, precision=highest))

def adam_update(master, grad_sum, first_old, second_old, step_rate, decay_rate):
    first_new = beta_one * first_old + (1.0 - beta_one) * grad_sum
    second_new = beta_two * second_old + (1.0 - beta_two) * grad_sum * grad_sum
    first_fix = first_new / (1.0 - beta_one ** STEP)
    second_fix = second_new / (1.0 - beta_two ** STEP)
    master_new = master - step_rate * (first_fix / (jnp.sqrt(second_fix) + adam_eps) + decay_rate * master)
    return (first_new, second_new, master_new)

def reference(tokens, out_grad, seq_lengths, span_order, attn_in, attn_out, gate_up, down_proj, norm_gains, first_attn_in, second_attn_in, first_attn_out, second_attn_out, first_gate_up, second_gate_up, first_down_proj, second_down_proj, first_norm_gains, second_norm_gains):
    slot_index = jnp.arange(SLOTS, dtype=jnp.int32)
    pos_one = slot_positions(slot_index, span_order, TOK_DEV)
    positions = jnp.broadcast_to(pos_one[None, :], (GROUPS, SLOTS)).astype(jnp.int32)

    def group_docs(lengths_row):
        return doc_numbers(pos_one, lengths_row)
    doc_ids = jax.vmap(group_docs)(seq_lengths).astype(jnp.int32)
    inputs = tokens.astype(jnp.float32)

    def apply_block(inputs_f, w_qkv, w_out, w_gu, w_down, gain_pair):
        return forward(inputs_f, w_qkv, w_out, w_gu, w_down, gain_pair, positions, doc_ids)
    outputs, pull_back = jax.vjp(apply_block, inputs, attn_in, attn_out, gate_up, down_proj, norm_gains)
    gradients = pull_back(out_grad.astype(jnp.float32))
    qkv_new = adam_update(attn_in, gradients[1], first_attn_in, second_attn_in, step_rates[0], decay_rates[0])
    out_new = adam_update(attn_out, gradients[2], first_attn_out, second_attn_out, step_rates[1], decay_rates[1])
    gu_new = adam_update(gate_up, gradients[3], first_gate_up, second_gate_up, step_rates[2], decay_rates[2])
    down_new = adam_update(down_proj, gradients[4], first_down_proj, second_down_proj, step_rates[3], decay_rates[3])
    gains_new = adam_update(norm_gains, gradients[5], first_norm_gains, second_norm_gains, step_rates[4], decay_rates[4])
    return (outputs.astype(jnp.bfloat16), gradients[0].astype(jnp.bfloat16), qkv_new[0], qkv_new[1], qkv_new[2], out_new[0], out_new[1], out_new[2], gu_new[0], gu_new[1], gu_new[2], down_new[0], down_new[1], down_new[2], gains_new[0], gains_new[1], gains_new[2])
```

```python
import jax
import jax.numpy as jnp
from jax import lax
from jax.experimental import pallas as pl
from jax.experimental.pallas import tpu as pltpu
from jax.sharding import Mesh
from jax.sharding import PartitionSpec as P

BF = jnp.bfloat16
F32 = jnp.float32
ALL = ("y", "zh", "x", "zl", "c")
TP = ("x", "c")
REP = ("y", "zh", "zl")

FF = 5632
FT = 704
FP = 768
HD = 64
STEP = 10
ROWS = 1024
KEYS = 2048

norm_eps = 1e-05
beta_one = 0.9
beta_two = 0.95
adam_eps = 1e-08
big_negative = -1e30
step_rates = (0.15, 0.3, 0.06, 0.04, 2.0)
decay_rates = (0.1, 0.1, 0.1, 0.1, 0.0)


def flat_index(f, x, zl, c):
    return ((f * 4 + x) * 2 + zl) * 2 + c


NATURAL = [
    (flat_index(f, 2 * h + a, b, c), flat_index(f, 2 * a + b, h, c))
    for f in range(8)
    for h in range(2)
    for a in range(2)
    for b in range(2)
    for c in range(2)
]
SPREAD = [
    (t * 16 + k, flat_index(k // 2, t // 2, k % 2, t % 2)) for t in range(8) for k in range(16)
]


def back(route):
    return [(b, a) for a, b in route]


def adam_update(master, grad_sum, first_old, second_old, step_rate, decay_rate):
    first_new = beta_one * first_old + (1.0 - beta_one) * grad_sum
    second_new = beta_two * second_old + (1.0 - beta_two) * grad_sum * grad_sum
    first_fix = first_new / (1.0 - beta_one**STEP)
    second_fix = second_new / (1.0 - beta_two**STEP)
    master_new = master - step_rate * (
        first_fix / (jnp.sqrt(second_fix) + adam_eps) + decay_rate * master
    )
    return (first_new, second_new, master_new)


def dot_nn(a, b):
    return lax.dot_general(a, b, (((1,), (0,)), ((), ())), preferred_element_type=F32)


def dot_nt(a, b):
    return lax.dot_general(a, b, (((1,), (1,)), ((), ())), preferred_element_type=F32)


def dot_tn(a, b):
    return lax.dot_general(a, b, (((0,), (0,)), ((), ())), preferred_element_type=F32)


QB = 256


def attend_kernel(q_ref, k_ref, vt_ref, kp_ref, lo_ref, hi_ref, o_ref, lse_ref):
    key_pos = kp_ref[...]
    high = hi_ref[...]
    allowed = (key_pos >= lo_ref[...]) & (key_pos <= high)
    keys = k_ref[...]
    for h in range(4):
        cols = slice(h * HD, (h + 1) * HD)
        s = jnp.where(allowed, dot_nt(keys, q_ref[:, cols]), big_negative)
        peak = jnp.max(s, axis=0, keepdims=True)
        p = jnp.exp(s - peak)
        total = jnp.sum(p, axis=0, keepdims=True)
        out = dot_nn(vt_ref[...], p.astype(BF))
        out = out * jnp.where(high >= 0, 1.0 / total, 0.0)
        o_ref[:, cols] = out.T.astype(BF)
        lse_ref[h : h + 1, :] = peak + jnp.log(total)


def attend(q, k, vt, kp, lo, hi):
    whole = lambda shape: pl.BlockSpec(shape, lambda i: (0, 0))
    row = pl.BlockSpec((1, QB), lambda i: (0, i))
    block = pl.BlockSpec((QB, 256), lambda i: (i, 0))
    return pl.pallas_call(
        attend_kernel,
        grid=(ROWS // QB,),
        in_specs=[block, whole((KEYS, HD)), whole((HD, KEYS)), whole((KEYS, QB)), row, row],
        out_specs=[block, pl.BlockSpec((4, QB), lambda i: (0, i))],
        out_shape=[
            jax.ShapeDtypeStruct((ROWS, 256), BF),
            jax.ShapeDtypeStruct((4, ROWS), F32),
        ],
        compiler_params=pltpu.CompilerParams(vmem_limit_bytes=40 * 1024 * 1024),
        cost_estimate=pl.CostEstimate(
            flops=4 * 4 * ROWS * KEYS * HD, bytes_accessed=8 << 20, transcendentals=4 * ROWS * KEYS
        ),
        name="attend",
    )(q, k, vt, kp, lo, hi)


def attend_back_kernel(
    q_ref, do_ref, o_ref, k_ref, kt_ref, v_ref, kp_ref, lo_ref, hi_ref, lse_ref, dq_ref, dk_ref, dv_ref
):
    @pl.when(pl.program_id(0) == 0)
    def _():
        dk_ref[...] = jnp.zeros_like(dk_ref)
        dv_ref[...] = jnp.zeros_like(dv_ref)

    key_pos = kp_ref[...]
    allowed = (key_pos >= lo_ref[...]) & (key_pos <= hi_ref[...])
    keys = k_ref[...]
    values = v_ref[...]
    delta_all = (do_ref[...].astype(F32) * o_ref[...].astype(F32)).T
    for h in range(4):
        cols = slice(h * HD, (h + 1) * HD)
        qh = q_ref[:, cols]
        doh = do_ref[:, cols]
        delta = jnp.sum(delta_all[cols], axis=0, keepdims=True)
        s = dot_nt(keys, qh)
        p = jnp.where(allowed, jnp.exp(s - lse_ref[h : h + 1, :]), 0.0)
        ds = (p * (dot_nt(values, doh) - delta)).astype(BF)
        dv_ref[...] += dot_nn(p.astype(BF), doh)
        dk_ref[...] += dot_nn(ds, qh)
        dq_ref[:, cols] = (dot_nn(kt_ref[...], ds) * HD**-0.5).T.astype(BF)


def attend_back(q, do, o, k, kt, v, kp, lo, hi, lse):
    whole = lambda shape: pl.BlockSpec(shape, lambda i: (0, 0))
    row = pl.BlockSpec((1, QB), lambda i: (0, i))
    block = pl.BlockSpec((QB, 256), lambda i: (i, 0))
    return pl.pallas_call(
        attend_back_kernel,
        grid=(ROWS // QB,),
        in_specs=[
            block,
            block,
            block,
            whole((KEYS, HD)),
            whole((HD, KEYS)),
            whole((KEYS, HD)),
            whole((KEYS, QB)),
            row,
            row,
            pl.BlockSpec((4, QB), lambda i: (0, i)),
        ],
        out_specs=[block, whole((KEYS, HD)), whole((KEYS, HD))],
        out_shape=[
            jax.ShapeDtypeStruct((ROWS, 256), BF),
            jax.ShapeDtypeStruct((KEYS, HD), F32),
            jax.ShapeDtypeStruct((KEYS, HD), F32),
        ],
        compiler_params=pltpu.CompilerParams(vmem_limit_bytes=48 * 1024 * 1024),
        cost_estimate=pl.CostEstimate(
            flops=10 * 4 * ROWS * KEYS * HD, bytes_accessed=8 << 20, transcendentals=4 * ROWS * KEYS
        ),
        name="attend_back",
    )(q, do, o, k, kt, v, kp, lo, hi, lse)


def gather_rows(block):
    return lax.all_gather(block, TP, axis=0, tiled=True)


def scatter_rows(partial):
    return lax.psum_scatter(partial, TP, scatter_dimension=0, tiled=True).astype(F32)


def row_positions(span_order, zl):
    spans = lax.dynamic_index_in_dim(span_order.reshape(4, 2, 4), zl, axis=1, keepdims=False)
    return (spans.reshape(16, 1) * 64 + jnp.arange(64, dtype=jnp.int32)[None, :]).reshape(ROWS)


def norm_scale(rows):
    return lax.rsqrt(jnp.mean(rows * rows, axis=-1, keepdims=True) + norm_eps)


def norm_back(grad_hat, hat, scale, rest):
    return rest + scale * (grad_hat - hat * jnp.mean(grad_hat * hat, axis=-1, keepdims=True))


def body(
    tokens,
    out_grad,
    seq_lengths,
    span_order,
    attn_in,
    attn_out,
    gate_up,
    down_proj,
    norm_gains,
    first_attn_in,
    second_attn_in,
    first_attn_out,
    second_attn_out,
    first_gate_up,
    second_gate_up,
    first_down_proj,
    second_down_proj,
    first_norm_gains,
    second_norm_gains,
):
    zl = lax.axis_index("zl")
    gains = norm_gains.astype(BF).astype(F32)
    gain_one = gains[0][:, None]
    gain_two = gains[1][:, None]
    low_qkv = attn_in.astype(BF).astype(F32)
    low_gu = gate_up.astype(BF).astype(F32)

    scaled_qkv = (low_qkv * gain_one).astype(BF)
    kv_cols = scaled_qkv[:, 2048:].reshape(16, 2, 4, 1, HD)
    kv_cols = jnp.broadcast_to(kv_cols, (16, 2, 4, 2, HD)).reshape(16, 2, 8, HD)
    qkv_cols = jnp.concatenate(
        [scaled_qkv[:, :2048].reshape(16, 8, 256), kv_cols[:, 0], kv_cols[:, 1]], axis=2
    ).transpose(1, 0, 2)
    gu_cols = (low_gu * gain_two).astype(BF).reshape(16, 2, 8, FT)
    gu_cols = jnp.pad(gu_cols, ((0, 0), (0, 0), (0, 0), (0, FP - FT)))
    gu_cols = gu_cols.transpose(2, 0, 1, 3).reshape(8, 16, 2 * FP)

    def to_rank(cols):
        moved = lax.ppermute(cols, ALL, NATURAL)
        return lax.all_to_all(moved, TP, 0, 0, tiled=True).reshape(128, cols.shape[2])

    qkv_part = to_rank(qkv_cols)
    gu_part = to_rank(gu_cols)
    out_part = lax.ppermute(attn_out.astype(BF), ALL, SPREAD)
    down_part = lax.ppermute(down_proj.astype(BF), ALL, SPREAD)
    w_qkv = lax.all_gather(qkv_part, REP, axis=0, tiled=True)
    w_out = lax.all_gather(out_part, REP, axis=0, tiled=True)
    w_gu = lax.all_gather(gu_part, REP, axis=0, tiled=True)
    w_down = lax.all_gather(down_part, REP, axis=0, tiled=False).reshape(FT, 2048)

    own_pos = row_positions(span_order, zl)
    other_pos = row_positions(span_order, 1 - zl)
    lengths = seq_lengths[0]
    bound_one = lengths[0]
    bound_two = lengths[0] + lengths[1]
    low_pos = jnp.where(own_pos < bound_one, 0, bound_one)[None, :]
    high_pos = jnp.where(own_pos < bound_two, own_pos, -1)[None, :]
    key_pos = jnp.concatenate([own_pos, other_pos])
    key_pos = jnp.broadcast_to(key_pos[:, None], (KEYS, QB))

    inputs = tokens.astype(F32)
    scale_one = norm_scale(inputs)
    hat_one = inputs * scale_one
    all_hat_one = gather_rows(hat_one.astype(BF))
    all_grad = gather_rows(out_grad)
    projected = dot_nn(all_hat_one, w_qkv).astype(BF)
    queries = projected[:, :256] * BF(HD**-0.5)
    own_kv = projected[:, 256:]
    other_kv = lax.ppermute(own_kv, "zl", [(0, 1), (1, 0)])
    kv = jnp.concatenate([own_kv, other_kv], axis=0)
    keys = kv[:, :HD]
    values = kv[:, HD:]
    att, lse = attend(queries, keys, values.T, key_pos, low_pos, high_pos)
    hidden = inputs + scatter_rows(dot_nn(att, w_out).astype(BF))

    scale_two = norm_scale(hidden)
    hat_two = hidden * scale_two
    all_hat_two = gather_rows(hat_two.astype(BF))
    w_gate = w_gu[:, :FT]
    w_up = w_gu[:, FP : FP + FT]
    gate = dot_nn(all_hat_two, w_gate)
    up = dot_nn(all_hat_two, w_up)
    sig = jax.nn.sigmoid(gate)
    silu = gate * sig
    hid = (silu * up).astype(BF)
    block_out = (hidden + scatter_rows(dot_nn(hid, w_down).astype(BF))).astype(BF)

    grad_hid = dot_nt(all_grad, w_down)
    grad_gate = (grad_hid * up * sig * (1.0 + gate * (1.0 - sig))).astype(BF)
    grad_up = (grad_hid * silu).astype(BF)
    grad_hat_two = scatter_rows((dot_nt(grad_gate, w_gate) + dot_nt(grad_up, w_up)).astype(BF))
    sum_down = dot_tn(hid, all_grad).astype(BF)
    grad_gu = jnp.concatenate(
        [
            jnp.pad(grad_gate, ((0, 0), (0, FP - FT))),
            jnp.pad(grad_up, ((0, 0), (0, FP - FT))),
        ],
        axis=1,
    )
    sum_gu = dot_tn(all_hat_two, grad_gu).astype(BF)
    sum_gu = lax.psum_scatter(sum_gu, REP, scatter_dimension=0, tiled=True)
    sum_down = lax.psum_scatter(sum_down.reshape(16, 44, 2048), REP, scatter_dimension=0, tiled=False)

    grad_hidden = norm_back(grad_hat_two, hat_two, scale_two, out_grad.astype(F32))
    all_grad_hidden = gather_rows(grad_hidden.astype(BF))
    grad_att = dot_nt(all_grad_hidden, w_out).astype(BF)
    sum_out = dot_tn(att, all_grad_hidden).astype(BF)
    sum_out = lax.psum_scatter(sum_out, REP, scatter_dimension=0, tiled=True)

    grad_q, grad_k, grad_v = attend_back(
        queries, grad_att, att, keys, keys.T, values, key_pos, low_pos, high_pos, lse
    )
    grad_kv = jnp.concatenate([grad_k, grad_v], axis=1)
    arrived = lax.ppermute(grad_kv[ROWS:].astype(BF), "zl", [(0, 1), (1, 0)])
    grad_mixed = jnp.concatenate(
        [grad_q, (grad_kv[:ROWS] + arrived.astype(F32)).astype(BF)], axis=1
    )
    grad_hat_one = scatter_rows(dot_nt(grad_mixed, w_qkv).astype(BF))
    in_grad = norm_back(grad_hat_one, hat_one, scale_one, grad_hidden).astype(BF)
    sum_qkv = dot_tn(all_hat_one, grad_mixed).astype(BF)
    sum_qkv = lax.psum_scatter(sum_qkv, REP, scatter_dimension=0, tiled=True)

    def to_shard(rows):
        mixed = lax.all_to_all(rows.reshape(8, 16, rows.shape[1]), TP, 0, 0, tiled=True)
        return lax.ppermute(mixed, ALL, back(NATURAL)).astype(F32)

    got_gu = to_shard(sum_gu).reshape(8, 16, 2, FP)[..., :FT]
    got_gu = got_gu.transpose(1, 2, 0, 3).reshape(16, 2 * FF)
    got_qkv = to_shard(sum_qkv).transpose(1, 0, 2)
    got_kv = got_qkv[:, :, 256:].reshape(16, 4, 2, 2, HD).sum(axis=2)
    got_qkv = jnp.concatenate(
        [
            got_qkv[:, :, :256].reshape(16, 2048),
            got_kv[:, :, 0].reshape(16, 256),
            got_kv[:, :, 1].reshape(16, 256),
        ],
        axis=1,
    )
    got_out = lax.ppermute(sum_out, ALL, back(SPREAD)).astype(F32)
    got_down = lax.ppermute(sum_down, ALL, back(SPREAD)).astype(F32)
    gain_sums = jnp.stack(
        [jnp.sum(low_qkv * got_qkv, axis=1), jnp.sum(low_gu * got_gu, axis=1)], axis=0
    )
    qkv_new = adam_update(
        attn_in, got_qkv * gain_one, first_attn_in, second_attn_in, step_rates[0], decay_rates[0]
    )
    out_new = adam_update(
        attn_out, got_out, first_attn_out, second_attn_out, step_rates[1], decay_rates[1]
    )
    gu_new = adam_update(
        gate_up, got_gu * gain_two, first_gate_up, second_gate_up, step_rates[2], decay_rates[2]
    )
    down_new = adam_update(
        down_proj, got_down, first_down_proj, second_down_proj, step_rates[3], decay_rates[3]
    )
    gains_new = adam_update(
        norm_gains, gain_sums, first_norm_gains, second_norm_gains, step_rates[4], decay_rates[4]
    )
    return (block_out, in_grad, *qkv_new, *out_new, *gu_new, *down_new, *gains_new)


def solution(mesh):
    split = Mesh(mesh.devices.reshape(4, 2, 4, 2, 2), ALL)
    rows = P(ALL, None)
    cols = P(None, ALL)
    group = P(("y", "zh"), None)
    in_specs = (rows, rows, group, P()) + (rows,) * 4 + (cols,) + (rows,) * 8 + (cols,) * 2
    out_specs = (rows,) * 14 + (cols,) * 3
    return jax.shard_map(body, mesh=split, in_specs=in_specs, out_specs=out_specs, check_vma=False)
```

```python
import jax
import jax.numpy as jnp
from jax import lax
from jax.experimental import pallas as pl
from jax.experimental.pallas import tpu as pltpu
from jax.sharding import Mesh
from jax.sharding import PartitionSpec as P

BF = jnp.bfloat16
F32 = jnp.float32
ALL = ("y", "zh", "x", "zl", "c")
TP = ("x", "c")
REP = ("y", "zh", "zl")

FF = 5632
FP = 768
HD = 64
STEP = 10
ROWS = 1024
KEYS = 2048

norm_eps = 1e-05
beta_one = 0.9
beta_two = 0.95
adam_eps = 1e-08
big_negative = -1e30
step_rates = (0.15, 0.3, 0.06, 0.04, 2.0)
decay_rates = (0.1, 0.1, 0.1, 0.1, 0.0)


def flat_index(f, x, zl, c):
    return ((f * 4 + x) * 2 + zl) * 2 + c


NATURAL = [
    (flat_index(f, 2 * h + a, b, c), flat_index(f, 2 * a + b, h, c))
    for f in range(8)
    for h in range(2)
    for a in range(2)
    for b in range(2)
    for c in range(2)
]
SPREAD = [
    (t * 16 + k, flat_index(k // 2, t // 2, k % 2, t % 2)) for t in range(8) for k in range(16)
]


def back(route):
    return [(b, a) for a, b in route]


def adam_update(master, grad_sum, first_old, second_old, step_rate, decay_rate):
    first_new = beta_one * first_old + (1.0 - beta_one) * grad_sum
    second_new = beta_two * second_old + (1.0 - beta_two) * grad_sum * grad_sum
    first_fix = first_new / (1.0 - beta_one**STEP)
    second_fix = second_new / (1.0 - beta_two**STEP)
    master_new = master - step_rate * (
        first_fix / (jnp.sqrt(second_fix) + adam_eps) + decay_rate * master
    )
    return (first_new, second_new, master_new)


def dot_nn(a, b):
    return lax.dot_general(a, b, (((1,), (0,)), ((), ())), preferred_element_type=F32)


def dot_nt(a, b):
    return lax.dot_general(a, b, (((1,), (1,)), ((), ())), preferred_element_type=F32)


def dot_tn(a, b):
    return lax.dot_general(a, b, (((0,), (0,)), ((), ())), preferred_element_type=F32)


QB = 256


def attend_kernel(q_ref, k_ref, vt_ref, kp_ref, lo_ref, hi_ref, o_ref, lse_ref):
    key_pos = kp_ref[...]
    high = hi_ref[...]
    allowed = (key_pos >= lo_ref[...]) & (key_pos <= high)
    keys = k_ref[...]
    for h in range(4):
        cols = slice(h * HD, (h + 1) * HD)
        s = jnp.where(allowed, dot_nt(keys, q_ref[:, cols]), big_negative)
        peak = jnp.max(s, axis=0, keepdims=True)
        p = jnp.exp(s - peak)
        total = jnp.sum(p, axis=0, keepdims=True)
        out = dot_nn(vt_ref[...], p.astype(BF))
        out = out * jnp.where(high >= 0, 1.0 / total, 0.0)
        o_ref[:, cols] = out.T.astype(BF)
        lse_ref[h : h + 1, :] = peak + jnp.log(total)


def attend(q, k, vt, kp, lo, hi):
    whole = lambda shape: pl.BlockSpec(shape, lambda i: (0, 0))
    row = pl.BlockSpec((1, QB), lambda i: (0, i))
    block = pl.BlockSpec((QB, 256), lambda i: (i, 0))
    return pl.pallas_call(
        attend_kernel,
        grid=(ROWS // QB,),
        in_specs=[block, whole((KEYS, HD)), whole((HD, KEYS)), whole((KEYS, QB)), row, row],
        out_specs=[block, pl.BlockSpec((4, QB), lambda i: (0, i))],
        out_shape=[
            jax.ShapeDtypeStruct((ROWS, 256), BF),
            jax.ShapeDtypeStruct((4, ROWS), F32),
        ],
        compiler_params=pltpu.CompilerParams(vmem_limit_bytes=40 * 1024 * 1024),
        cost_estimate=pl.CostEstimate(
            flops=4 * 4 * ROWS * KEYS * HD, bytes_accessed=8 << 20, transcendentals=4 * ROWS * KEYS
        ),
        name="attend",
    )(q, k, vt, kp, lo, hi)


def attend_back_kernel(
    q_ref, do_ref, o_ref, k_ref, kt_ref, v_ref, kp_ref, lo_ref, hi_ref, lse_ref, dq_ref, dk_ref, dv_ref
):
    @pl.when(pl.program_id(0) == 0)
    def _():
        dk_ref[...] = jnp.zeros_like(dk_ref)
        dv_ref[...] = jnp.zeros_like(dv_ref)

    key_pos = kp_ref[...]
    allowed = (key_pos >= lo_ref[...]) & (key_pos <= hi_ref[...])
    keys = k_ref[...]
    values = v_ref[...]
    delta_all = (do_ref[...].astype(F32) * o_ref[...].astype(F32)).T
    for h in range(4):
        cols = slice(h * HD, (h + 1) * HD)
        qh = q_ref[:, cols]
        doh = do_ref[:, cols]
        delta = jnp.sum(delta_all[cols], axis=0, keepdims=True)
        s = dot_nt(keys, qh)
        p = jnp.where(allowed, jnp.exp(s - lse_ref[h : h + 1, :]), 0.0)
        ds = (p * (dot_nt(values, doh) - delta)).astype(BF)
        dv_ref[...] += dot_nn(p.astype(BF), doh)
        dk_ref[...] += dot_nn(ds, qh)
        dq_ref[:, cols] = (dot_nn(kt_ref[...], ds) * HD**-0.5).T.astype(BF)


def attend_back(q, do, o, k, kt, v, kp, lo, hi, lse):
    whole = lambda shape: pl.BlockSpec(shape, lambda i: (0, 0))
    row = pl.BlockSpec((1, QB), lambda i: (0, i))
    block = pl.BlockSpec((QB, 256), lambda i: (i, 0))
    return pl.pallas_call(
        attend_back_kernel,
        grid=(ROWS // QB,),
        in_specs=[
            block,
            block,
            block,
            whole((KEYS, HD)),
            whole((HD, KEYS)),
            whole((KEYS, HD)),
            whole((KEYS, QB)),
            row,
            row,
            pl.BlockSpec((4, QB), lambda i: (0, i)),
        ],
        out_specs=[block, whole((KEYS, HD)), whole((KEYS, HD))],
        out_shape=[
            jax.ShapeDtypeStruct((ROWS, 256), BF),
            jax.ShapeDtypeStruct((KEYS, HD), F32),
            jax.ShapeDtypeStruct((KEYS, HD), F32),
        ],
        compiler_params=pltpu.CompilerParams(vmem_limit_bytes=48 * 1024 * 1024),
        cost_estimate=pl.CostEstimate(
            flops=10 * 4 * ROWS * KEYS * HD, bytes_accessed=8 << 20, transcendentals=4 * ROWS * KEYS
        ),
        name="attend_back",
    )(q, do, o, k, kt, v, kp, lo, hi, lse)


def shift(block, distance):
    return lax.ppermute(block, "x", [(i, (i + distance) % 4) for i in range(4)])


def swap(block):
    return lax.ppermute(block, "c", [(0, 1), (1, 0)])


ORDER = ((0, 0), (1, 0), (3, 0), (0, 1), (1, 1), (3, 1), (2, 0), (2, 1))
NEAR = 768


def gather_rows(block):
    right = shift(block, 1)
    left = shift(block, -1)
    near = jnp.concatenate([block, right, left], axis=0)
    near = jnp.concatenate([near, swap(near)], axis=0)
    far = jnp.concatenate([shift(right[:64], 1), shift(left[64:], -1)], axis=0)
    far = jnp.concatenate([far, swap(far)], axis=0)
    return near, far


def scatter_rows(left_side, contract, weight):
    near, far = left_side
    far_part = contract(far, weight).astype(BF)
    far_sum = (far_part[:128].astype(F32) + swap(far_part[128:]).astype(F32)).astype(BF)
    by_left = shift(far_sum[:64], -1)
    by_right = shift(far_sum[64:], 1)
    other = swap(contract(near[384:], weight).astype(BF))
    mine = contract(near[:384], weight) + other.astype(F32)
    to_left = jnp.concatenate([mine[128:192] + by_left.astype(F32), mine[192:256]], axis=0)
    to_right = jnp.concatenate([mine[256:320], mine[320:] + by_right.astype(F32)], axis=0)
    from_right = shift(to_left.astype(BF), -1).astype(F32)
    from_left = shift(to_right.astype(BF), 1).astype(F32)
    return mine[:128] + from_right + from_left


def whole(pair):
    return jnp.concatenate(pair, axis=0)


def row_positions(span_order, zl):
    x = lax.axis_index("x")
    c = lax.axis_index("c")
    holders = jnp.stack([((x - dx) % 4 * 2 + zl) * 2 + (c + dc) % 2 for dx, dc in ORDER])
    picked = (holders[:, None] == jnp.arange(16, dtype=jnp.int32)[None, :]).astype(jnp.int32)
    spans = jnp.sum(picked[:, :, None] * span_order.reshape(1, 16, 2), axis=1)
    return (spans.reshape(16, 1) * 64 + jnp.arange(64, dtype=jnp.int32)[None, :]).reshape(ROWS)


def norm_scale(rows):
    return lax.rsqrt(jnp.mean(rows * rows, axis=-1, keepdims=True) + norm_eps)


def norm_back(grad_hat, hat, scale, rest):
    return rest + scale * (grad_hat - hat * jnp.mean(grad_hat * hat, axis=-1, keepdims=True))


def body(
    tokens,
    out_grad,
    seq_lengths,
    span_order,
    attn_in,
    attn_out,
    gate_up,
    down_proj,
    norm_gains,
    first_attn_in,
    second_attn_in,
    first_attn_out,
    second_attn_out,
    first_gate_up,
    second_gate_up,
    first_down_proj,
    second_down_proj,
    first_norm_gains,
    second_norm_gains,
):
    zl = lax.axis_index("zl")
    gains = norm_gains.astype(BF).astype(F32)
    gain_one = gains[0][:, None]
    gain_two = gains[1][:, None]
    low_qkv = attn_in.astype(BF).astype(F32)
    low_gu = gate_up.astype(BF).astype(F32)

    scaled_qkv = (low_qkv * gain_one).astype(BF)
    kv_cols = scaled_qkv[:, 2048:].reshape(16, 2, 4, 1, HD)
    kv_cols = jnp.broadcast_to(kv_cols, (16, 2, 4, 2, HD)).reshape(16, 2, 8, HD)
    qkv_cols = jnp.concatenate(
        [scaled_qkv[:, :2048].reshape(16, 8, 256), kv_cols[:, 0], kv_cols[:, 1]], axis=2
    ).transpose(1, 0, 2)
    gu_cols = (low_gu * gain_two).astype(BF).reshape(16, 2, 8, 16, 44)
    gu_cols = jnp.pad(gu_cols, ((0, 0), (0, 0), (0, 0), (0, 0), (0, 4)))
    gu_cols = gu_cols.transpose(2, 0, 1, 3, 4).reshape(8, 16, 2 * FP)

    def to_rank(cols):
        moved = lax.ppermute(cols, ALL, NATURAL)
        return lax.all_to_all(moved, TP, 0, 0, tiled=True).reshape(128, cols.shape[2])

    def spread_all(part):
        copies = jnp.broadcast_to(part[None], (16, *part.shape))
        moved = lax.all_to_all(copies, REP, 0, 0, tiled=True)
        return moved.reshape(16 * part.shape[0], part.shape[1])

    w_qkv = spread_all(to_rank(qkv_cols))
    gu_part = to_rank(gu_cols)
    w_out = spread_all(lax.ppermute(attn_out.astype(BF), ALL, SPREAD))
    down_rows = jnp.pad(down_proj.astype(BF), ((0, 4), (0, 0)))
    down_part = lax.ppermute(down_rows, ALL, SPREAD)
    w_gu = lax.all_gather(gu_part, REP, axis=0, tiled=True)
    w_down = lax.all_gather(down_part, REP, axis=0, tiled=True)

    own_pos = row_positions(span_order, zl)
    other_pos = row_positions(span_order, 1 - zl)
    lengths = seq_lengths[0]
    bound_one = lengths[0]
    bound_two = lengths[0] + lengths[1]
    low_pos = jnp.where(own_pos < bound_one, 0, bound_one)[None, :]
    high_pos = jnp.where(own_pos < bound_two, own_pos, -1)[None, :]
    key_pos = jnp.concatenate([own_pos, other_pos])
    key_pos = jnp.broadcast_to(key_pos[:, None], (KEYS, QB))

    inputs = tokens.astype(F32)
    scale_one = norm_scale(inputs)
    hat_one = inputs * scale_one
    hat_one_pair = gather_rows(hat_one.astype(BF))
    grad_pair = gather_rows(out_grad)
    projected = whole([dot_nn(part, w_qkv).astype(BF) for part in hat_one_pair])
    queries = projected[:, :256] * BF(HD**-0.5)
    own_kv = projected[:, 256:]
    other_kv = lax.ppermute(own_kv, "zl", [(0, 1), (1, 0)])
    kv = jnp.concatenate([own_kv, other_kv], axis=0)
    keys = kv[:, :HD]
    values = kv[:, HD:]
    att, lse = attend(queries, keys, values.T, key_pos, low_pos, high_pos)
    hidden = inputs + scatter_rows((att[:NEAR], att[NEAR:]), dot_nn, w_out)

    scale_two = norm_scale(hidden)
    hat_two = hidden * scale_two
    hat_two_pair = gather_rows(hat_two.astype(BF))
    hid_pair = []
    grad_gu_pair = []
    for hat_part, grad_part in zip(hat_two_pair, grad_pair):
        gate_up_val = dot_nn(hat_part, w_gu)
        gate = gate_up_val[:, :FP]
        up = gate_up_val[:, FP:]
        sig = jax.nn.sigmoid(gate)
        silu = gate * sig
        hid_pair.append((silu * up).astype(BF))
        grad_hid = dot_nt(grad_part, w_down)
        grad_gate = grad_hid * up * sig * (1.0 + gate * (1.0 - sig))
        grad_up = grad_hid * silu
        grad_gu_pair.append(jnp.concatenate([grad_gate.astype(BF), grad_up.astype(BF)], axis=1))
    grad_hat_two = scatter_rows(grad_gu_pair, dot_nt, w_gu)
    sum_gu = dot_tn(whole(hat_two_pair), whole(grad_gu_pair)).astype(BF)
    sum_gu = lax.psum_scatter(sum_gu, REP, scatter_dimension=0, tiled=True)
    sum_down = dot_tn(whole(hid_pair), whole(grad_pair)).astype(BF)

    def sum_replicas(partial):
        split = partial.reshape(16, partial.shape[0] // 16, partial.shape[1])
        return jnp.sum(lax.all_to_all(split, REP, 0, 0, tiled=True).astype(F32), axis=0).astype(BF)

    sum_down = sum_replicas(sum_down)
    grad_hidden = norm_back(grad_hat_two, hat_two, scale_two, out_grad.astype(F32))
    all_grad_hidden = whole(gather_rows(grad_hidden.astype(BF)))
    block_out = (hidden + scatter_rows(hid_pair, dot_nn, w_down)).astype(BF)
    grad_att = dot_nt(all_grad_hidden, w_out).astype(BF)
    sum_out = sum_replicas(dot_tn(att, all_grad_hidden).astype(BF))

    grad_q, grad_k, grad_v = attend_back(
        queries, grad_att, att, keys, keys.T, values, key_pos, low_pos, high_pos, lse
    )
    grad_kv = jnp.concatenate([grad_k, grad_v], axis=1)
    arrived = lax.ppermute(grad_kv[ROWS:].astype(BF), "zl", [(0, 1), (1, 0)])
    grad_mixed = jnp.concatenate(
        [grad_q, (grad_kv[:ROWS] + arrived.astype(F32)).astype(BF)], axis=1
    )
    sum_qkv = sum_replicas(dot_tn(whole(hat_one_pair), grad_mixed).astype(BF))
    grad_hat_one = scatter_rows((grad_mixed[:NEAR], grad_mixed[NEAR:]), dot_nt, w_qkv)
    in_grad = norm_back(grad_hat_one, hat_one, scale_one, grad_hidden).astype(BF)

    def to_shard(rows):
        mixed = lax.all_to_all(rows.reshape(8, 16, rows.shape[1]), TP, 0, 0, tiled=True)
        return lax.ppermute(mixed, ALL, back(NATURAL)).astype(F32)

    got_gu = to_shard(sum_gu).reshape(8, 16, 2, 16, 48)[..., :44]
    got_gu = got_gu.transpose(1, 2, 0, 3, 4).reshape(16, 2 * FF)
    got_qkv = to_shard(sum_qkv).transpose(1, 0, 2)
    got_kv = got_qkv[:, :, 256:].reshape(16, 4, 2, 2, HD).sum(axis=2)
    got_qkv = jnp.concatenate(
        [
            got_qkv[:, :, :256].reshape(16, 2048),
            got_kv[:, :, 0].reshape(16, 256),
            got_kv[:, :, 1].reshape(16, 256),
        ],
        axis=1,
    )
    got_out = lax.ppermute(sum_out, ALL, back(SPREAD)).astype(F32)
    got_down = lax.ppermute(sum_down, ALL, back(SPREAD))[:44].astype(F32)
    gain_sums = jnp.stack(
        [jnp.sum(low_qkv * got_qkv, axis=1), jnp.sum(low_gu * got_gu, axis=1)], axis=0
    )
    qkv_new = adam_update(
        attn_in, got_qkv * gain_one, first_attn_in, second_attn_in, step_rates[0], decay_rates[0]
    )
    out_new = adam_update(
        attn_out, got_out, first_attn_out, second_attn_out, step_rates[1], decay_rates[1]
    )
    gu_new = adam_update(
        gate_up, got_gu * gain_two, first_gate_up, second_gate_up, step_rates[2], decay_rates[2]
    )
    down_new = adam_update(
        down_proj, got_down, first_down_proj, second_down_proj, step_rates[3], decay_rates[3]
    )
    gains_new = adam_update(
        norm_gains, gain_sums, first_norm_gains, second_norm_gains, step_rates[4], decay_rates[4]
    )
    return (block_out, in_grad, *qkv_new, *out_new, *gu_new, *down_new, *gains_new)


def solution(mesh):
    split = Mesh(mesh.devices.reshape(4, 2, 4, 2, 2), ALL)
    rows = P(ALL, None)
    cols = P(None, ALL)
    group = P(("y", "zh"), None)
    in_specs = (rows, rows, group, P()) + (rows,) * 4 + (cols,) + (rows,) * 8 + (cols,) * 2
    out_specs = (rows,) * 14 + (cols,) * 3
    return jax.shard_map(body, mesh=split, in_specs=in_specs, out_specs=out_specs, check_vma=False)
```

```python
import functools

import jax
import jax.numpy as jnp
from jax import lax
from jax.experimental import pallas as pl
from jax.experimental.pallas import tpu as pltpu
from jax.sharding import Mesh
from jax.sharding import PartitionSpec as P

BF = jnp.bfloat16
F32 = jnp.float32
ALL = ("y", "zh", "x", "zl", "c")
TP = ("x", "c")
REP = ("y", "zh", "zl")

FF = 5632
FP = 768
HD = 64
STEP = 10
ROWS = 1024
KEYS = 2048

norm_eps = 1e-05
beta_one = 0.9
beta_two = 0.95
adam_eps = 1e-08
big_negative = -1e30
step_rates = (0.15, 0.3, 0.06, 0.04, 2.0)
decay_rates = (0.1, 0.1, 0.1, 0.1, 0.0)


def flat_index(f, x, zl, c):
    return ((f * 4 + x) * 2 + zl) * 2 + c


SPREAD = [
    (t * 16 + k, flat_index(k // 2, t // 2, k % 2, t % 2)) for t in range(8) for k in range(16)
]


def back(route):
    return [(b, a) for a, b in route]


def adam_update(master, grad_sum, first_old, second_old, step_rate, decay_rate):
    first_new = beta_one * first_old + (1.0 - beta_one) * grad_sum
    second_new = beta_two * second_old + (1.0 - beta_two) * grad_sum * grad_sum
    first_fix = first_new / (1.0 - beta_one**STEP)
    second_fix = second_new / (1.0 - beta_two**STEP)
    master_new = master - step_rate * (
        first_fix / (jnp.sqrt(second_fix) + adam_eps) + decay_rate * master
    )
    return (first_new, second_new, master_new)


def dot_nn(a, b):
    return lax.dot_general(a, b, (((1,), (0,)), ((), ())), preferred_element_type=F32)


def dot_nt(a, b):
    return lax.dot_general(a, b, (((1,), (1,)), ((), ())), preferred_element_type=F32)


def dot_tn(a, b):
    return lax.dot_general(a, b, (((0,), (0,)), ((), ())), preferred_element_type=F32)


QB = 256


def takes(microseconds):
    return pl.CostEstimate(
        flops=int(microseconds * 1.15e9), bytes_accessed=1 << 20, transcendentals=0
    )


WHOLE = pl.BlockSpec(memory_space=pltpu.VMEM)
ANYWHERE = pl.BlockSpec(memory_space=pl.ANY)


def fixed(shape):
    return pl.BlockSpec(shape, lambda i: (0,) * len(shape), pipeline_mode=pl.Buffered(1))


def params(mib):
    return pltpu.CompilerParams(vmem_limit_bytes=mib * 1024 * 1024)


def attend_kernel(first, q_ref, kv_ref, kp_ref, lo_ref, hi_ref, *rest):
    turned = rest[-1]

    @pl.when(pl.program_id(0) == 0)
    def _():
        turned[...] = kv_ref[...].T

    key_pos = kp_ref[...]
    high = hi_ref[...]
    allowed = (key_pos >= lo_ref[...]) & (key_pos <= high)
    keys = kv_ref[:, :HD]
    for h in range(4):
        cols = slice(h * HD, (h + 1) * HD)
        row = slice(h, h + 1)
        s = jnp.where(allowed, dot_nt(keys, q_ref[:, cols]), big_negative)
        peak = jnp.max(s, axis=0, keepdims=True)
        if not first:
            out_before, peak_before, total_before = rest[:3]
            peak = jnp.maximum(peak, peak_before[row, :])
        p = jnp.exp(s - peak)
        total = jnp.sum(p, axis=0, keepdims=True)
        out = dot_nn(turned[HD:, :], p.astype(BF))
        if first:
            out_ref, peak_ref, total_ref = rest[-4:-1]
            out_ref[cols, :] = out
            peak_ref[row, :] = peak
            total_ref[row, :] = total
        else:
            o_ref, lse_ref = rest[-3:-1]
            fade = jnp.exp(peak_before[row, :] - peak)
            total = total + fade * total_before[row, :]
            out = out + fade * out_before[cols, :]
            out = out * jnp.where(high >= 0, 1.0 / total, 0.0)
            o_ref[:, cols] = out.T.astype(BF)
            lse_ref[row, :] = peak + jnp.log(total)


def attend(q, kv, kp, lo, hi, before, *earlier):
    first = before is None
    count = kv.shape[0]
    row = pl.BlockSpec((1, QB), lambda i: (0, i))
    rows = pl.BlockSpec((4, QB), lambda i: (0, i))
    flat = pl.BlockSpec((256, QB), lambda i: (0, i))
    block = pl.BlockSpec((QB, 256), lambda i: (i, 0))
    stat = jax.ShapeDtypeStruct((4, ROWS), F32)
    carried = [] if first else list(before)
    return pl.pallas_call(
        functools.partial(attend_kernel, first),
        grid=(ROWS // QB,),
        in_specs=[block, fixed((count, 2 * HD)), fixed((count, QB)), row, row]
        + [flat, rows, rows][: len(carried)]
        + [ANYWHERE] * len(earlier),
        out_specs=[flat, rows, rows] if first else [block, rows],
        out_shape=[jax.ShapeDtypeStruct((256, ROWS), F32), stat, stat]
        if first
        else [jax.ShapeDtypeStruct((ROWS, 256), BF), stat],
        scratch_shapes=[pltpu.VMEM((2 * HD, count), BF)],
        compiler_params=params(40),
        cost_estimate=takes(11),
        name="attend",
    )(q, kv, kp, lo, hi, *carried, *earlier)


def attend_back_kernel(first, q_ref, do_ref, o_ref, kv_ref, kp_ref, lo_ref, hi_ref, lse_ref, *rest):
    dq_ref, dkv_ref, turned, values = rest[-4:]

    @pl.when(pl.program_id(0) == 0)
    def _():
        dkv_ref[...] = jnp.zeros_like(dkv_ref)
        turned[...] = kv_ref[...].T
        values[...] = kv_ref[:, HD:]

    key_pos = kp_ref[...]
    allowed = (key_pos >= lo_ref[...]) & (key_pos <= hi_ref[...])
    keys = kv_ref[:, :HD]
    delta_all = (do_ref[...].astype(F32) * o_ref[...].astype(F32)).T
    for h in range(4):
        cols = slice(h * HD, (h + 1) * HD)
        qh = q_ref[:, cols]
        doh = do_ref[:, cols]
        delta = jnp.sum(delta_all[cols], axis=0, keepdims=True)
        s = dot_nt(keys, qh)
        p = jnp.where(allowed, jnp.exp(s - lse_ref[h : h + 1, :]), 0.0)
        ds = (p * (dot_nt(values[...], doh) - delta)).astype(BF)
        dkv_ref[:, :HD] += dot_nn(ds, qh)
        dkv_ref[:, HD:] += dot_nn(p.astype(BF), doh)
        dq = dot_nn(turned[:HD, :], ds) * HD**-0.5
        if first:
            dq_ref[cols, :] = dq
        else:
            dq_ref[:, cols] = (dq + rest[0][cols, :]).T.astype(BF)


def attend_back(q, do, o, kv, kp, lo, hi, lse, earlier_dq, *earlier):
    first = earlier_dq is None
    count = kv.shape[0]
    row = pl.BlockSpec((1, QB), lambda i: (0, i))
    block = pl.BlockSpec((QB, 256), lambda i: (i, 0))
    flat = pl.BlockSpec((256, QB), lambda i: (0, i))
    carried = [] if first else [earlier_dq]
    return pl.pallas_call(
        functools.partial(attend_back_kernel, first),
        grid=(ROWS // QB,),
        in_specs=[block, block, block, fixed((count, 2 * HD)), fixed((count, QB)), row, row]
        + [pl.BlockSpec((4, QB), lambda i: (0, i))]
        + [flat] * len(carried)
        + [ANYWHERE] * len(earlier),
        out_specs=[
            flat if first else block,
            pl.BlockSpec((count, 2 * HD), lambda i: (0, 0)),
        ],
        out_shape=[
            jax.ShapeDtypeStruct((256, ROWS), F32)
            if first
            else jax.ShapeDtypeStruct((ROWS, 256), BF),
            jax.ShapeDtypeStruct((count, 2 * HD), F32),
        ],
        scratch_shapes=[pltpu.VMEM((2 * HD, count), BF), pltpu.VMEM((count, HD), BF)],
        compiler_params=params(40),
        cost_estimate=takes(12.5),
        name="attend_back",
    )(q, do, o, kv, kp, lo, hi, lse, *carried, *earlier)


def project_kernel(*refs):
    pieces = refs[:8]
    raw_ref = refs[8]
    q_ref, kv_ref, w_ref = refs[-4:-1]
    hat = refs[-1]
    for f in range(8):
        for zl in range(2):
            for x in range(4):
                row = 256 * f + 64 * x + 32 * zl
                w_ref[row : row + 32, :] = raw_ref[2 * f + zl, 32 * x : 32 * x + 32, :]
    for k in range(8):
        hat[128 * k : 128 * k + 128, :] = pieces[k][...]
    for k in range(2):
        rows = slice(512 * k, 512 * k + 512)
        product = dot_nn(hat[rows, :], w_ref[...]).astype(BF)
        q_ref[rows, :] = product[:, :256] * BF(HD**-0.5)
        kv_ref[rows, :] = product[:, 256:]


def project(pieces, raw, *earlier):
    shape = lambda *dims: jax.ShapeDtypeStruct(dims, BF)
    return pl.pallas_call(
        project_kernel,
        in_specs=[WHOLE] * 9 + [ANYWHERE] * len(earlier),
        out_specs=[WHOLE] * 3,
        out_shape=[shape(ROWS, 256), shape(ROWS, 128), shape(2048, 384)],
        scratch_shapes=[pltpu.VMEM((ROWS, 2048), BF)],
        compiler_params=params(40),
        cost_estimate=takes(5),
        name="project",
    )(*pieces, raw, *earlier)


def hidden_products_kernel(*refs):
    pieces = refs[:8]
    att_ref, w_ref = refs[8:10]
    grad_att_ref, sum_ref, grad = refs[-3:]
    for k in range(8):
        grad[128 * k : 128 * k + 128, :] = pieces[k][...]
    grad_att_ref[...] = dot_nt(grad[...], w_ref[...]).astype(BF)
    for k in range(4):
        cols = slice(512 * k, 512 * k + 512)
        sum_ref[:, cols] = dot_tn(att_ref[...], grad[:, cols]).astype(BF)


def hidden_products(pieces, att, w_out, *earlier):
    return pl.pallas_call(
        hidden_products_kernel,
        in_specs=[WHOLE] * 10 + [ANYWHERE] * len(earlier),
        out_specs=[WHOLE] * 2,
        out_shape=[jax.ShapeDtypeStruct((ROWS, 256), BF), jax.ShapeDtypeStruct((256, 2048), BF)],
        scratch_shapes=[pltpu.VMEM((ROWS, 2048), BF)],
        compiler_params=params(40),
        cost_estimate=takes(6),
        name="hidden_products",
    )(*pieces, att, w_out, *earlier)


def feed_forward_kernel(*refs):
    hat_pieces, grad_pieces, ff_ref = refs[:8], refs[8:16], refs[16]
    hid_ref, grad_gu_ref, back_mine, back_other, ahead_mine, ahead_other = refs[17:23]
    w_gu, w_down, hat, grad = refs[23:]
    step = pl.program_id(0)

    @pl.when(step == 0)
    def _():
        for f in range(8):
            for zl in range(2):
                r = 2 * f + zl
                for x in range(4):
                    row = 256 * f + 64 * x + 32 * zl
                    w_gu[row : row + 32, :] = ff_ref[192 * r + 32 * x : 192 * r + 32 * x + 32, :]
                w_down[48 * r : 48 * r + 48, :1536] = ff_ref[192 * r + 128 : 192 * r + 176, :]
                for part in range(3):
                    w_down[48 * r + 16 * part : 48 * r + 16 * part + 16, 1536:] = ff_ref[
                        192 * r + 176 : 192 * r + 192, 512 * part : 512 * part + 512
                    ]

    for k in range(4):

        @pl.when(step == k)
        def _():
            for half in range(2):
                piece = (2 * k + 4) % 8 + half
                rows = slice(128 * half, 128 * half + 128)
                hat[rows, :] = hat_pieces[piece][...]
                grad[rows, :] = grad_pieces[piece][...]

    gate_up_val = dot_nn(hat[...], w_gu[...])
    gate = gate_up_val[:, :FP]
    up = gate_up_val[:, FP:]
    sig = jax.nn.sigmoid(gate)
    silu = gate * sig
    hid_ref[...] = (silu * up).astype(BF)
    grad_hid = dot_nt(grad[...], w_down[...])
    grad_gu_ref[:, :FP] = (grad_hid * up * sig * (1.0 + gate * (1.0 - sig))).astype(BF)
    grad_gu_ref[:, FP:] = (grad_hid * silu).astype(BF)
    back = dot_nt(grad_gu_ref[...], w_gu[...]).astype(BF)
    ahead = dot_nn(hid_ref[...], w_down[...]).astype(BF)

    @pl.when(step < 2)
    def _():
        back_other[...] = back
        ahead_other[...] = ahead

    @pl.when(step >= 2)
    def _():
        back_mine[...] = back
        ahead_mine[...] = ahead


def feed_forward(hat_pieces, grad_pieces, ff_all):
    piece = fixed((128, 2048))
    block = lambda cols: pl.BlockSpec((256, cols), lambda i: ((i + 2) % 4, 0))
    mine = pl.BlockSpec((256, 2048), lambda i: (jnp.maximum(i - 2, 0), 0))
    other = pl.BlockSpec((256, 2048), lambda i: (jnp.minimum(i, 1), 0))
    shape = lambda rows, cols: jax.ShapeDtypeStruct((rows, cols), BF)
    half = shape(ROWS // 2, 2048)
    return pl.pallas_call(
        feed_forward_kernel,
        grid=(4,),
        in_specs=[piece] * 16 + [fixed((3072, 1536))],
        out_specs=[block(FP), block(2 * FP), mine, other, mine, other],
        out_shape=[shape(ROWS, FP), shape(ROWS, 2 * FP), half, half, half, half],
        scratch_shapes=[
            pltpu.VMEM((2048, 2 * FP), BF),
            pltpu.VMEM((FP, 2048), BF),
            pltpu.VMEM((256, 2048), BF),
            pltpu.VMEM((256, 2048), BF),
        ],
        compiler_params=params(58),
        cost_estimate=takes(28),
        name="feed_forward",
    )(*hat_pieces, *grad_pieces, ff_all)


def weight_grads_kernel(*refs):
    hat_pieces, grad_pieces = refs[:8], refs[8:16]
    grad_gu_ref, hid_ref = refs[16:18]
    out_ref, hid_t, grad, hat = refs[-4:]

    @pl.when(pl.program_id(0) == 0)
    def _():
        hid_t[...] = hid_ref[...].T
        for k in range(8):
            grad[128 * k : 128 * k + 128, :] = grad_pieces[k][...]

    for k in range(8):
        hat[128 * k : 128 * k + 128, :] = hat_pieces[k][...]
    for half in range(2):
        total = dot_tn(hat[:, 256 * half : 256 * half + 256], grad_gu_ref[...])
        total = total.astype(BF).reshape(4, 2, 32, 2 * FP)
        for zl in range(2):
            out_ref[2 * half + zl, :128, :] = total[:, zl].reshape(128, 2 * FP)
    rows = pl.ds(pl.multiple_of(pl.program_id(0) * 192, 64), 192)
    total = dot_nn(hid_t[rows, :], grad[...]).astype(BF).reshape(4, 48, 2048)
    out_ref[:, 128:176, :] = total[:, :, :1536]
    for part in range(3):
        out_ref[:, 176:192, 512 * part : 512 * part + 512] = total[:, 16 * part : 16 * part + 16, 1536:]


def weight_grads(hat_pieces, grad_pieces, grad_gu, hid, *earlier):
    return pl.pallas_call(
        weight_grads_kernel,
        grid=(4,),
        in_specs=[pl.BlockSpec((128, 512), lambda j: (0, j))] * 8
        + [fixed((128, 2048))] * 8
        + [fixed((ROWS, 2 * FP)), fixed((ROWS, FP))]
        + [ANYWHERE] * len(earlier),
        out_specs=pl.BlockSpec((4, 192, 1536), lambda j: (j, 0, 0)),
        out_shape=jax.ShapeDtypeStruct((16, 192, 1536), BF),
        scratch_shapes=[
            pltpu.VMEM((FP, ROWS), BF),
            pltpu.VMEM((ROWS, 2048), BF),
            pltpu.VMEM((ROWS, 512), BF),
        ],
        compiler_params=params(56),
        cost_estimate=takes(16.5),
        name="weight_grads",
    )(*hat_pieces, *grad_pieces, grad_gu, hid, *earlier)


def ff_columns():
    for f in range(8):
        for x in range(4):
            for zl in range(2):
                for c in range(2):
                    for g in range(2):
                        yield (
                            x * 2 + c,
                            g * FP + (f * 2 + zl) * 48,
                            g * FF + flat_index(f, x, zl, c) * 44,
                        )


def pack_kernel(qkv_ref, gate_up_ref, gains_ref, out_ref, scaled_qkv, scaled, packed):
    gains = gains_ref[...]
    scaled_qkv[...] = qkv_ref[...].astype(BF).astype(F32) * gains[:, 0:1]
    scaled[...] = gate_up_ref[...].astype(BF).astype(F32) * gains[:, 1:2]
    packed[...] = jnp.zeros_like(packed)
    for rank in range(8):
        head = 2048 + rank // 2 * HD
        packed[rank, :, :256] = scaled_qkv[:, rank * 256 : rank * 256 + 256]
        packed[rank, :, 256:320] = scaled_qkv[:, head : head + HD]
        packed[rank, :, 320:384] = scaled_qkv[:, head + 256 : head + 256 + HD]
    for rank, there, here in ff_columns():
        packed[rank, :, 384 + there : 384 + there + 44] = scaled[:, here : here + 44]
    out_ref[...] = packed[...].astype(BF)


def pack(qkv, gate_up, gains):
    return pl.pallas_call(
        pack_kernel,
        in_specs=[WHOLE] * 3,
        out_specs=WHOLE,
        out_shape=jax.ShapeDtypeStruct((8, 16, 1920), BF),
        scratch_shapes=[
            pltpu.VMEM((16, 2560), F32),
            pltpu.VMEM((16, 2 * FF), F32),
            pltpu.VMEM((8, 16, 1920), F32),
        ],
        compiler_params=params(24),
        cost_estimate=takes(3),
        name="pack",
    )(qkv, gate_up, gains)


def update_kernel(
    got_ref, master_ref, gain_ref, first_ref, second_ref, new_first, new_second, new_master, gain_sum, packed, sums
):
    packed[...] = got_ref[...].astype(F32)
    for rank, there, here in ff_columns():
        sums[:, here : here + 44] = packed[rank, :, 384 + there : 384 + there + 44]
    master = master_ref[...]
    gain_sum[...] = jnp.sum(
        master.astype(BF).astype(F32) * sums[...], axis=1, keepdims=True
    )
    new_first[...], new_second[...], new_master[...] = adam_update(
        master,
        sums[...] * gain_ref[...],
        first_ref[...],
        second_ref[...],
        step_rates[2],
        decay_rates[2],
    )


def update_gate_up(got, master, gain, first, second):
    shape = jax.ShapeDtypeStruct((16, 2 * FF), F32)
    return pl.pallas_call(
        update_kernel,
        in_specs=[WHOLE] * 5,
        out_specs=[WHOLE] * 4,
        out_shape=[shape, shape, shape, jax.ShapeDtypeStruct((16, 1), F32)],
        scratch_shapes=[pltpu.VMEM((8, 16, 1920), F32), pltpu.VMEM((16, 2 * FF), F32)],
        compiler_params=params(32),
        cost_estimate=takes(4),
        name="update_gate_up",
    )(got, master, gain, first, second)


def shift(block, distance):
    return lax.ppermute(block, "x", [(i, (i + distance) % 4) for i in range(4)])


def swap(block):
    return lax.ppermute(block, "c", [(0, 1), (1, 0)])


ORDER = ((0, 0), (1, 0), (3, 0), (2, 0), (0, 1), (1, 1), (3, 1), (2, 1))


def tie_kernel(*refs):
    pass


def tie(value, *earlier):
    anywhere = pl.BlockSpec(memory_space=pl.ANY)
    return pl.pallas_call(
        tie_kernel,
        in_specs=[anywhere] * (1 + len(earlier)),
        out_specs=anywhere,
        out_shape=jax.ShapeDtypeStruct(value.shape, value.dtype),
        input_output_aliases={0: 0},
        cost_estimate=pl.CostEstimate(flops=0, bytes_accessed=0, transcendentals=0),
        name="tie",
    )(value, *earlier)


def gather_pieces(block):
    mine = [block, shift(block, 1), shift(block, -1), shift(block, 2)]
    return mine + [swap(piece) for piece in mine]


def scatter_first(mine, other):
    return mine.astype(F32) + swap(other).astype(F32)


def scatter_second(mine):
    far = mine[384:].astype(BF)
    by_left = shift(far[:64], -1)
    by_right = shift(far[64:], 1)
    to_left = jnp.concatenate([mine[128:192] + by_left.astype(F32), mine[192:256]], axis=0)
    to_right = jnp.concatenate([mine[256:320], mine[320:384] + by_right.astype(F32)], axis=0)
    return to_left.astype(BF), to_right.astype(BF), mine[:128]


def scatter_third(to_left, to_right):
    return shift(to_left, -1), shift(to_right, 1)


def total(parts):
    first, second, third = parts
    return first.astype(F32) + second.astype(F32) + third.astype(F32)


def last_products_kernel(place_ref, mixed_ref, w_ref, out_ref, rows):
    for k in range(4):
        first = pl.multiple_of(place_ref[pl.program_id(0) * 4 + k] * 128, 128)
        rows[128 * k : 128 * k + 128, :] = mixed_ref[pl.ds(first, 128), :]
    out_ref[...] = dot_nt(rows[...], w_ref[...]).astype(BF)


def last_products(grad_mixed, w_qkv):
    owner = jnp.arange(8, dtype=jnp.int32)
    dx = (lax.axis_index("x") - owner // 2) % 4
    dc = (lax.axis_index("c") + owner) % 2
    place = 4 * dc + jnp.where(dx < 2, dx, 5 - dx)
    return pl.pallas_call(
        last_products_kernel,
        grid_spec=pltpu.PrefetchScalarGridSpec(
            num_scalar_prefetch=1,
            grid=(2,),
            in_specs=[
                pl.BlockSpec((ROWS, 384), lambda j, place: (0, 0)),
                pl.BlockSpec((2048, 384), lambda j, place: (0, 0)),
            ],
            out_specs=pl.BlockSpec((512, 2048), lambda j, place: (j, 0)),
            scratch_shapes=[pltpu.VMEM((512, 384), BF)],
        ),
        out_shape=jax.ShapeDtypeStruct((ROWS, 2048), BF),
        compiler_params=pltpu.CompilerParams(vmem_limit_bytes=32 * 1024 * 1024),
        cost_estimate=takes(5),
        name="last_products",
    )(place, grad_mixed, w_qkv)


def attn_grads_kernel(*refs):
    pieces = refs[:8]
    mixed_ref, out_grad_ref, sum_ref, hat = refs[8:]
    for k in range(8):
        hat[128 * k : 128 * k + 128, :] = pieces[k][...]
    total = dot_tn(hat[...], mixed_ref[...]).astype(BF).reshape(4, 2, 32, 384)
    for zl in range(2):
        sum_ref[zl, :, :384] = total[:, zl].reshape(128, 384)
        for k in range(8):
            sum_ref[zl, 16 * k : 16 * k + 16, 384:] = out_grad_ref[
                16 * zl : 16 * zl + 16, 256 * k : 256 * k + 256
            ]


def attn_grads(pieces, grad_mixed, sum_out):
    return pl.pallas_call(
        attn_grads_kernel,
        grid=(8,),
        in_specs=[pl.BlockSpec((128, 256), lambda f: (0, f))] * 8
        + [fixed((ROWS, 384)), pl.BlockSpec((32, 2048), lambda f: (f, 0))],
        out_specs=pl.BlockSpec((2, 128, 640), lambda f: (f, 0, 0)),
        out_shape=jax.ShapeDtypeStruct((16, 128, 640), BF),
        scratch_shapes=[pltpu.VMEM((ROWS, 256), BF)],
        compiler_params=params(40),
        cost_estimate=takes(4),
        name="attn_grads",
    )(*pieces, grad_mixed, sum_out)


def row_positions(span_order, zl):
    x = lax.axis_index("x")
    c = lax.axis_index("c")
    holders = jnp.stack([((x - dx) % 4 * 2 + zl) * 2 + (c + dc) % 2 for dx, dc in ORDER])
    picked = (holders[:, None] == jnp.arange(16, dtype=jnp.int32)[None, :]).astype(jnp.int32)
    spans = jnp.sum(picked[:, :, None] * span_order.reshape(1, 16, 2), axis=1)
    return (spans.reshape(16, 1) * 64 + jnp.arange(64, dtype=jnp.int32)[None, :]).reshape(ROWS)


def norm_scale(rows):
    return lax.rsqrt(jnp.mean(rows * rows, axis=-1, keepdims=True) + norm_eps)


def norm_back(grad_hat, hat, scale, rest):
    return rest + scale * (grad_hat - hat * jnp.mean(grad_hat * hat, axis=-1, keepdims=True))


def body(
    tokens,
    out_grad,
    seq_lengths,
    span_order,
    attn_in,
    attn_out,
    gate_up,
    down_proj,
    norm_gains,
    first_attn_in,
    second_attn_in,
    first_attn_out,
    second_attn_out,
    first_gate_up,
    second_gate_up,
    first_down_proj,
    second_down_proj,
    first_norm_gains,
    second_norm_gains,
):
    zl = lax.axis_index("zl")
    gains = norm_gains.astype(BF).astype(F32)
    gain_one = gains[0][:, None]
    gain_two = gains[1][:, None]
    low_qkv = attn_in.astype(BF).astype(F32)

    inputs = tokens.astype(F32)
    scale_one = norm_scale(inputs)
    hat_one = inputs * scale_one
    packed = pack(attn_in, gate_up, gains.T)
    ranked = lax.all_to_all(packed, TP, 0, 0, tiled=True).reshape(128, 1920)
    hat_pieces = gather_pieces(tie(hat_one.astype(BF), ranked))
    qkv_copies = jnp.broadcast_to(ranked[None, :, :384], (16, 128, 384))
    qkv_all = lax.all_to_all(qkv_copies, REP, 0, 0, tiled=True)
    out_part = lax.ppermute(tie(attn_out.astype(BF), ranked), ALL, SPREAD)
    down_rows = jnp.pad(down_proj.astype(BF), ((0, 4), (0, 0)))
    down_tail = [down_rows[16 * part : 16 * part + 16, 1536:] for part in range(3)]
    ff_part = jnp.concatenate(
        [ranked[:, 384:], down_rows[:, :1536], jnp.concatenate(down_tail, axis=1)], axis=0
    )
    ff_all = lax.all_gather(ff_part, REP, axis=0, tiled=True)
    grad_pieces = gather_pieces(tie(out_grad, *hat_pieces[1:4]))

    own_pos = row_positions(span_order, zl)
    other_pos = row_positions(span_order, 1 - zl)
    lengths = seq_lengths[0]
    bound_one = lengths[0]
    bound_two = lengths[0] + lengths[1]
    low_pos = jnp.where(own_pos < bound_one, 0, bound_one)[None, :]
    high_pos = jnp.where(own_pos < bound_two, own_pos, -1)[None, :]
    key_pos = jnp.concatenate([own_pos, other_pos])
    key_pos = jnp.broadcast_to(key_pos[:, None], (KEYS, QB))

    queries, own_kv, w_qkv = project(hat_pieces, qkv_all)
    other_kv = lax.ppermute(own_kv, "zl", [(0, 1), (1, 0)])
    out_copies = jnp.broadcast_to(tie(out_part, own_kv)[None], (16, 16, 2048))
    w_out = lax.all_to_all(out_copies, REP, 0, 0, tiled=True).reshape(256, 2048)
    before = attend(queries, own_kv, key_pos[:ROWS], low_pos, high_pos, None)
    att, lse = attend(
        queries, other_kv, key_pos[ROWS:], low_pos, high_pos, before, *grad_pieces[1:4]
    )
    att_other = dot_nn(att[512:], w_out).astype(BF)
    att_mine = dot_nn(att[:512], w_out)
    to_left, to_right, stays = scatter_second(scatter_first(att_mine, att_other))
    hidden = inputs + total((stays, *scatter_third(to_left, to_right)))

    scale_two = norm_scale(hidden)
    hat_two = hidden * scale_two
    hat_two_pieces = gather_pieces(hat_two.astype(BF))
    hid, grad_gu, back_mine, back_other, ahead_mine, ahead_other = feed_forward(
        hat_two_pieces, grad_pieces, ff_all
    )
    to_left, to_right, stays = scatter_second(scatter_first(back_mine, back_other))
    grad_hat_two = total((stays, *scatter_third(to_left, to_right)))
    grad_hidden = norm_back(grad_hat_two, hat_two, scale_two, out_grad.astype(F32))
    grad_hidden_low = grad_hidden.astype(BF)
    hidden_pieces = gather_pieces(grad_hidden_low)
    sum_ff = weight_grads(hat_two_pieces, grad_pieces, grad_gu, hid, grad_hidden_low)
    all_sum_ff = sum_ff.reshape(16 * 192, 1536)
    sum_ff = lax.psum_scatter(all_sum_ff, REP, scatter_dimension=0, tiled=True)
    grad_att, sum_out = hidden_products(hidden_pieces, att, w_out, all_sum_ff)
    ahead = scatter_first(ahead_mine, tie(ahead_other, hidden_pieces[3]))

    grad_q, grad_kv = attend_back(
        queries, grad_att, att, other_kv, key_pos[ROWS:], low_pos, high_pos, lse, None, ahead
    )
    arrived = lax.ppermute(grad_kv.astype(BF), "zl", [(0, 1), (1, 0)])
    ahead_left, ahead_right, ahead_stays = scatter_second(ahead)
    grad_q, grad_kv = attend_back(
        queries,
        grad_att,
        att,
        own_kv,
        key_pos[:ROWS],
        low_pos,
        high_pos,
        lse,
        grad_q,
        ahead_left,
        ahead_right,
    )
    ahead = scatter_third(ahead_left, ahead_right)
    block_out = (hidden + total((ahead_stays, *ahead))).astype(BF)
    grad_mixed = jnp.concatenate([grad_q, (grad_kv + arrived.astype(F32)).astype(BF)], axis=1)
    grad_mixed = tie(grad_mixed, *ahead)
    attn_sums = attn_grads(hat_pieces, grad_mixed, sum_out)
    attn_sums = lax.all_to_all(attn_sums, REP, 0, 0, tiled=True)
    grad_hat_one = lax.psum_scatter(
        last_products(tie(grad_mixed, sum_ff), w_qkv), TP, scatter_dimension=0, tiled=True
    ).astype(F32)
    attn_sums = jnp.sum(attn_sums.astype(F32), axis=0).astype(BF)
    in_grad = norm_back(grad_hat_one, hat_one, scale_one, grad_hidden).astype(BF)

    got = jnp.concatenate([attn_sums[:, :384], sum_ff[:128]], axis=1).reshape(8, 16, 1920)
    got = lax.all_to_all(got, TP, 0, 0, tiled=True)
    got_qkv = got[:, :, :384].transpose(1, 0, 2).astype(F32)
    got_kv = got_qkv[:, :, 256:].reshape(16, 4, 2, 2, HD).sum(axis=2)
    got_qkv = jnp.concatenate(
        [
            got_qkv[:, :, :256].reshape(16, 2048),
            got_kv[:, :, 0].reshape(16, 256),
            got_kv[:, :, 1].reshape(16, 256),
        ],
        axis=1,
    )
    sum_out = attn_sums[:, 384:].reshape(8, 16, 256).transpose(1, 0, 2).reshape(16, 2048)
    got_out = lax.ppermute(sum_out, ALL, back(SPREAD)).astype(F32)
    tail = [sum_ff[176:192, 512 * part : 512 * part + 512] for part in range(3)]
    got_down = jnp.concatenate([sum_ff[128:176], jnp.concatenate(tail, axis=0)], axis=1)
    got_down = got_down[:44].astype(F32)
    gu_new = update_gate_up(got, gate_up, gain_two, first_gate_up, second_gate_up)
    gain_sums = jnp.stack([jnp.sum(low_qkv * got_qkv, axis=1), gu_new[3][:, 0]], axis=0)
    qkv_new = adam_update(
        attn_in, got_qkv * gain_one, first_attn_in, second_attn_in, step_rates[0], decay_rates[0]
    )
    out_new = adam_update(
        attn_out, got_out, first_attn_out, second_attn_out, step_rates[1], decay_rates[1]
    )
    down_new = adam_update(
        down_proj, got_down, first_down_proj, second_down_proj, step_rates[3], decay_rates[3]
    )
    gains_new = adam_update(
        norm_gains, gain_sums, first_norm_gains, second_norm_gains, step_rates[4], decay_rates[4]
    )
    return (block_out, in_grad, *qkv_new, *out_new, *gu_new[:3], *down_new, *gains_new)


def solution(mesh):
    split = Mesh(mesh.devices.reshape(4, 2, 4, 2, 2), ALL)
    rows = P(ALL, None)
    cols = P(None, ALL)
    group = P(("y", "zh"), None)
    in_specs = (rows, rows, group, P()) + (rows,) * 4 + (cols,) + (rows,) * 8 + (cols,) * 2
    out_specs = (rows,) * 14 + (cols,) * 3
    return jax.shard_map(body, mesh=split, in_specs=in_specs, out_specs=out_specs, check_vma=False)
```

```python
import functools

import jax
import jax.numpy as jnp
from jax import lax
from jax.experimental import pallas as pl
from jax.experimental.pallas import tpu as pltpu
from jax.sharding import Mesh
from jax.sharding import PartitionSpec as P

BF = jnp.bfloat16
F32 = jnp.float32
ALL = ("y", "zh", "x", "zl", "c")
TP = ("x", "c")
REP = ("y", "zh", "zl")

FF = 5632
FP = 768
HD = 64
STEP = 10
ROWS = 1024
KEYS = 2048

norm_eps = 1e-05
beta_one = 0.9
beta_two = 0.95
adam_eps = 1e-08
big_negative = -1e30
step_rates = (0.15, 0.3, 0.06, 0.04, 2.0)
decay_rates = (0.1, 0.1, 0.1, 0.1, 0.0)


def flat_index(f, x, zl, c):
    return ((f * 4 + x) * 2 + zl) * 2 + c


SPREAD = [
    (t * 16 + k, flat_index(k // 2, t // 2, k % 2, t % 2)) for t in range(8) for k in range(16)
]


def back(route):
    return [(b, a) for a, b in route]


def adam_update(master, grad_sum, first_old, second_old, step_rate, decay_rate):
    first_new = beta_one * first_old + (1.0 - beta_one) * grad_sum
    second_new = beta_two * second_old + (1.0 - beta_two) * grad_sum * grad_sum
    first_fix = first_new / (1.0 - beta_one**STEP)
    second_fix = second_new / (1.0 - beta_two**STEP)
    master_new = master - step_rate * (
        first_fix / (jnp.sqrt(second_fix) + adam_eps) + decay_rate * master
    )
    return (first_new, second_new, master_new)


def dot_nn(a, b):
    return lax.dot_general(a, b, (((1,), (0,)), ((), ())), preferred_element_type=F32)


def dot_nt(a, b):
    return lax.dot_general(a, b, (((1,), (1,)), ((), ())), preferred_element_type=F32)


def dot_tn(a, b):
    return lax.dot_general(a, b, (((0,), (0,)), ((), ())), preferred_element_type=F32)


QB = 256


def takes(microseconds):
    return pl.CostEstimate(
        flops=int(microseconds * 1.15e9), bytes_accessed=1 << 20, transcendentals=0
    )


WHOLE = pl.BlockSpec(memory_space=pltpu.VMEM)
ANYWHERE = pl.BlockSpec(memory_space=pl.ANY)


def fixed(shape):
    return pl.BlockSpec(shape, lambda i: (0,) * len(shape), pipeline_mode=pl.Buffered(1))


def params(mib):
    return pltpu.CompilerParams(vmem_limit_bytes=mib * 1024 * 1024)


def attend_kernel(first, q_ref, kv_ref, kp_ref, lo_ref, hi_ref, *rest):
    turned = rest[-1]

    @pl.when(pl.program_id(0) == 0)
    def _():
        turned[...] = kv_ref[...].T

    key_pos = kp_ref[...]
    high = hi_ref[...]
    allowed = (key_pos >= lo_ref[...]) & (key_pos <= high)
    keys = kv_ref[:, :HD]
    for h in range(4):
        cols = slice(h * HD, (h + 1) * HD)
        row = slice(h, h + 1)
        s = jnp.where(allowed, dot_nt(keys, q_ref[:, cols]), big_negative)
        peak = jnp.max(s, axis=0, keepdims=True)
        if not first:
            out_before, peak_before, total_before = rest[:3]
            peak = jnp.maximum(peak, peak_before[row, :])
        p = jnp.exp(s - peak)
        total = jnp.sum(p, axis=0, keepdims=True)
        out = dot_nn(turned[HD:, :], p.astype(BF))
        if first:
            out_ref, peak_ref, total_ref = rest[-4:-1]
            out_ref[cols, :] = out
            peak_ref[row, :] = peak
            total_ref[row, :] = total
        else:
            o_ref, lse_ref = rest[-3:-1]
            fade = jnp.exp(peak_before[row, :] - peak)
            total = total + fade * total_before[row, :]
            out = out + fade * out_before[cols, :]
            out = out * jnp.where(high >= 0, 1.0 / total, 0.0)
            o_ref[:, cols] = out.T.astype(BF)
            lse_ref[row, :] = peak + jnp.log(total)


def attend(q, kv, kp, lo, hi, before, *earlier):
    first = before is None
    count = kv.shape[0]
    row = pl.BlockSpec((1, QB), lambda i: (0, i))
    rows = pl.BlockSpec((4, QB), lambda i: (0, i))
    flat = pl.BlockSpec((256, QB), lambda i: (0, i))
    block = pl.BlockSpec((QB, 256), lambda i: (i, 0))
    stat = jax.ShapeDtypeStruct((4, ROWS), F32)
    carried = [] if first else list(before)
    return pl.pallas_call(
        functools.partial(attend_kernel, first),
        grid=(ROWS // QB,),
        in_specs=[block, fixed((count, 2 * HD)), fixed((count, QB)), row, row]
        + [flat, rows, rows][: len(carried)]
        + [ANYWHERE] * len(earlier),
        out_specs=[flat, rows, rows] if first else [block, rows],
        out_shape=[jax.ShapeDtypeStruct((256, ROWS), F32), stat, stat]
        if first
        else [jax.ShapeDtypeStruct((ROWS, 256), BF), stat],
        scratch_shapes=[pltpu.VMEM((2 * HD, count), BF)],
        compiler_params=params(40),
        cost_estimate=takes(11),
        name="attend",
    )(q, kv, kp, lo, hi, *carried, *earlier)


def attend_back_kernel(first, q_ref, do_ref, o_ref, kv_ref, kp_ref, lo_ref, hi_ref, lse_ref, *rest):
    dq_ref, dkv_ref, turned, values = rest[-4:]

    @pl.when(pl.program_id(0) == 0)
    def _():
        dkv_ref[...] = jnp.zeros_like(dkv_ref)
        turned[...] = kv_ref[...].T
        values[...] = kv_ref[:, HD:]

    key_pos = kp_ref[...]
    allowed = (key_pos >= lo_ref[...]) & (key_pos <= hi_ref[...])
    keys = kv_ref[:, :HD]
    delta_all = (do_ref[...].astype(F32) * o_ref[...].astype(F32)).T
    for h in range(4):
        cols = slice(h * HD, (h + 1) * HD)
        qh = q_ref[:, cols]
        doh = do_ref[:, cols]
        delta = jnp.sum(delta_all[cols], axis=0, keepdims=True)
        s = dot_nt(keys, qh)
        p = jnp.where(allowed, jnp.exp(s - lse_ref[h : h + 1, :]), 0.0)
        ds = (p * (dot_nt(values[...], doh) - delta)).astype(BF)
        dkv_ref[:, :HD] += dot_nn(ds, qh)
        dkv_ref[:, HD:] += dot_nn(p.astype(BF), doh)
        dq = dot_nn(turned[:HD, :], ds) * HD**-0.5
        if first:
            dq_ref[cols, :] = dq
        else:
            dq_ref[:, cols] = (dq + rest[0][cols, :]).T.astype(BF)


def attend_back(q, do, o, kv, kp, lo, hi, lse, earlier_dq, *earlier):
    first = earlier_dq is None
    count = kv.shape[0]
    row = pl.BlockSpec((1, QB), lambda i: (0, i))
    block = pl.BlockSpec((QB, 256), lambda i: (i, 0))
    flat = pl.BlockSpec((256, QB), lambda i: (0, i))
    carried = [] if first else [earlier_dq]
    return pl.pallas_call(
        functools.partial(attend_back_kernel, first),
        grid=(ROWS // QB,),
        in_specs=[block, block, block, fixed((count, 2 * HD)), fixed((count, QB)), row, row]
        + [pl.BlockSpec((4, QB), lambda i: (0, i))]
        + [flat] * len(carried)
        + [ANYWHERE] * len(earlier),
        out_specs=[
            flat if first else block,
            pl.BlockSpec((count, 2 * HD), lambda i: (0, 0)),
        ],
        out_shape=[
            jax.ShapeDtypeStruct((256, ROWS), F32)
            if first
            else jax.ShapeDtypeStruct((ROWS, 256), BF),
            jax.ShapeDtypeStruct((count, 2 * HD), F32),
        ],
        scratch_shapes=[pltpu.VMEM((2 * HD, count), BF), pltpu.VMEM((count, HD), BF)],
        compiler_params=params(40),
        cost_estimate=takes(12.5),
        name="attend_back",
    )(q, do, o, kv, kp, lo, hi, lse, *carried, *earlier)


def fetch(pieces, rows, sems):
    copies = [
        pltpu.make_async_copy(piece, rows.at[pl.ds(128 * k, 128), :], sems.at[k])
        for k, piece in enumerate(pieces)
    ]
    for copy in copies:
        copy.start()
    return copies


def project_kernel(*refs):
    pieces, raw_hbm = refs[:8], refs[8]
    q_ref, kv_ref, w_ref, w_out_ref, hat, raw_ref, sems, raw_sem = refs[9:]
    raw_copy = pltpu.make_async_copy(raw_hbm, raw_ref, raw_sem)
    raw_copy.start()
    copies = fetch(pieces, hat, sems)
    raw_copy.wait()
    for f in range(8):
        for zl in range(2):
            r = 2 * f + zl
            for x in range(4):
                row = 256 * f + 64 * x + 32 * zl
                w_ref[row : row + 32, :] = raw_ref[128 * r + 32 * x : 128 * r + 32 * x + 32, :384]
            for k in range(8):
                w_out_ref[16 * r : 16 * r + 16, 256 * k : 256 * k + 256] = raw_ref[
                    128 * r + 16 * k : 128 * r + 16 * k + 16, 384:
                ]
    for copy in copies:
        copy.wait()
    for k in range(2):
        rows = slice(512 * k, 512 * k + 512)
        product = dot_nn(hat[rows, :], w_ref[...]).astype(BF)
        q_ref[rows, :] = product[:, :256] * BF(HD**-0.5)
        kv_ref[rows, :] = product[:, 256:]


def project(pieces, raw):
    shape = lambda *dims: jax.ShapeDtypeStruct(dims, BF)
    return pl.pallas_call(
        project_kernel,
        in_specs=[ANYWHERE] * 9,
        out_specs=[WHOLE] * 4,
        out_shape=[shape(ROWS, 256), shape(ROWS, 128), shape(2048, 384), shape(256, 2048)],
        scratch_shapes=[
            pltpu.VMEM((ROWS, 2048), BF),
            pltpu.VMEM((2048, 640), BF),
            pltpu.SemaphoreType.DMA((8,)),
            pltpu.SemaphoreType.DMA,
        ],
        compiler_params=params(60),
        cost_estimate=takes(5),
        name="project",
    )(*pieces, raw)


def hidden_products_kernel(*refs):
    pieces = refs[:8]
    att_ref, w_ref = refs[8:10]
    grad_att_ref, sum_ref, grad, sems = refs[-4:]
    for copy in fetch(pieces, grad, sems):
        copy.wait()
    grad_att_ref[...] = dot_nt(grad[...], w_ref[...]).astype(BF)
    for k in range(4):
        cols = slice(512 * k, 512 * k + 512)
        sum_ref[:, cols] = dot_tn(att_ref[...], grad[:, cols]).astype(BF)


def hidden_products(pieces, att, w_out, *earlier):
    return pl.pallas_call(
        hidden_products_kernel,
        in_specs=[ANYWHERE] * 8 + [WHOLE] * 2 + [ANYWHERE] * len(earlier),
        out_specs=[WHOLE] * 2,
        out_shape=[jax.ShapeDtypeStruct((ROWS, 256), BF), jax.ShapeDtypeStruct((256, 2048), BF)],
        scratch_shapes=[pltpu.VMEM((ROWS, 2048), BF), pltpu.SemaphoreType.DMA((8,))],
        compiler_params=params(60),
        cost_estimate=takes(6),
        name="hidden_products",
    )(*pieces, att, w_out, *earlier)


def feed_forward_kernel(*refs):
    hat_pieces, grad_pieces, ff_ref = refs[:8], refs[8:16], refs[16]
    hid_ref, grad_gu_ref, back_mine, back_other, ahead_mine, ahead_other = refs[17:23]
    w_gu_ref, w_down_ref, hat, grad, w_sems, hat_sems, grad_sems = refs[23:]
    step = pl.program_id(0)

    def copies(first, count):
        return (
            [
                pltpu.make_async_copy(
                    hat_pieces[k], hat.at[pl.ds(128 * k, 128), :], hat_sems.at[k]
                )
                for k in range(first, first + count)
            ],
            [
                pltpu.make_async_copy(
                    grad_pieces[k], grad.at[pl.ds(128 * k, 128), :], grad_sems.at[k]
                )
                for k in range(first, first + count)
            ],
        )

    gu_copies = [
        pltpu.make_async_copy(
            ff_ref.at[:, zl, pl.ds(0, 4)], w_gu_ref.at[:, :, zl], w_sems.at[zl]
        )
        for zl in range(2)
    ]
    down_copies = [
        pltpu.make_async_copy(
            ff_ref.at[:, :, 4], w_down_ref.at[:, :, pl.ds(0, 32), pl.ds(0, 1536)], w_sems.at[2]
        ),
        pltpu.make_async_copy(
            ff_ref.at[:, :, 5, pl.ds(0, 16)],
            w_down_ref.at[:, :, pl.ds(32, 16), pl.ds(0, 1536)],
            w_sems.at[3],
        ),
    ] + [
        pltpu.make_async_copy(
            ff_ref.at[:, :, 5, pl.ds(16, 16), pl.ds(512 * part, 512)],
            w_down_ref.at[:, :, pl.ds(16 * part, 16), pl.ds(1536, 512)],
            w_sems.at[4 + part],
        )
        for part in range(3)
    ]
    mine_hat, mine_grad = copies(0, 4)
    other_hat, other_grad = copies(4, 4)

    @pl.when(step == 0)
    def _():
        for copy in gu_copies + other_hat + down_copies + other_grad + mine_hat + mine_grad:
            copy.start()
        for copy in gu_copies + other_hat:
            copy.wait()

    @pl.when(step == 1)
    def _():
        for copy in mine_hat + mine_grad:
            copy.wait()

    rows = pl.ds(pl.multiple_of((1 - step) * 512, 512), 512)
    w_gu = w_gu_ref[...].reshape(2048, 2 * FP)
    gate_up_val = dot_nn(hat[rows, :], w_gu)
    gate = gate_up_val[:, :FP]
    up = gate_up_val[:, FP:]
    sig = jax.nn.sigmoid(gate)
    silu = gate * sig
    hid_ref[...] = (silu * up).astype(BF)

    @pl.when(step == 0)
    def _():
        for copy in down_copies + other_grad:
            copy.wait()

    w_down = w_down_ref[...].reshape(FP, 2048)
    grad_hid = dot_nt(grad[rows, :], w_down)
    grad_gu_ref[:, :FP] = (grad_hid * up * sig * (1.0 + gate * (1.0 - sig))).astype(BF)
    grad_gu_ref[:, FP:] = (grad_hid * silu).astype(BF)
    for back_ref, ahead_ref, now in ((back_other, ahead_other, 0), (back_mine, ahead_mine, 1)):

        @pl.when(step == now)
        def _():
            for k in range(2):
                cols = slice(1024 * k, 1024 * k + 1024)
                w_cols = w_gu_ref[4 * k : 4 * k + 4].reshape(1024, 2 * FP)
                back_ref[:, cols] = dot_nt(grad_gu_ref[...], w_cols).astype(BF)
                w_cols = w_down_ref[:, :, :, cols].reshape(FP, 1024)
                ahead_ref[:, cols] = dot_nn(hid_ref[...], w_cols).astype(BF)


def feed_forward(hat_pieces, grad_pieces, ff_all):
    block = lambda cols: pl.BlockSpec((512, cols), lambda i: (1 - i, 0))
    held = pl.BlockSpec((512, 2048), lambda i: (0, 0))
    shape = lambda rows, cols: jax.ShapeDtypeStruct((rows, cols), BF)
    half = shape(ROWS // 2, 2048)
    return pl.pallas_call(
        feed_forward_kernel,
        grid=(2,),
        in_specs=[ANYWHERE] * 17,
        out_specs=[block(FP), block(2 * FP)] + [held] * 4,
        out_shape=[shape(ROWS, FP), shape(ROWS, 2 * FP)] + [half] * 4,
        scratch_shapes=[
            pltpu.VMEM((8, 4, 2, 32, 2 * FP), BF),
            pltpu.VMEM((8, 2, 48, 2048), BF),
            pltpu.VMEM((ROWS, 2048), BF),
            pltpu.VMEM((ROWS, 2048), BF),
            pltpu.SemaphoreType.DMA((7,)),
            pltpu.SemaphoreType.DMA((8,)),
            pltpu.SemaphoreType.DMA((8,)),
        ],
        compiler_params=params(60),
        cost_estimate=takes(28),
        name="feed_forward",
    )(*hat_pieces, *grad_pieces, ff_all.reshape(8, 2, 6, 32, 1536))


def weight_grads_kernel(*refs):
    hat_pieces, grad_pieces = refs[:8], refs[8:16]
    grad_gu_ref, hid_ref = refs[16:18]
    out_ref, hid_t, grad, hat = refs[-4:]

    @pl.when(pl.program_id(0) == 0)
    def _():
        hid_t[...] = hid_ref[...].T
        for k in range(8):
            grad[128 * k : 128 * k + 128, :] = grad_pieces[k][...]

    for k in range(8):
        hat[128 * k : 128 * k + 128, :] = hat_pieces[k][...]
    for half in range(2):
        total = dot_tn(hat[:, 256 * half : 256 * half + 256], grad_gu_ref[...])
        total = total.astype(BF).reshape(4, 2, 32, 2 * FP)
        for zl in range(2):
            out_ref[2 * half + zl, :128, :] = total[:, zl].reshape(128, 2 * FP)
    rows = pl.ds(pl.multiple_of(pl.program_id(0) * 192, 64), 192)
    total = dot_nn(hid_t[rows, :], grad[...]).astype(BF).reshape(4, 48, 2048)
    out_ref[:, 128:176, :] = total[:, :, :1536]
    for part in range(3):
        out_ref[:, 176:192, 512 * part : 512 * part + 512] = total[:, 16 * part : 16 * part + 16, 1536:]


def weight_grads(hat_pieces, grad_pieces, grad_gu, hid, *earlier):
    return pl.pallas_call(
        weight_grads_kernel,
        grid=(4,),
        in_specs=[pl.BlockSpec((128, 512), lambda j: (0, j))] * 8
        + [fixed((128, 2048))] * 8
        + [fixed((ROWS, 2 * FP)), fixed((ROWS, FP))]
        + [ANYWHERE] * len(earlier),
        out_specs=pl.BlockSpec((4, 192, 1536), lambda j: (j, 0, 0)),
        out_shape=jax.ShapeDtypeStruct((16, 192, 1536), BF),
        scratch_shapes=[
            pltpu.VMEM((FP, ROWS), BF),
            pltpu.VMEM((ROWS, 2048), BF),
            pltpu.VMEM((ROWS, 512), BF),
        ],
        compiler_params=params(56),
        cost_estimate=takes(16.5),
        name="weight_grads",
    )(*hat_pieces, *grad_pieces, grad_gu, hid, *earlier)


def ff_columns():
    for f in range(8):
        for x in range(4):
            for zl in range(2):
                for c in range(2):
                    for g in range(2):
                        yield (
                            x * 2 + c,
                            g * FP + (f * 2 + zl) * 48,
                            g * FF + flat_index(f, x, zl, c) * 44,
                        )


def pack_kernel(qkv_ref, gate_up_ref, gains_ref, out_ref, scaled_qkv, scaled, packed):
    gains = gains_ref[...]
    scaled_qkv[...] = qkv_ref[...].astype(BF).astype(F32) * gains[:, 0:1]
    scaled[...] = gate_up_ref[...].astype(BF).astype(F32) * gains[:, 1:2]
    packed[...] = jnp.zeros_like(packed)
    for rank in range(8):
        head = 2048 + rank // 2 * HD
        packed[rank, :, :256] = scaled_qkv[:, rank * 256 : rank * 256 + 256]
        packed[rank, :, 256:320] = scaled_qkv[:, head : head + HD]
        packed[rank, :, 320:384] = scaled_qkv[:, head + 256 : head + 256 + HD]
    for rank, there, here in ff_columns():
        packed[rank, :, 384 + there : 384 + there + 44] = scaled[:, here : here + 44]
    out_ref[...] = packed[...].astype(BF)


def pack(qkv, gate_up, gains):
    return pl.pallas_call(
        pack_kernel,
        in_specs=[WHOLE] * 3,
        out_specs=WHOLE,
        out_shape=jax.ShapeDtypeStruct((8, 16, 1920), BF),
        scratch_shapes=[
            pltpu.VMEM((16, 2560), F32),
            pltpu.VMEM((16, 2 * FF), F32),
            pltpu.VMEM((8, 16, 1920), F32),
        ],
        compiler_params=params(24),
        cost_estimate=takes(3),
        name="pack",
    )(qkv, gate_up, gains)


def update_kernel(
    got_ref, master_ref, gain_ref, first_ref, second_ref, new_first, new_second, new_master, gain_sum, packed, sums
):
    packed[...] = got_ref[...].astype(F32)
    for rank, there, here in ff_columns():
        sums[:, here : here + 44] = packed[rank, :, 384 + there : 384 + there + 44]
    master = master_ref[...]
    gain_sum[...] = jnp.sum(
        master.astype(BF).astype(F32) * sums[...], axis=1, keepdims=True
    )
    new_first[...], new_second[...], new_master[...] = adam_update(
        master,
        sums[...] * gain_ref[...],
        first_ref[...],
        second_ref[...],
        step_rates[2],
        decay_rates[2],
    )


def update_gate_up(got, master, gain, first, second):
    shape = jax.ShapeDtypeStruct((16, 2 * FF), F32)
    return pl.pallas_call(
        update_kernel,
        in_specs=[WHOLE] * 5,
        out_specs=[WHOLE] * 4,
        out_shape=[shape, shape, shape, jax.ShapeDtypeStruct((16, 1), F32)],
        scratch_shapes=[pltpu.VMEM((8, 16, 1920), F32), pltpu.VMEM((16, 2 * FF), F32)],
        compiler_params=params(32),
        cost_estimate=takes(4),
        name="update_gate_up",
    )(got, master, gain, first, second)


def shift(block, distance):
    return lax.ppermute(block, "x", [(i, (i + distance) % 4) for i in range(4)])


def swap(block):
    return lax.ppermute(block, "c", [(0, 1), (1, 0)])


ORDER = ((0, 0), (1, 0), (3, 0), (2, 0), (0, 1), (1, 1), (3, 1), (2, 1))


def tie_kernel(*refs):
    pass


def tie(value, *earlier):
    anywhere = pl.BlockSpec(memory_space=pl.ANY)
    return pl.pallas_call(
        tie_kernel,
        in_specs=[anywhere] * (1 + len(earlier)),
        out_specs=anywhere,
        out_shape=jax.ShapeDtypeStruct(value.shape, value.dtype),
        input_output_aliases={0: 0},
        cost_estimate=pl.CostEstimate(flops=0, bytes_accessed=0, transcendentals=0),
        name="tie",
    )(value, *earlier)


def gather_pieces(block):
    mine = [block, shift(block, 1), shift(block, -1), shift(block, 2)]
    return mine + [swap(piece) for piece in mine]


def scatter_first(mine, other):
    return mine.astype(F32) + swap(other).astype(F32)


def scatter_second(mine):
    far = mine[384:].astype(BF)
    by_left = shift(far[:64], -1)
    by_right = shift(far[64:], 1)
    to_left = jnp.concatenate([mine[128:192] + by_left.astype(F32), mine[192:256]], axis=0)
    to_right = jnp.concatenate([mine[256:320], mine[320:384] + by_right.astype(F32)], axis=0)
    return to_left.astype(BF), to_right.astype(BF), mine[:128]


def scatter_third(to_left, to_right):
    return shift(to_left, -1), shift(to_right, 1)


def total(parts):
    first, second, third = parts
    return first.astype(F32) + second.astype(F32) + third.astype(F32)


def attn_grads_kernel(*refs):
    pieces = refs[:8]
    mixed_ref, out_grad_ref, sum_ref, hat, sems = refs[8:]
    copies = fetch(pieces, hat, sems)
    for r in range(16):
        for k in range(8):
            sum_ref[r, 16 * k : 16 * k + 16, 384:] = out_grad_ref[
                16 * r : 16 * r + 16, 256 * k : 256 * k + 256
            ]
    for copy in copies:
        copy.wait()
    for f in range(8):
        total = dot_tn(hat[:, 256 * f : 256 * f + 256], mixed_ref[...])
        total = total.astype(BF).reshape(4, 2, 32, 384)
        for zl in range(2):
            sum_ref[2 * f + zl, :, :384] = total[:, zl].reshape(128, 384)


def attn_grads(pieces, grad_mixed, sum_out):
    return pl.pallas_call(
        attn_grads_kernel,
        in_specs=[ANYWHERE] * 8 + [WHOLE] * 2,
        out_specs=WHOLE,
        out_shape=jax.ShapeDtypeStruct((16, 128, 640), BF),
        scratch_shapes=[pltpu.VMEM((ROWS, 2048), BF), pltpu.SemaphoreType.DMA((8,))],
        compiler_params=params(60),
        cost_estimate=takes(4),
        name="attn_grads",
    )(*pieces, grad_mixed, sum_out)


def row_positions(span_order, zl):
    x = lax.axis_index("x")
    c = lax.axis_index("c")
    holders = jnp.stack([((x - dx) % 4 * 2 + zl) * 2 + (c + dc) % 2 for dx, dc in ORDER])
    picked = (holders[:, None] == jnp.arange(16, dtype=jnp.int32)[None, :]).astype(jnp.int32)
    spans = jnp.sum(picked[:, :, None] * span_order.reshape(1, 16, 2), axis=1)
    return (spans.reshape(16, 1) * 64 + jnp.arange(64, dtype=jnp.int32)[None, :]).reshape(ROWS)


def norm_scale(rows):
    return lax.rsqrt(jnp.mean(rows * rows, axis=-1, keepdims=True) + norm_eps)


def norm_back(grad_hat, hat, scale, rest):
    return rest + scale * (grad_hat - hat * jnp.mean(grad_hat * hat, axis=-1, keepdims=True))


def body(
    tokens,
    out_grad,
    seq_lengths,
    span_order,
    attn_in,
    attn_out,
    gate_up,
    down_proj,
    norm_gains,
    first_attn_in,
    second_attn_in,
    first_attn_out,
    second_attn_out,
    first_gate_up,
    second_gate_up,
    first_down_proj,
    second_down_proj,
    first_norm_gains,
    second_norm_gains,
):
    zl = lax.axis_index("zl")
    gains = norm_gains.astype(BF).astype(F32)
    gain_one = gains[0][:, None]
    gain_two = gains[1][:, None]
    low_qkv = attn_in.astype(BF).astype(F32)

    inputs = tokens.astype(F32)
    scale_one = norm_scale(inputs)
    hat_one = inputs * scale_one
    packed = pack(attn_in, gate_up, gains.T)
    ranked = lax.all_to_all(packed, TP, 0, 0, tiled=True).reshape(128, 1920)
    hat_pieces = gather_pieces(tie(hat_one.astype(BF), ranked))
    out_part = lax.ppermute(attn_out.astype(BF), ALL, SPREAD)
    out_part = out_part.reshape(16, 8, 256).transpose(1, 0, 2).reshape(128, 256)
    attn_part = jnp.concatenate([ranked[:, :384], out_part], axis=1)
    attn_all = lax.all_gather(attn_part, REP, axis=0, tiled=True)
    down_rows = jnp.pad(down_proj.astype(BF), ((0, 4), (0, 0)))
    down_tail = [down_rows[16 * part : 16 * part + 16, 1536:] for part in range(3)]
    ff_part = jnp.concatenate(
        [ranked[:, 384:], down_rows[:, :1536], jnp.concatenate(down_tail, axis=1)], axis=0
    )
    grad_pieces = gather_pieces(tie(out_grad, *hat_pieces[1:4]))
    ff_all = lax.all_gather(
        tie(ff_part, attn_all, *hat_pieces[1:]), REP, axis=0, tiled=True
    )

    own_pos = row_positions(span_order, zl)
    other_pos = row_positions(span_order, 1 - zl)
    lengths = seq_lengths[0]
    bound_one = lengths[0]
    bound_two = lengths[0] + lengths[1]
    low_pos = jnp.where(own_pos < bound_one, 0, bound_one)[None, :]
    high_pos = jnp.where(own_pos < bound_two, own_pos, -1)[None, :]
    key_pos = jnp.concatenate([own_pos, other_pos])
    key_pos = jnp.broadcast_to(key_pos[:, None], (KEYS, QB))

    queries, own_kv, w_qkv, w_out = project(hat_pieces, attn_all)
    other_kv = lax.ppermute(own_kv, "zl", [(0, 1), (1, 0)])
    before = attend(queries, own_kv, key_pos[:ROWS], low_pos, high_pos, None)
    att, lse = attend(
        queries, other_kv, key_pos[ROWS:], low_pos, high_pos, before, *grad_pieces[1:4]
    )
    att_other = dot_nn(att[512:], w_out).astype(BF)
    att_mine = dot_nn(att[:512], w_out)
    to_left, to_right, stays = scatter_second(scatter_first(att_mine, att_other))
    hidden = inputs + total((stays, *scatter_third(to_left, to_right)))

    scale_two = norm_scale(hidden)
    hat_two = hidden * scale_two
    hat_two_pieces = gather_pieces(hat_two.astype(BF))
    hid, grad_gu, back_mine, back_other, ahead_mine, ahead_other = feed_forward(
        hat_two_pieces, grad_pieces, ff_all
    )
    to_left, to_right, stays = scatter_second(scatter_first(back_mine, back_other))
    grad_hat_two = total((stays, *scatter_third(to_left, to_right)))
    grad_hidden = norm_back(grad_hat_two, hat_two, scale_two, out_grad.astype(F32))
    sums = weight_grads(hat_two_pieces, grad_pieces, grad_gu, hid, to_left, to_right)
    sums = sums.reshape(16 * 192, 1536)
    grad_hidden_low = tie(grad_hidden.astype(BF), sums)
    hidden_pieces = gather_pieces(grad_hidden_low)
    sums = lax.psum_scatter(tie(sums, grad_hidden_low), REP, scatter_dimension=0, tiled=True)
    ahead = scatter_first(ahead_mine, tie(ahead_other, hidden_pieces[0]))
    grad_att, sum_out = hidden_products(hidden_pieces, att, w_out, ahead)

    grad_q, grad_kv = attend_back(
        queries, grad_att, att, other_kv, key_pos[ROWS:], low_pos, high_pos, lse, None, ahead
    )
    arrived = lax.ppermute(grad_kv.astype(BF), "zl", [(0, 1), (1, 0)])
    ahead_left, ahead_right, ahead_stays = scatter_second(ahead)
    grad_q, grad_kv = attend_back(
        queries,
        grad_att,
        att,
        own_kv,
        key_pos[:ROWS],
        low_pos,
        high_pos,
        lse,
        grad_q,
        ahead_left,
        ahead_right,
    )
    ahead = scatter_third(ahead_left, ahead_right)
    block_out = (hidden + total((ahead_stays, *ahead))).astype(BF)
    grad_mixed = jnp.concatenate([grad_q, (grad_kv + arrived.astype(F32)).astype(BF)], axis=1)
    grad_mixed = tie(grad_mixed, *ahead)
    attn_parts = attn_grads(hat_pieces, grad_mixed, sum_out)
    attn_sums = lax.all_to_all(attn_parts, REP, 0, 0, tiled=True)
    attn_sums = jnp.sum(attn_sums.astype(F32), axis=0).astype(BF)
    last_rows = tie(grad_mixed, attn_parts)
    last_other = dot_nt(last_rows[512:], w_qkv).astype(BF)
    last_mine = dot_nt(last_rows[:512], w_qkv)
    to_left, to_right, stays = scatter_second(scatter_first(last_mine, last_other))
    grad_hat_one = total((stays, *scatter_third(to_left, to_right)))
    in_grad = norm_back(grad_hat_one, hat_one, scale_one, grad_hidden).astype(BF)

    got = jnp.concatenate([attn_sums[:, :384], sums[:128]], axis=1).reshape(8, 16, 1920)
    got = lax.all_to_all(got, TP, 0, 0, tiled=True)
    got_qkv = got[:, :, :384].transpose(1, 0, 2).astype(F32)
    got_kv = got_qkv[:, :, 256:].reshape(16, 4, 2, 2, HD).sum(axis=2)
    got_qkv = jnp.concatenate(
        [
            got_qkv[:, :, :256].reshape(16, 2048),
            got_kv[:, :, 0].reshape(16, 256),
            got_kv[:, :, 1].reshape(16, 256),
        ],
        axis=1,
    )
    sum_out = attn_sums[:, 384:].reshape(8, 16, 256).transpose(1, 0, 2).reshape(16, 2048)
    got_out = lax.ppermute(tie(sum_out, got), ALL, back(SPREAD)).astype(F32)
    tail = [sums[176:192, 512 * part : 512 * part + 512] for part in range(3)]
    got_down = jnp.concatenate([sums[128:176], jnp.concatenate(tail, axis=0)], axis=1)
    got_down = got_down[:44].astype(F32)
    gu_new = update_gate_up(got, gate_up, gain_two, first_gate_up, second_gate_up)
    gain_sums = jnp.stack([jnp.sum(low_qkv * got_qkv, axis=1), gu_new[3][:, 0]], axis=0)
    qkv_new = adam_update(
        attn_in, got_qkv * gain_one, first_attn_in, second_attn_in, step_rates[0], decay_rates[0]
    )
    out_new = adam_update(
        attn_out, got_out, first_attn_out, second_attn_out, step_rates[1], decay_rates[1]
    )
    down_new = adam_update(
        down_proj, got_down, first_down_proj, second_down_proj, step_rates[3], decay_rates[3]
    )
    gains_new = adam_update(
        norm_gains, gain_sums, first_norm_gains, second_norm_gains, step_rates[4], decay_rates[4]
    )
    return (block_out, in_grad, *qkv_new, *out_new, *gu_new[:3], *down_new, *gains_new)


def solution(mesh):
    split = Mesh(mesh.devices.reshape(4, 2, 4, 2, 2), ALL)
    rows = P(ALL, None)
    cols = P(None, ALL)
    group = P(("y", "zh"), None)
    in_specs = (rows, rows, group, P()) + (rows,) * 4 + (cols,) + (rows,) * 8 + (cols,) * 2
    out_specs = (rows,) * 14 + (cols,) * 3
    return jax.shard_map(body, mesh=split, in_specs=in_specs, out_specs=out_specs, check_vma=False)
```

```python
import functools

import jax
import jax.numpy as jnp
from jax import lax
from jax.experimental import pallas as pl
from jax.experimental.pallas import tpu as pltpu
from jax.sharding import Mesh
from jax.sharding import PartitionSpec as P

BF = jnp.bfloat16
F32 = jnp.float32
ALL = ("y", "zh", "x", "zl", "c")
TP = ("x", "c")
REP = ("y", "zh", "zl")

FF = 5632
FP = 768
HD = 64
STEP = 10
ROWS = 1024
KEYS = 2048

norm_eps = 1e-05
beta_one = 0.9
beta_two = 0.95
adam_eps = 1e-08
big_negative = -1e30
step_rates = (0.15, 0.3, 0.06, 0.04, 2.0)
decay_rates = (0.1, 0.1, 0.1, 0.1, 0.0)


def flat_index(f, x, zl, c):
    return ((f * 4 + x) * 2 + zl) * 2 + c


SPREAD = [
    (t * 16 + k, flat_index(k // 2, t // 2, k % 2, t % 2)) for t in range(8) for k in range(16)
]


def back(route):
    return [(b, a) for a, b in route]


def adam_update(master, grad_sum, first_old, second_old, step_rate, decay_rate):
    first_new = beta_one * first_old + (1.0 - beta_one) * grad_sum
    second_new = beta_two * second_old + (1.0 - beta_two) * grad_sum * grad_sum
    first_fix = first_new / (1.0 - beta_one**STEP)
    second_fix = second_new / (1.0 - beta_two**STEP)
    master_new = master - step_rate * (
        first_fix / (jnp.sqrt(second_fix) + adam_eps) + decay_rate * master
    )
    return (first_new, second_new, master_new)


def dot_nn(a, b):
    return lax.dot_general(a, b, (((1,), (0,)), ((), ())), preferred_element_type=F32)


def dot_nt(a, b):
    return lax.dot_general(a, b, (((1,), (1,)), ((), ())), preferred_element_type=F32)


def dot_tn(a, b):
    return lax.dot_general(a, b, (((0,), (0,)), ((), ())), preferred_element_type=F32)


QB = 256


def takes(microseconds):
    return pl.CostEstimate(
        flops=int(microseconds * 1.15e9), bytes_accessed=1 << 20, transcendentals=0
    )


WHOLE = pl.BlockSpec(memory_space=pltpu.VMEM)
ANYWHERE = pl.BlockSpec(memory_space=pl.ANY)


def fixed(shape):
    return pl.BlockSpec(shape, lambda i: (0,) * len(shape), pipeline_mode=pl.Buffered(1))


def params(mib):
    return pltpu.CompilerParams(vmem_limit_bytes=mib * 1024 * 1024)


def natural_rows(block, piece):
    first = (block % 2) * 512 + (block // 2) * 64 + 128 * piece
    return pl.ds(pl.multiple_of(first, 64), 64)


def attend_kernel(first, q_ref, kv_ref, kp_ref, lo_ref, hi_ref, *rest):
    turned = rest[-1]

    @pl.when(pl.program_id(0) == 0)
    def _():
        turned[...] = kv_ref[...].T

    def over(count):
        key_pos = kp_ref[:count, :]
        high = hi_ref[...]
        allowed = (key_pos >= lo_ref[...]) & (key_pos <= high)
        keys = kv_ref[:count, :HD]
        for h in range(4):
            cols = slice(h * HD, (h + 1) * HD)
            row = slice(h, h + 1)
            s = jnp.where(allowed, dot_nt(keys, q_ref[:, cols]), big_negative)
            peak = jnp.max(s, axis=0, keepdims=True)
            if not first:
                out_before, peak_before, total_before = rest[:3]
                peak = jnp.maximum(peak, peak_before[row, :])
            p = jnp.exp(s - peak)
            total = jnp.sum(p, axis=0, keepdims=True)
            out = dot_nn(turned[HD:, :count], p.astype(BF))
            if first:
                out_ref, peak_ref, total_ref = rest[-4:-1]
                out_ref[cols, :] = out
                peak_ref[row, :] = peak
                total_ref[row, :] = total
            else:
                natural_ref, o_ref, lse_ref = rest[-4:-1]
                fade = jnp.exp(peak_before[row, :] - peak)
                total = total + fade * total_before[row, :]
                out = out + fade * out_before[cols, :]
                out = out * jnp.where(high >= 0, 1.0 / total, 0.0)
                out = out.T.astype(BF)
                o_ref[:, cols] = out
                for piece in range(4):
                    natural_ref[natural_rows(pl.program_id(0), piece), cols] = out[
                        64 * piece : 64 * piece + 64
                    ]
                lse_ref[row, :] = peak + jnp.log(total)

    pl.when(pl.program_id(0) < 2)(lambda: over(ROWS // 2))
    pl.when(pl.program_id(0) >= 2)(lambda: over(ROWS))


def attend(q, kv, kp, lo, hi, before, *earlier):
    first = before is None
    row = pl.BlockSpec((1, QB), lambda i: (0, i))
    rows = pl.BlockSpec((4, QB), lambda i: (0, i))
    flat = pl.BlockSpec((256, QB), lambda i: (0, i))
    block = pl.BlockSpec((QB, 256), lambda i: (i, 0))
    held = pl.BlockSpec((ROWS, 256), lambda i: (0, 0))
    stat = jax.ShapeDtypeStruct((4, ROWS), F32)
    result = jax.ShapeDtypeStruct((ROWS, 256), BF)
    carried = [] if first else list(before)
    return pl.pallas_call(
        functools.partial(attend_kernel, first),
        grid=(ROWS // QB,),
        in_specs=[block, fixed((ROWS, 2 * HD)), fixed((ROWS, QB)), row, row]
        + [flat, rows, rows][: len(carried)]
        + [ANYWHERE] * len(earlier),
        out_specs=[flat, rows, rows] if first else [held, block, rows],
        out_shape=[jax.ShapeDtypeStruct((256, ROWS), F32), stat, stat]
        if first
        else [result, result, stat],
        scratch_shapes=[pltpu.VMEM((2 * HD, ROWS), BF)],
        compiler_params=params(40),
        cost_estimate=takes(10),
        name="attend",
    )(q, kv, kp, lo, hi, *carried, *earlier)


def attend_back_kernel(first, q_ref, do_ref, o_ref, kv_ref, kp_ref, lo_ref, hi_ref, lse_ref, *rest):
    dq_ref, dkv_ref, turned, values = rest[-4:]

    @pl.when(pl.program_id(0) == 0)
    def _():
        dkv_ref[...] = jnp.zeros_like(dkv_ref)
        turned[...] = kv_ref[...].T
        values[...] = kv_ref[:, HD:]

    def over(count):
        key_pos = kp_ref[:count, :]
        allowed = (key_pos >= lo_ref[...]) & (key_pos <= hi_ref[...])
        keys = kv_ref[:count, :HD]
        delta_all = (do_ref[...].astype(F32) * o_ref[...].astype(F32)).T
        for h in range(4):
            cols = slice(h * HD, (h + 1) * HD)
            qh = q_ref[:, cols]
            doh = do_ref[:, cols]
            delta = jnp.sum(delta_all[cols], axis=0, keepdims=True)
            s = dot_nt(keys, qh)
            p = jnp.where(allowed, jnp.exp(s - lse_ref[h : h + 1, :]), 0.0)
            ds = (p * (dot_nt(values[:count, :], doh) - delta)).astype(BF)
            dkv_ref[:count, :HD] += dot_nn(ds, qh)
            dkv_ref[:count, HD:] += dot_nn(p.astype(BF), doh)
            dq = dot_nn(turned[:HD, :count], ds) * HD**-0.5
            if first:
                dq_ref[cols, :] = dq
            else:
                dq = (dq + rest[0][cols, :]).T.astype(BF)
                for piece in range(4):
                    dq_ref[natural_rows(pl.program_id(0), piece), cols] = dq[
                        64 * piece : 64 * piece + 64
                    ]

    pl.when(pl.program_id(0) < 2)(lambda: over(ROWS // 2))
    pl.when(pl.program_id(0) >= 2)(lambda: over(ROWS))


def attend_back(q, do, o, kv, kp, lo, hi, lse, earlier_dq, *earlier):
    first = earlier_dq is None
    row = pl.BlockSpec((1, QB), lambda i: (0, i))
    block = pl.BlockSpec((QB, 256), lambda i: (i, 0))
    flat = pl.BlockSpec((256, QB), lambda i: (0, i))
    held = lambda cols: pl.BlockSpec((ROWS, cols), lambda i: (0, 0))
    carried = [] if first else [earlier_dq]
    return pl.pallas_call(
        functools.partial(attend_back_kernel, first),
        grid=(ROWS // QB,),
        in_specs=[block, block, block, fixed((ROWS, 2 * HD)), fixed((ROWS, QB)), row, row]
        + [pl.BlockSpec((4, QB), lambda i: (0, i))]
        + [flat] * len(carried)
        + [ANYWHERE] * len(earlier),
        out_specs=[flat if first else held(256), held(2 * HD)],
        out_shape=[
            jax.ShapeDtypeStruct((256, ROWS), F32)
            if first
            else jax.ShapeDtypeStruct((ROWS, 256), BF),
            jax.ShapeDtypeStruct((ROWS, 2 * HD), F32),
        ],
        scratch_shapes=[pltpu.VMEM((2 * HD, ROWS), BF), pltpu.VMEM((ROWS, HD), BF)],
        compiler_params=params(40),
        cost_estimate=takes(10),
        name="attend_back",
    )(q, do, o, kv, kp, lo, hi, lse, *carried, *earlier)


def fetch(pieces, rows, sems):
    copies = [
        pltpu.make_async_copy(piece, rows.at[pl.ds(128 * k, 128), :], sems.at[k])
        for k, piece in enumerate(pieces)
    ]
    for copy in copies:
        copy.start()
    return copies


def project_kernel(*refs):
    pieces, raw_hbm = refs[:8], refs[8]
    q_ref, kv_ref, w_ref, w_out_ref, hat, raw_ref, sems, raw_sem = refs[9:]
    raw_copy = pltpu.make_async_copy(raw_hbm, raw_ref, raw_sem)
    raw_copy.start()
    copies = fetch(pieces, hat, sems)
    raw_copy.wait()
    for f in range(8):
        for zl in range(2):
            r = 2 * f + zl
            for x in range(4):
                row = 256 * f + 64 * x + 32 * zl
                w_ref[row : row + 32, :] = raw_ref[128 * r + 32 * x : 128 * r + 32 * x + 32, :384]
            for k in range(8):
                w_out_ref[16 * r : 16 * r + 16, 256 * k : 256 * k + 256] = raw_ref[
                    128 * r + 16 * k : 128 * r + 16 * k + 16, 384:
                ]
    for copy in copies:
        copy.wait()
    for k in range(2):
        rows = slice(512 * k, 512 * k + 512)
        product = dot_nn(hat[rows, :], w_ref[...]).astype(BF)
        for piece in range(4):
            for late in range(2):
                here = slice(128 * piece + 64 * late, 128 * piece + 64 * late + 64)
                there = 512 * late + 256 * k + 64 * piece
                q_ref[there : there + 64, :] = product[here, :256] * BF(HD**-0.5)
                kv_ref[there : there + 64, :] = product[here, 256:]


def project(pieces, raw):
    shape = lambda *dims: jax.ShapeDtypeStruct(dims, BF)
    return pl.pallas_call(
        project_kernel,
        in_specs=[ANYWHERE] * 9,
        out_specs=[WHOLE] * 4,
        out_shape=[shape(ROWS, 256), shape(ROWS, 128), shape(2048, 384), shape(256, 2048)],
        scratch_shapes=[
            pltpu.VMEM((ROWS, 2048), BF),
            pltpu.VMEM((2048, 640), BF),
            pltpu.SemaphoreType.DMA((8,)),
            pltpu.SemaphoreType.DMA,
        ],
        compiler_params=params(60),
        cost_estimate=takes(5),
        name="project",
    )(*pieces, raw)


def hidden_products_kernel(*refs):
    pieces = refs[:8]
    att_ref, w_ref = refs[8:10]
    grad_att_ref, sum_ref, grad, sems = refs[-4:]
    for copy in fetch(pieces, grad, sems):
        copy.wait()
    grad_att = dot_nt(grad[...], w_ref[...]).astype(BF)
    for piece in range(8):
        for late in range(2):
            here = 128 * piece + 64 * late
            there = 512 * late + 64 * piece
            grad_att_ref[there : there + 64, :] = grad_att[here : here + 64]
    for k in range(4):
        cols = slice(512 * k, 512 * k + 512)
        sum_ref[:, cols] = dot_tn(att_ref[...], grad[:, cols]).astype(BF)


def hidden_products(pieces, att, w_out, *earlier):
    return pl.pallas_call(
        hidden_products_kernel,
        in_specs=[ANYWHERE] * 8 + [WHOLE] * 2 + [ANYWHERE] * len(earlier),
        out_specs=[WHOLE] * 2,
        out_shape=[jax.ShapeDtypeStruct((ROWS, 256), BF), jax.ShapeDtypeStruct((256, 2048), BF)],
        scratch_shapes=[pltpu.VMEM((ROWS, 2048), BF), pltpu.SemaphoreType.DMA((8,))],
        compiler_params=params(60),
        cost_estimate=takes(6),
        name="hidden_products",
    )(*pieces, att, w_out, *earlier)


def feed_forward_kernel(*refs):
    hat_pieces, grad_pieces, ff_ref = refs[:8], refs[8:16], refs[16]
    hid_ref, grad_gu_ref, back_mine, back_other, ahead_mine, ahead_other = refs[17:23]
    w_gu_ref, w_down_ref, hat, grad, w_sems, hat_sems, grad_sems = refs[23:]
    step = pl.program_id(0)

    def copies(first, count):
        return (
            [
                pltpu.make_async_copy(
                    hat_pieces[k], hat.at[pl.ds(128 * k, 128), :], hat_sems.at[k]
                )
                for k in range(first, first + count)
            ],
            [
                pltpu.make_async_copy(
                    grad_pieces[k], grad.at[pl.ds(128 * k, 128), :], grad_sems.at[k]
                )
                for k in range(first, first + count)
            ],
        )

    gu_copies = [
        pltpu.make_async_copy(
            ff_ref.at[:, zl, pl.ds(0, 4)], w_gu_ref.at[:, :, zl], w_sems.at[zl]
        )
        for zl in range(2)
    ]
    down_copies = [
        pltpu.make_async_copy(
            ff_ref.at[:, :, 4], w_down_ref.at[:, :, pl.ds(0, 32), pl.ds(0, 1536)], w_sems.at[2]
        ),
        pltpu.make_async_copy(
            ff_ref.at[:, :, 5, pl.ds(0, 16)],
            w_down_ref.at[:, :, pl.ds(32, 16), pl.ds(0, 1536)],
            w_sems.at[3],
        ),
    ] + [
        pltpu.make_async_copy(
            ff_ref.at[:, :, 5, pl.ds(16, 16), pl.ds(512 * part, 512)],
            w_down_ref.at[:, :, pl.ds(16 * part, 16), pl.ds(1536, 512)],
            w_sems.at[4 + part],
        )
        for part in range(3)
    ]
    mine_hat, mine_grad = copies(0, 4)
    other_hat, other_grad = copies(4, 4)

    @pl.when(step == 0)
    def _():
        for copy in gu_copies + other_hat + down_copies + other_grad + mine_hat + mine_grad:
            copy.start()
        for copy in gu_copies + other_hat:
            copy.wait()

    @pl.when(step == 1)
    def _():
        for copy in mine_hat + mine_grad:
            copy.wait()

    rows = pl.ds(pl.multiple_of((1 - step) * 512, 512), 512)
    w_gu = w_gu_ref[...].reshape(2048, 2 * FP)
    gate_up_val = dot_nn(hat[rows, :], w_gu)
    gate = gate_up_val[:, :FP]
    up = gate_up_val[:, FP:]
    sig = jax.nn.sigmoid(gate)
    silu = gate * sig
    hid_ref[...] = (silu * up).astype(BF)

    @pl.when(step == 0)
    def _():
        for copy in down_copies + other_grad:
            copy.wait()

    w_down = w_down_ref[...].reshape(FP, 2048)
    grad_hid = dot_nt(grad[rows, :], w_down)
    grad_gu_ref[:, :FP] = (grad_hid * up * sig * (1.0 + gate * (1.0 - sig))).astype(BF)
    grad_gu_ref[:, FP:] = (grad_hid * silu).astype(BF)
    for back_ref, ahead_ref, now in ((back_other, ahead_other, 0), (back_mine, ahead_mine, 1)):

        @pl.when(step == now)
        def _():
            for k in range(2):
                cols = slice(1024 * k, 1024 * k + 1024)
                w_cols = w_gu_ref[4 * k : 4 * k + 4].reshape(1024, 2 * FP)
                back_ref[:, cols] = dot_nt(grad_gu_ref[...], w_cols).astype(BF)
                w_cols = w_down_ref[:, :, :, cols].reshape(FP, 1024)
                ahead_ref[:, cols] = dot_nn(hid_ref[...], w_cols).astype(BF)


def feed_forward(hat_pieces, grad_pieces, ff_all):
    block = lambda cols: pl.BlockSpec((512, cols), lambda i: (1 - i, 0))
    held = pl.BlockSpec((512, 2048), lambda i: (0, 0))
    shape = lambda rows, cols: jax.ShapeDtypeStruct((rows, cols), BF)
    half = shape(ROWS // 2, 2048)
    return pl.pallas_call(
        feed_forward_kernel,
        grid=(2,),
        in_specs=[ANYWHERE] * 17,
        out_specs=[block(FP), block(2 * FP)] + [held] * 4,
        out_shape=[shape(ROWS, FP), shape(ROWS, 2 * FP)] + [half] * 4,
        scratch_shapes=[
            pltpu.VMEM((8, 4, 2, 32, 2 * FP), BF),
            pltpu.VMEM((8, 2, 48, 2048), BF),
            pltpu.VMEM((ROWS, 2048), BF),
            pltpu.VMEM((ROWS, 2048), BF),
            pltpu.SemaphoreType.DMA((7,)),
            pltpu.SemaphoreType.DMA((8,)),
            pltpu.SemaphoreType.DMA((8,)),
        ],
        compiler_params=params(60),
        cost_estimate=takes(28),
        name="feed_forward",
    )(*hat_pieces, *grad_pieces, ff_all.reshape(8, 2, 6, 32, 1536))


def weight_grads_kernel(*refs):
    hat_pieces, grad_pieces = refs[:8], refs[8:16]
    grad_gu_ref, hid_ref = refs[16:18]
    out_ref, hid_t, grad, hat = refs[-4:]

    @pl.when(pl.program_id(0) == 0)
    def _():
        hid_t[...] = hid_ref[...].T
        for k in range(8):
            grad[128 * k : 128 * k + 128, :] = grad_pieces[k][...]

    for k in range(8):
        hat[128 * k : 128 * k + 128, :] = hat_pieces[k][...]
    for half in range(2):
        total = dot_tn(hat[:, 256 * half : 256 * half + 256], grad_gu_ref[...])
        total = total.astype(BF).reshape(4, 2, 32, 2 * FP)
        for zl in range(2):
            out_ref[2 * half + zl, :128, :] = total[:, zl].reshape(128, 2 * FP)
    rows = pl.ds(pl.multiple_of(pl.program_id(0) * 192, 64), 192)
    total = dot_nn(hid_t[rows, :], grad[...]).astype(BF).reshape(4, 48, 2048)
    out_ref[:, 128:176, :] = total[:, :, :1536]
    for part in range(3):
        out_ref[:, 176:192, 512 * part : 512 * part + 512] = total[:, 16 * part : 16 * part + 16, 1536:]


def weight_grads(hat_pieces, grad_pieces, grad_gu, hid, *earlier):
    return pl.pallas_call(
        weight_grads_kernel,
        grid=(4,),
        in_specs=[pl.BlockSpec((128, 512), lambda j: (0, j))] * 8
        + [fixed((128, 2048))] * 8
        + [fixed((ROWS, 2 * FP)), fixed((ROWS, FP))]
        + [ANYWHERE] * len(earlier),
        out_specs=pl.BlockSpec((4, 192, 1536), lambda j: (j, 0, 0)),
        out_shape=jax.ShapeDtypeStruct((16, 192, 1536), BF),
        scratch_shapes=[
            pltpu.VMEM((FP, ROWS), BF),
            pltpu.VMEM((ROWS, 2048), BF),
            pltpu.VMEM((ROWS, 512), BF),
        ],
        compiler_params=params(56),
        cost_estimate=takes(16.5),
        name="weight_grads",
    )(*hat_pieces, *grad_pieces, grad_gu, hid, *earlier)


def ff_columns():
    for f in range(8):
        for x in range(4):
            for zl in range(2):
                for c in range(2):
                    for g in range(2):
                        yield (
                            x * 2 + c,
                            g * FP + (f * 2 + zl) * 48,
                            g * FF + flat_index(f, x, zl, c) * 44,
                        )


def pack_kernel(qkv_ref, gate_up_ref, gains_ref, out_ref, scaled_qkv, scaled, packed):
    gains = gains_ref[...]
    scaled_qkv[...] = qkv_ref[...].astype(BF).astype(F32) * gains[:, 0:1]
    scaled[...] = gate_up_ref[...].astype(BF).astype(F32) * gains[:, 1:2]
    packed[...] = jnp.zeros_like(packed)
    for rank in range(8):
        head = 2048 + rank // 2 * HD
        packed[rank, :, :256] = scaled_qkv[:, rank * 256 : rank * 256 + 256]
        packed[rank, :, 256:320] = scaled_qkv[:, head : head + HD]
        packed[rank, :, 320:384] = scaled_qkv[:, head + 256 : head + 256 + HD]
    for rank, there, here in ff_columns():
        packed[rank, :, 384 + there : 384 + there + 44] = scaled[:, here : here + 44]
    out_ref[...] = packed[...].astype(BF)


def pack(qkv, gate_up, gains):
    return pl.pallas_call(
        pack_kernel,
        in_specs=[WHOLE] * 3,
        out_specs=WHOLE,
        out_shape=jax.ShapeDtypeStruct((8, 16, 1920), BF),
        scratch_shapes=[
            pltpu.VMEM((16, 2560), F32),
            pltpu.VMEM((16, 2 * FF), F32),
            pltpu.VMEM((8, 16, 1920), F32),
        ],
        compiler_params=params(24),
        cost_estimate=takes(3),
        name="pack",
    )(qkv, gate_up, gains)


def update_kernel(
    got_ref, master_ref, gain_ref, first_ref, second_ref, new_first, new_second, new_master, gain_sum, packed, sums
):
    packed[...] = got_ref[...].astype(F32)
    for rank, there, here in ff_columns():
        sums[:, here : here + 44] = packed[rank, :, 384 + there : 384 + there + 44]
    master = master_ref[...]
    gain_sum[...] = jnp.sum(
        master.astype(BF).astype(F32) * sums[...], axis=1, keepdims=True
    )
    new_first[...], new_second[...], new_master[...] = adam_update(
        master,
        sums[...] * gain_ref[...],
        first_ref[...],
        second_ref[...],
        step_rates[2],
        decay_rates[2],
    )


def update_gate_up(got, master, gain, first, second):
    shape = jax.ShapeDtypeStruct((16, 2 * FF), F32)
    return pl.pallas_call(
        update_kernel,
        in_specs=[WHOLE] * 5,
        out_specs=[WHOLE] * 4,
        out_shape=[shape, shape, shape, jax.ShapeDtypeStruct((16, 1), F32)],
        scratch_shapes=[pltpu.VMEM((8, 16, 1920), F32), pltpu.VMEM((16, 2 * FF), F32)],
        compiler_params=params(32),
        cost_estimate=takes(4),
        name="update_gate_up",
    )(got, master, gain, first, second)


def shift(block, distance):
    return lax.ppermute(block, "x", [(i, (i + distance) % 4) for i in range(4)])


def swap(block):
    return lax.ppermute(block, "c", [(0, 1), (1, 0)])


ORDER = ((0, 0), (1, 0), (3, 0), (2, 0), (0, 1), (1, 1), (3, 1), (2, 1))


def tie_kernel(*refs):
    pass


def tie(value, *earlier):
    anywhere = pl.BlockSpec(memory_space=pl.ANY)
    return pl.pallas_call(
        tie_kernel,
        in_specs=[anywhere] * (1 + len(earlier)),
        out_specs=anywhere,
        out_shape=jax.ShapeDtypeStruct(value.shape, value.dtype),
        input_output_aliases={0: 0},
        cost_estimate=pl.CostEstimate(flops=0, bytes_accessed=0, transcendentals=0),
        name="tie",
    )(value, *earlier)


def gather_pieces(block):
    mine = [block, shift(block, 1), shift(block, -1), shift(block, 2)]
    return mine + [swap(piece) for piece in mine]


def scatter_first(mine, other):
    return mine.astype(F32) + swap(other).astype(F32)


def scatter_second(mine):
    far = mine[384:].astype(BF)
    by_left = shift(far[:64], -1)
    by_right = shift(far[64:], 1)
    to_left = jnp.concatenate([mine[128:192] + by_left.astype(F32), mine[192:256]], axis=0)
    to_right = jnp.concatenate([mine[256:320], mine[320:384] + by_right.astype(F32)], axis=0)
    return to_left.astype(BF), to_right.astype(BF), mine[:128]


def scatter_third(to_left, to_right):
    return shift(to_left, -1), shift(to_right, 1)


def total(parts):
    first, second, third = parts
    return first.astype(F32) + second.astype(F32) + third.astype(F32)


def attn_grads_kernel(*refs):
    pieces = refs[:8]
    mixed_ref, out_grad_ref, sum_ref, hat, sems = refs[8:]
    copies = fetch(pieces, hat, sems)
    for r in range(16):
        for k in range(8):
            sum_ref[r, 16 * k : 16 * k + 16, 384:] = out_grad_ref[
                16 * r : 16 * r + 16, 256 * k : 256 * k + 256
            ]
    for copy in copies:
        copy.wait()
    for f in range(8):
        total = dot_tn(hat[:, 256 * f : 256 * f + 256], mixed_ref[...])
        total = total.astype(BF).reshape(4, 2, 32, 384)
        for zl in range(2):
            sum_ref[2 * f + zl, :, :384] = total[:, zl].reshape(128, 384)


def attn_grads(pieces, grad_mixed, sum_out):
    return pl.pallas_call(
        attn_grads_kernel,
        in_specs=[ANYWHERE] * 8 + [WHOLE] * 2,
        out_specs=WHOLE,
        out_shape=jax.ShapeDtypeStruct((16, 128, 640), BF),
        scratch_shapes=[pltpu.VMEM((ROWS, 2048), BF), pltpu.SemaphoreType.DMA((8,))],
        compiler_params=params(60),
        cost_estimate=takes(4),
        name="attn_grads",
    )(*pieces, grad_mixed, sum_out)


def row_positions(span_order, zl):
    x = lax.axis_index("x")
    c = lax.axis_index("c")
    holders = jnp.stack([((x - dx) % 4 * 2 + zl) * 2 + (c + dc) % 2 for dx, dc in ORDER])
    picked = (holders[:, None] == jnp.arange(16, dtype=jnp.int32)[None, :]).astype(jnp.int32)
    spans = jnp.sum(picked[:, :, None] * span_order.reshape(1, 16, 2), axis=1)
    spans = spans.T.reshape(16, 1)
    return (spans * 64 + jnp.arange(64, dtype=jnp.int32)[None, :]).reshape(ROWS)


def norm_scale(rows):
    return lax.rsqrt(jnp.mean(rows * rows, axis=-1, keepdims=True) + norm_eps)


def norm_back(grad_hat, hat, scale, rest):
    return rest + scale * (grad_hat - hat * jnp.mean(grad_hat * hat, axis=-1, keepdims=True))


def body(
    tokens,
    out_grad,
    seq_lengths,
    span_order,
    attn_in,
    attn_out,
    gate_up,
    down_proj,
    norm_gains,
    first_attn_in,
    second_attn_in,
    first_attn_out,
    second_attn_out,
    first_gate_up,
    second_gate_up,
    first_down_proj,
    second_down_proj,
    first_norm_gains,
    second_norm_gains,
):
    zl = lax.axis_index("zl")
    gains = norm_gains.astype(BF).astype(F32)
    gain_one = gains[0][:, None]
    gain_two = gains[1][:, None]
    low_qkv = attn_in.astype(BF).astype(F32)

    inputs = tokens.astype(F32)
    scale_one = norm_scale(inputs)
    hat_one = inputs * scale_one
    packed = pack(attn_in, gate_up, gains.T)
    ranked = lax.all_to_all(packed, TP, 0, 0, tiled=True).reshape(128, 1920)
    hat_pieces = gather_pieces(tie(hat_one.astype(BF), ranked))
    out_part = lax.ppermute(attn_out.astype(BF), ALL, SPREAD)
    out_part = out_part.reshape(16, 8, 256).transpose(1, 0, 2).reshape(128, 256)
    attn_part = jnp.concatenate([ranked[:, :384], out_part], axis=1)
    attn_all = lax.all_gather(attn_part, REP, axis=0, tiled=True)
    down_rows = jnp.pad(down_proj.astype(BF), ((0, 4), (0, 0)))
    down_tail = [down_rows[16 * part : 16 * part + 16, 1536:] for part in range(3)]
    ff_part = jnp.concatenate(
        [ranked[:, 384:], down_rows[:, :1536], jnp.concatenate(down_tail, axis=1)], axis=0
    )
    grad_pieces = gather_pieces(tie(out_grad, *hat_pieces[1:4]))
    ff_all = lax.all_gather(
        tie(ff_part, attn_all, *hat_pieces[1:]), REP, axis=0, tiled=True
    )

    own_pos = row_positions(span_order, zl)
    other_pos = row_positions(span_order, 1 - zl)
    lengths = seq_lengths[0]
    bound_one = lengths[0]
    bound_two = lengths[0] + lengths[1]
    low_pos = jnp.where(own_pos < bound_one, 0, bound_one)[None, :]
    high_pos = jnp.where(own_pos < bound_two, own_pos, -1)[None, :]
    key_pos = jnp.concatenate([own_pos, other_pos])
    key_pos = jnp.broadcast_to(key_pos[:, None], (KEYS, QB))

    queries, own_kv, w_qkv, w_out = project(hat_pieces, attn_all)
    other_kv = lax.ppermute(own_kv, "zl", [(0, 1), (1, 0)])
    before = attend(queries, own_kv, key_pos[:ROWS], low_pos, high_pos, None)
    att, att_early, lse = attend(
        queries, other_kv, key_pos[ROWS:], low_pos, high_pos, before, *grad_pieces[1:4]
    )
    att_other = dot_nn(att[512:], w_out).astype(BF)
    att_mine = dot_nn(att[:512], w_out)
    to_left, to_right, stays = scatter_second(scatter_first(att_mine, att_other))
    hidden = inputs + total((stays, *scatter_third(to_left, to_right)))

    scale_two = norm_scale(hidden)
    hat_two = hidden * scale_two
    hat_two_pieces = gather_pieces(hat_two.astype(BF))
    hid, grad_gu, back_mine, back_other, ahead_mine, ahead_other = feed_forward(
        hat_two_pieces, grad_pieces, ff_all
    )
    to_left, to_right, stays = scatter_second(scatter_first(back_mine, back_other))
    grad_hat_two = total((stays, *scatter_third(to_left, to_right)))
    grad_hidden = norm_back(grad_hat_two, hat_two, scale_two, out_grad.astype(F32))
    sums = weight_grads(hat_two_pieces, grad_pieces, grad_gu, hid, to_left, to_right)
    sums = sums.reshape(16 * 192, 1536)
    grad_hidden_low = tie(grad_hidden.astype(BF), sums)
    hidden_pieces = gather_pieces(grad_hidden_low)
    sums = lax.psum_scatter(tie(sums, grad_hidden_low), REP, scatter_dimension=0, tiled=True)
    ahead = scatter_first(ahead_mine, tie(ahead_other, hidden_pieces[0]))
    grad_att, sum_out = hidden_products(hidden_pieces, att, w_out, ahead)

    grad_q, grad_kv = attend_back(
        queries, grad_att, att_early, other_kv, key_pos[ROWS:], low_pos, high_pos, lse, None, ahead
    )
    arrived = lax.ppermute(grad_kv.astype(BF), "zl", [(0, 1), (1, 0)])
    ahead_left, ahead_right, ahead_stays = scatter_second(ahead)
    grad_q, grad_kv = attend_back(
        queries,
        grad_att,
        att_early,
        own_kv,
        key_pos[:ROWS],
        low_pos,
        high_pos,
        lse,
        grad_q,
        ahead_left,
        ahead_right,
    )
    ahead = scatter_third(ahead_left, ahead_right)
    block_out = (hidden + total((ahead_stays, *ahead))).astype(BF)
    grad_kv = (grad_kv + arrived.astype(F32)).astype(BF)
    grad_kv = grad_kv.reshape(2, 8, 64, 2 * HD).transpose(1, 0, 2, 3).reshape(ROWS, 2 * HD)
    grad_mixed = jnp.concatenate([grad_q, grad_kv], axis=1)
    grad_mixed = tie(grad_mixed, *ahead)
    attn_parts = attn_grads(hat_pieces, grad_mixed, sum_out)
    attn_sums = lax.all_to_all(attn_parts, REP, 0, 0, tiled=True)
    attn_sums = jnp.sum(attn_sums.astype(F32), axis=0).astype(BF)
    last_rows = tie(grad_mixed, attn_parts)
    last_other = dot_nt(last_rows[512:], w_qkv).astype(BF)
    last_mine = dot_nt(last_rows[:512], w_qkv)
    to_left, to_right, stays = scatter_second(scatter_first(last_mine, last_other))
    last_thirds = scatter_third(to_left, to_right)
    got = jnp.concatenate([attn_sums[:, :384], sums[:128]], axis=1).reshape(8, 16, 1920)
    grad_hat_one = total((tie(stays, got), *last_thirds))
    in_grad = norm_back(grad_hat_one, hat_one, scale_one, grad_hidden).astype(BF)
    sum_out = tie(attn_sums[:, 384:], got)
    got = lax.all_to_all(got, TP, 0, 0, tiled=True)
    got_qkv = got[:, :, :384].transpose(1, 0, 2).astype(F32)
    got_kv = got_qkv[:, :, 256:].reshape(16, 4, 2, 2, HD).sum(axis=2)
    got_qkv = jnp.concatenate(
        [
            got_qkv[:, :, :256].reshape(16, 2048),
            got_kv[:, :, 0].reshape(16, 256),
            got_kv[:, :, 1].reshape(16, 256),
        ],
        axis=1,
    )
    sum_out = sum_out.reshape(8, 16, 256).transpose(1, 0, 2).reshape(16, 2048)
    got_out = lax.ppermute(sum_out, ALL, back(SPREAD)).astype(F32)
    tail = [sums[176:192, 512 * part : 512 * part + 512] for part in range(3)]
    got_down = jnp.concatenate([sums[128:176], jnp.concatenate(tail, axis=0)], axis=1)
    got_down = got_down[:44].astype(F32)
    gu_new = update_gate_up(got, gate_up, gain_two, first_gate_up, second_gate_up)
    gain_sums = jnp.stack([jnp.sum(low_qkv * got_qkv, axis=1), gu_new[3][:, 0]], axis=0)
    qkv_new = adam_update(
        attn_in, got_qkv * gain_one, first_attn_in, second_attn_in, step_rates[0], decay_rates[0]
    )
    out_new = adam_update(
        attn_out, got_out, first_attn_out, second_attn_out, step_rates[1], decay_rates[1]
    )
    down_new = adam_update(
        down_proj, got_down, first_down_proj, second_down_proj, step_rates[3], decay_rates[3]
    )
    gains_new = adam_update(
        norm_gains, gain_sums, first_norm_gains, second_norm_gains, step_rates[4], decay_rates[4]
    )
    return (block_out, in_grad, *qkv_new, *out_new, *gu_new[:3], *down_new, *gains_new)


def solution(mesh):
    split = Mesh(mesh.devices.reshape(4, 2, 4, 2, 2), ALL)
    rows = P(ALL, None)
    cols = P(None, ALL)
    group = P(("y", "zh"), None)
    in_specs = (rows, rows, group, P()) + (rows,) * 4 + (cols,) + (rows,) * 8 + (cols,) * 2
    out_specs = (rows,) * 14 + (cols,) * 3
    return jax.shard_map(body, mesh=split, in_specs=in_specs, out_specs=out_specs, check_vma=False)
```

```python
import functools

import jax
import jax.numpy as jnp
from jax import lax
from jax.experimental import pallas as pl
from jax.experimental.pallas import tpu as pltpu
from jax.sharding import Mesh
from jax.sharding import PartitionSpec as P

BF = jnp.bfloat16
F32 = jnp.float32
ALL = ("y", "zh", "x", "zl", "c")
TP = ("x", "c")
REP = ("y", "zh", "zl")

FF = 5632
FP = 768
HD = 64
STEP = 10
ROWS = 1024
KEYS = 2048

norm_eps = 1e-05
beta_one = 0.9
beta_two = 0.95
adam_eps = 1e-08
big_negative = -1e30
step_rates = (0.15, 0.3, 0.06, 0.04, 2.0)
decay_rates = (0.1, 0.1, 0.1, 0.1, 0.0)


def flat_index(f, x, zl, c):
    return ((f * 4 + x) * 2 + zl) * 2 + c


SPREAD = [
    (t * 16 + k, flat_index(k // 2, t // 2, k % 2, t % 2)) for t in range(8) for k in range(16)
]


def back(route):
    return [(b, a) for a, b in route]


def adam_update(master, grad_sum, first_old, second_old, step_rate, decay_rate):
    first_new = beta_one * first_old + (1.0 - beta_one) * grad_sum
    second_new = beta_two * second_old + (1.0 - beta_two) * grad_sum * grad_sum
    first_fix = first_new / (1.0 - beta_one**STEP)
    second_fix = second_new / (1.0 - beta_two**STEP)
    master_new = master - step_rate * (
        first_fix / (jnp.sqrt(second_fix) + adam_eps) + decay_rate * master
    )
    return (first_new, second_new, master_new)


def dot_nn(a, b):
    return lax.dot_general(a, b, (((1,), (0,)), ((), ())), preferred_element_type=F32)


def dot_nt(a, b):
    return lax.dot_general(a, b, (((1,), (1,)), ((), ())), preferred_element_type=F32)


def dot_tn(a, b):
    return lax.dot_general(a, b, (((0,), (0,)), ((), ())), preferred_element_type=F32)


QB = 256


def takes(microseconds):
    return pl.CostEstimate(
        flops=int(microseconds * 1.15e9), bytes_accessed=1 << 20, transcendentals=0
    )


WHOLE = pl.BlockSpec(memory_space=pltpu.VMEM)
ANYWHERE = pl.BlockSpec(memory_space=pl.ANY)


def fixed(shape):
    return pl.BlockSpec(shape, lambda i: (0,) * len(shape), pipeline_mode=pl.Buffered(1))


def params(mib):
    return pltpu.CompilerParams(vmem_limit_bytes=mib * 1024 * 1024)


def natural_rows(block, piece):
    first = (block % 2) * 512 + (block // 2) * 64 + 128 * piece
    return pl.ds(pl.multiple_of(first, 64), 64)


def attend_kernel(first, q_ref, kv_ref, kp_ref, lo_ref, hi_ref, *rest):
    turned = rest[-1]

    @pl.when(pl.program_id(0) == 0)
    def _():
        turned[...] = kv_ref[...].T

    def over(count):
        key_pos = kp_ref[:count, :]
        high = hi_ref[...]
        allowed = (key_pos >= lo_ref[...]) & (key_pos <= high)
        keys = kv_ref[:count, :HD]
        for h in range(4):
            cols = slice(h * HD, (h + 1) * HD)
            row = slice(h, h + 1)
            s = jnp.where(allowed, dot_nt(keys, q_ref[:, cols]), big_negative)
            peak = jnp.max(s, axis=0, keepdims=True)
            if not first:
                out_before, peak_before, total_before = rest[:3]
                peak = jnp.maximum(peak, peak_before[row, :])
            p = jnp.exp(s - peak)
            total = jnp.sum(p, axis=0, keepdims=True)
            out = dot_nn(turned[HD:, :count], p.astype(BF))
            if first:
                out_ref, peak_ref, total_ref = rest[-4:-1]
                out_ref[cols, :] = out
                peak_ref[row, :] = peak
                total_ref[row, :] = total
            else:
                natural_ref, o_ref, lse_ref = rest[-4:-1]
                fade = jnp.exp(peak_before[row, :] - peak)
                total = total + fade * total_before[row, :]
                out = out + fade * out_before[cols, :]
                out = out * jnp.where(high >= 0, 1.0 / total, 0.0)
                out = out.T.astype(BF)
                o_ref[:, cols] = out
                for piece in range(4):
                    natural_ref[natural_rows(pl.program_id(0), piece), cols] = out[
                        64 * piece : 64 * piece + 64
                    ]
                lse_ref[row, :] = peak + jnp.log(total)

    pl.when(pl.program_id(0) < 2)(lambda: over(ROWS // 2))
    pl.when(pl.program_id(0) >= 2)(lambda: over(ROWS))


def attend(q, kv, kp, lo, hi, before, *earlier):
    first = before is None
    row = pl.BlockSpec((1, QB), lambda i: (0, i))
    rows = pl.BlockSpec((4, QB), lambda i: (0, i))
    flat = pl.BlockSpec((256, QB), lambda i: (0, i))
    block = pl.BlockSpec((QB, 256), lambda i: (i, 0))
    held = pl.BlockSpec((ROWS, 256), lambda i: (0, 0))
    stat = jax.ShapeDtypeStruct((4, ROWS), F32)
    result = jax.ShapeDtypeStruct((ROWS, 256), BF)
    carried = [] if first else list(before)
    return pl.pallas_call(
        functools.partial(attend_kernel, first),
        grid=(ROWS // QB,),
        in_specs=[block, fixed((ROWS, 2 * HD)), fixed((ROWS, QB)), row, row]
        + [flat, rows, rows][: len(carried)]
        + [ANYWHERE] * len(earlier),
        out_specs=[flat, rows, rows] if first else [held, block, rows],
        out_shape=[jax.ShapeDtypeStruct((256, ROWS), F32), stat, stat]
        if first
        else [result, result, stat],
        scratch_shapes=[pltpu.VMEM((2 * HD, ROWS), BF)],
        compiler_params=params(40),
        cost_estimate=takes(10),
        name="attend",
    )(q, kv, kp, lo, hi, *carried, *earlier)


def attend_back_kernel(first, q_ref, do_ref, o_ref, kv_ref, kp_ref, lo_ref, hi_ref, lse_ref, *rest):
    dq_ref, dkv_ref, turned, values = rest[-4:]

    @pl.when(pl.program_id(0) == 0)
    def _():
        dkv_ref[...] = jnp.zeros_like(dkv_ref)
        turned[...] = kv_ref[...].T
        values[...] = kv_ref[:, HD:]

    def over(count):
        key_pos = kp_ref[:count, :]
        allowed = (key_pos >= lo_ref[...]) & (key_pos <= hi_ref[...])
        keys = kv_ref[:count, :HD]
        delta_all = (do_ref[...].astype(F32) * o_ref[...].astype(F32)).T
        for h in range(4):
            cols = slice(h * HD, (h + 1) * HD)
            qh = q_ref[:, cols]
            doh = do_ref[:, cols]
            delta = jnp.sum(delta_all[cols], axis=0, keepdims=True)
            s = dot_nt(keys, qh)
            p = jnp.where(allowed, jnp.exp(s - lse_ref[h : h + 1, :]), 0.0)
            ds = (p * (dot_nt(values[:count, :], doh) - delta)).astype(BF)
            dkv_ref[:count, :HD] += dot_nn(ds, qh)
            dkv_ref[:count, HD:] += dot_nn(p.astype(BF), doh)
            dq = dot_nn(turned[:HD, :count], ds) * HD**-0.5
            if first:
                dq_ref[cols, :] = dq
            else:
                dq = (dq + rest[0][cols, :]).T.astype(BF)
                for piece in range(4):
                    dq_ref[natural_rows(pl.program_id(0), piece), cols] = dq[
                        64 * piece : 64 * piece + 64
                    ]

    pl.when(pl.program_id(0) < 2)(lambda: over(ROWS // 2))
    pl.when(pl.program_id(0) >= 2)(lambda: over(ROWS))


def attend_back(q, do, o, kv, kp, lo, hi, lse, earlier_dq, *earlier):
    first = earlier_dq is None
    row = pl.BlockSpec((1, QB), lambda i: (0, i))
    block = pl.BlockSpec((QB, 256), lambda i: (i, 0))
    flat = pl.BlockSpec((256, QB), lambda i: (0, i))
    held = lambda cols: pl.BlockSpec((ROWS, cols), lambda i: (0, 0))
    carried = [] if first else [earlier_dq]
    return pl.pallas_call(
        functools.partial(attend_back_kernel, first),
        grid=(ROWS // QB,),
        in_specs=[block, block, block, fixed((ROWS, 2 * HD)), fixed((ROWS, QB)), row, row]
        + [pl.BlockSpec((4, QB), lambda i: (0, i))]
        + [flat] * len(carried)
        + [ANYWHERE] * len(earlier),
        out_specs=[flat if first else held(256), held(2 * HD)],
        out_shape=[
            jax.ShapeDtypeStruct((256, ROWS), F32)
            if first
            else jax.ShapeDtypeStruct((ROWS, 256), BF),
            jax.ShapeDtypeStruct((ROWS, 2 * HD), F32),
        ],
        scratch_shapes=[pltpu.VMEM((2 * HD, ROWS), BF), pltpu.VMEM((ROWS, HD), BF)],
        compiler_params=params(40),
        cost_estimate=takes(10),
        name="attend_back",
    )(q, do, o, kv, kp, lo, hi, lse, *carried, *earlier)


def fetch(pieces, rows, sems):
    copies = [
        pltpu.make_async_copy(piece, rows.at[pl.ds(128 * k, 128), :], sems.at[k])
        for k, piece in enumerate(pieces)
    ]
    for copy in copies:
        copy.start()
    return copies


def project_kernel(*refs):
    pieces, raw_hbm = refs[:8], refs[8]
    q_ref, kv_ref, w_ref, w_out_ref, hat, raw_ref, sems, raw_sem = refs[9:]
    raw_copy = pltpu.make_async_copy(raw_hbm, raw_ref, raw_sem)
    raw_copy.start()
    copies = fetch(pieces, hat, sems)
    raw_copy.wait()
    for f in range(8):
        for zl in range(2):
            r = 2 * f + zl
            for x in range(4):
                row = 256 * f + 64 * x + 32 * zl
                w_ref[row : row + 32, :] = raw_ref[128 * r + 32 * x : 128 * r + 32 * x + 32, :384]
            for k in range(8):
                w_out_ref[16 * r : 16 * r + 16, 256 * k : 256 * k + 256] = raw_ref[
                    128 * r + 16 * k : 128 * r + 16 * k + 16, 384:
                ]
    for copy in copies:
        copy.wait()
    for k in range(2):
        rows = slice(512 * k, 512 * k + 512)
        product = dot_nn(hat[rows, :], w_ref[...]).astype(BF)
        for piece in range(4):
            for late in range(2):
                here = slice(128 * piece + 64 * late, 128 * piece + 64 * late + 64)
                there = 512 * late + 256 * k + 64 * piece
                q_ref[there : there + 64, :] = product[here, :256] * BF(HD**-0.5)
                kv_ref[there : there + 64, :] = product[here, 256:]


def project(pieces, raw):
    shape = lambda *dims: jax.ShapeDtypeStruct(dims, BF)
    return pl.pallas_call(
        project_kernel,
        in_specs=[ANYWHERE] * 9,
        out_specs=[WHOLE] * 4,
        out_shape=[shape(ROWS, 256), shape(ROWS, 128), shape(2048, 384), shape(256, 2048)],
        scratch_shapes=[
            pltpu.VMEM((ROWS, 2048), BF),
            pltpu.VMEM((2048, 640), BF),
            pltpu.SemaphoreType.DMA((8,)),
            pltpu.SemaphoreType.DMA,
        ],
        compiler_params=params(60),
        cost_estimate=takes(5),
        name="project",
    )(*pieces, raw)


def hidden_products_kernel(*refs):
    pieces = refs[:8]
    att_ref, w_ref = refs[8:10]
    grad_att_ref, sum_ref, grad, sems = refs[-4:]
    for copy in fetch(pieces, grad, sems):
        copy.wait()
    grad_att = dot_nt(grad[...], w_ref[...]).astype(BF)
    for piece in range(8):
        for late in range(2):
            here = 128 * piece + 64 * late
            there = 512 * late + 64 * piece
            grad_att_ref[there : there + 64, :] = grad_att[here : here + 64]
    for k in range(4):
        cols = slice(512 * k, 512 * k + 512)
        sum_ref[:, cols] = dot_tn(att_ref[...], grad[:, cols]).astype(BF)


def hidden_products(pieces, att, w_out, *earlier):
    return pl.pallas_call(
        hidden_products_kernel,
        in_specs=[ANYWHERE] * 8 + [WHOLE] * 2 + [ANYWHERE] * len(earlier),
        out_specs=[WHOLE] * 2,
        out_shape=[jax.ShapeDtypeStruct((ROWS, 256), BF), jax.ShapeDtypeStruct((256, 2048), BF)],
        scratch_shapes=[pltpu.VMEM((ROWS, 2048), BF), pltpu.SemaphoreType.DMA((8,))],
        compiler_params=params(40),
        cost_estimate=takes(6),
        name="hidden_products",
    )(*pieces, att, w_out, *earlier)


def feed_forward_kernel(*refs):
    hat_pieces, grad_pieces, ff_ref = refs[:8], refs[8:16], refs[16]
    hid_ref, grad_gu_ref, back_mine, back_other, ahead_mine, ahead_other = refs[17:23]
    w_gu_ref, w_down_ref, hat, grad, w_sems, hat_sems, grad_sems = refs[23:]
    step = pl.program_id(0)

    def copies(first, count):
        return (
            [
                pltpu.make_async_copy(
                    hat_pieces[k], hat.at[pl.ds(128 * k, 128), :], hat_sems.at[k]
                )
                for k in range(first, first + count)
            ],
            [
                pltpu.make_async_copy(
                    grad_pieces[k], grad.at[pl.ds(128 * k, 128), :], grad_sems.at[k]
                )
                for k in range(first, first + count)
            ],
        )

    gu_copies = [
        pltpu.make_async_copy(
            ff_ref.at[:, zl, pl.ds(0, 4)], w_gu_ref.at[:, :, zl], w_sems.at[zl]
        )
        for zl in range(2)
    ]
    down_copies = [
        pltpu.make_async_copy(
            ff_ref.at[:, :, 4], w_down_ref.at[:, :, pl.ds(0, 32), pl.ds(0, 1536)], w_sems.at[2]
        ),
        pltpu.make_async_copy(
            ff_ref.at[:, :, 5, pl.ds(0, 16)],
            w_down_ref.at[:, :, pl.ds(32, 16), pl.ds(0, 1536)],
            w_sems.at[3],
        ),
    ] + [
        pltpu.make_async_copy(
            ff_ref.at[:, :, 5, pl.ds(16, 16), pl.ds(512 * part, 512)],
            w_down_ref.at[:, :, pl.ds(16 * part, 16), pl.ds(1536, 512)],
            w_sems.at[4 + part],
        )
        for part in range(3)
    ]
    mine_hat, mine_grad = copies(0, 4)
    other_hat, other_grad = copies(4, 4)

    @pl.when(step == 0)
    def _():
        for copy in gu_copies + other_hat + down_copies + other_grad + mine_hat + mine_grad:
            copy.start()
        for copy in gu_copies + other_hat:
            copy.wait()

    @pl.when(step == 1)
    def _():
        for copy in mine_hat + mine_grad:
            copy.wait()

    rows = pl.ds(pl.multiple_of((1 - step) * 512, 512), 512)
    w_gu = w_gu_ref[...].reshape(2048, 2 * FP)
    gate_up_val = dot_nn(hat[rows, :], w_gu)
    gate = gate_up_val[:, :FP]
    up = gate_up_val[:, FP:]
    sig = jax.nn.sigmoid(gate)
    silu = gate * sig
    hid_ref[...] = (silu * up).astype(BF)

    @pl.when(step == 0)
    def _():
        for copy in down_copies + other_grad:
            copy.wait()

    w_down = w_down_ref[...].reshape(FP, 2048)
    grad_hid = dot_nt(grad[rows, :], w_down)
    grad_gu_ref[:, :FP] = (grad_hid * up * sig * (1.0 + gate * (1.0 - sig))).astype(BF)
    grad_gu_ref[:, FP:] = (grad_hid * silu).astype(BF)
    for back_ref, ahead_ref, now in ((back_other, ahead_other, 0), (back_mine, ahead_mine, 1)):

        @pl.when(step == now)
        def _():
            for k in range(2):
                cols = slice(1024 * k, 1024 * k + 1024)
                w_cols = w_gu_ref[4 * k : 4 * k + 4].reshape(1024, 2 * FP)
                back_ref[:, cols] = dot_nt(grad_gu_ref[...], w_cols).astype(BF)
                w_cols = w_down_ref[:, :, :, cols].reshape(FP, 1024)
                ahead_ref[:, cols] = dot_nn(hid_ref[...], w_cols).astype(BF)


def feed_forward(hat_pieces, grad_pieces, ff_all):
    block = lambda cols: pl.BlockSpec((512, cols), lambda i: (1 - i, 0))
    held = pl.BlockSpec((512, 2048), lambda i: (0, 0))
    shape = lambda rows, cols: jax.ShapeDtypeStruct((rows, cols), BF)
    half = shape(ROWS // 2, 2048)
    return pl.pallas_call(
        feed_forward_kernel,
        grid=(2,),
        in_specs=[ANYWHERE] * 17,
        out_specs=[block(FP), block(2 * FP)] + [held] * 4,
        out_shape=[shape(ROWS, FP), shape(ROWS, 2 * FP)] + [half] * 4,
        scratch_shapes=[
            pltpu.VMEM((8, 4, 2, 32, 2 * FP), BF),
            pltpu.VMEM((8, 2, 48, 2048), BF),
            pltpu.VMEM((ROWS, 2048), BF),
            pltpu.VMEM((ROWS, 2048), BF),
            pltpu.SemaphoreType.DMA((7,)),
            pltpu.SemaphoreType.DMA((8,)),
            pltpu.SemaphoreType.DMA((8,)),
        ],
        compiler_params=params(60),
        cost_estimate=takes(28),
        name="feed_forward",
    )(*hat_pieces, *grad_pieces, ff_all.reshape(8, 2, 6, 32, 1536))


def weight_grads_kernel(*refs):
    hat_pieces, grad_pieces = refs[:8], refs[8:16]
    grad_gu_ref, hid_ref = refs[16:18]
    out_ref, hid_t, grad, hat = refs[-4:]

    @pl.when(pl.program_id(0) == 0)
    def _():
        hid_t[...] = hid_ref[...].T
        for k in range(8):
            grad[128 * k : 128 * k + 128, :] = grad_pieces[k][...]

    for k in range(8):
        hat[128 * k : 128 * k + 128, :] = hat_pieces[k][...]
    for half in range(2):
        total = dot_tn(hat[:, 256 * half : 256 * half + 256], grad_gu_ref[...])
        total = total.astype(BF).reshape(4, 2, 32, 2 * FP)
        for zl in range(2):
            out_ref[2 * half + zl, :128, :] = total[:, zl].reshape(128, 2 * FP)
    rows = pl.ds(pl.multiple_of(pl.program_id(0) * 192, 64), 192)
    total = dot_nn(hid_t[rows, :], grad[...]).astype(BF).reshape(4, 48, 2048)
    out_ref[:, 128:176, :] = total[:, :, :1536]
    for part in range(3):
        out_ref[:, 176:192, 512 * part : 512 * part + 512] = total[:, 16 * part : 16 * part + 16, 1536:]


def weight_grads(hat_pieces, grad_pieces, grad_gu, hid, *earlier):
    return pl.pallas_call(
        weight_grads_kernel,
        grid=(4,),
        in_specs=[pl.BlockSpec((128, 512), lambda j: (0, j))] * 8
        + [fixed((128, 2048))] * 8
        + [fixed((ROWS, 2 * FP)), fixed((ROWS, FP))]
        + [ANYWHERE] * len(earlier),
        out_specs=pl.BlockSpec((4, 192, 1536), lambda j: (j, 0, 0)),
        out_shape=jax.ShapeDtypeStruct((16, 192, 1536), BF),
        scratch_shapes=[
            pltpu.VMEM((FP, ROWS), BF),
            pltpu.VMEM((ROWS, 2048), BF),
            pltpu.VMEM((ROWS, 512), BF),
        ],
        compiler_params=params(56),
        cost_estimate=takes(16.5),
        name="weight_grads",
    )(*hat_pieces, *grad_pieces, grad_gu, hid, *earlier)


def ff_columns():
    for f in range(8):
        for x in range(4):
            for zl in range(2):
                for c in range(2):
                    for g in range(2):
                        yield (
                            x * 2 + c,
                            g * FP + (f * 2 + zl) * 48,
                            g * FF + flat_index(f, x, zl, c) * 44,
                        )


def pack_kernel(qkv_ref, gate_up_ref, gains_ref, out_ref, scaled_qkv, scaled, packed):
    gains = gains_ref[...]
    scaled_qkv[...] = qkv_ref[...].astype(BF).astype(F32) * gains[:, 0:1]
    scaled[...] = gate_up_ref[...].astype(BF).astype(F32) * gains[:, 1:2]
    packed[...] = jnp.zeros_like(packed)
    for rank in range(8):
        head = 2048 + rank // 2 * HD
        packed[rank, :, :256] = scaled_qkv[:, rank * 256 : rank * 256 + 256]
        packed[rank, :, 256:320] = scaled_qkv[:, head : head + HD]
        packed[rank, :, 320:384] = scaled_qkv[:, head + 256 : head + 256 + HD]
    for rank, there, here in ff_columns():
        packed[rank, :, 384 + there : 384 + there + 44] = scaled[:, here : here + 44]
    out_ref[...] = packed[...].astype(BF)


def pack(qkv, gate_up, gains):
    return pl.pallas_call(
        pack_kernel,
        in_specs=[WHOLE] * 3,
        out_specs=WHOLE,
        out_shape=jax.ShapeDtypeStruct((8, 16, 1920), BF),
        scratch_shapes=[
            pltpu.VMEM((16, 2560), F32),
            pltpu.VMEM((16, 2 * FF), F32),
            pltpu.VMEM((8, 16, 1920), F32),
        ],
        compiler_params=params(24),
        cost_estimate=takes(3),
        name="pack",
    )(qkv, gate_up, gains)


def update_kernel(
    got_ref, master_ref, gain_ref, first_ref, second_ref, new_first, new_second, new_master, gain_sum, packed, sums
):
    packed[...] = got_ref[...].astype(F32)
    for rank, there, here in ff_columns():
        sums[:, here : here + 44] = packed[rank, :, 384 + there : 384 + there + 44]
    master = master_ref[...]
    gain_sum[...] = jnp.sum(
        master.astype(BF).astype(F32) * sums[...], axis=1, keepdims=True
    )
    new_first[...], new_second[...], new_master[...] = adam_update(
        master,
        sums[...] * gain_ref[...],
        first_ref[...],
        second_ref[...],
        step_rates[2],
        decay_rates[2],
    )


def update_gate_up(got, master, gain, first, second):
    shape = jax.ShapeDtypeStruct((16, 2 * FF), F32)
    return pl.pallas_call(
        update_kernel,
        in_specs=[WHOLE] * 5,
        out_specs=[WHOLE] * 4,
        out_shape=[shape, shape, shape, jax.ShapeDtypeStruct((16, 1), F32)],
        scratch_shapes=[pltpu.VMEM((8, 16, 1920), F32), pltpu.VMEM((16, 2 * FF), F32)],
        compiler_params=params(32),
        cost_estimate=takes(4),
        name="update_gate_up",
    )(got, master, gain, first, second)


def shift(block, distance):
    return lax.ppermute(block, "x", [(i, (i + distance) % 4) for i in range(4)])


def swap(block):
    return lax.ppermute(block, "c", [(0, 1), (1, 0)])


ORDER = ((0, 0), (1, 0), (3, 0), (2, 0), (0, 1), (1, 1), (3, 1), (2, 1))


def tie_kernel(*refs):
    pass


def tie(value, *earlier):
    anywhere = pl.BlockSpec(memory_space=pl.ANY)
    return pl.pallas_call(
        tie_kernel,
        in_specs=[anywhere] * (1 + len(earlier)),
        out_specs=anywhere,
        out_shape=jax.ShapeDtypeStruct(value.shape, value.dtype),
        input_output_aliases={0: 0},
        cost_estimate=pl.CostEstimate(flops=0, bytes_accessed=0, transcendentals=0),
        name="tie",
    )(value, *earlier)


def gather_pieces(block, *earlier):
    mine = [block, shift(block, 1), shift(block, -1), shift(block, 2)]
    if earlier:
        mine[1] = tie(mine[1], *earlier)
    return mine + [swap(piece) for piece in mine]


def scatter_first(mine, other):
    return mine.astype(F32) + swap(other).astype(F32)


def scatter_second(mine):
    far = mine[384:].astype(BF)
    by_left = shift(far[:64], -1)
    by_right = shift(far[64:], 1)
    to_left = jnp.concatenate([mine[128:192] + by_left.astype(F32), mine[192:256]], axis=0)
    to_right = jnp.concatenate([mine[256:320], mine[320:384] + by_right.astype(F32)], axis=0)
    return to_left.astype(BF), to_right.astype(BF), mine[:128]


def scatter_third(to_left, to_right):
    return shift(to_left, -1), shift(to_right, 1)


def total(parts):
    first, second, third = parts
    return first.astype(F32) + second.astype(F32) + third.astype(F32)


def attn_grads_kernel(*refs):
    pieces = refs[:8]
    mixed_ref, out_grad_ref, sum_ref, hat, sems = refs[8:]
    copies = fetch(pieces, hat, sems)
    for r in range(16):
        for k in range(8):
            sum_ref[r, 16 * k : 16 * k + 16, 384:] = out_grad_ref[
                16 * r : 16 * r + 16, 256 * k : 256 * k + 256
            ]
    for copy in copies:
        copy.wait()
    for f in range(8):
        total = dot_tn(hat[:, 256 * f : 256 * f + 256], mixed_ref[...])
        total = total.astype(BF).reshape(4, 2, 32, 384)
        for zl in range(2):
            sum_ref[2 * f + zl, :, :384] = total[:, zl].reshape(128, 384)


def attn_grads(pieces, grad_mixed, sum_out):
    return pl.pallas_call(
        attn_grads_kernel,
        in_specs=[ANYWHERE] * 8 + [WHOLE] * 2,
        out_specs=WHOLE,
        out_shape=jax.ShapeDtypeStruct((16, 128, 640), BF),
        scratch_shapes=[pltpu.VMEM((ROWS, 2048), BF), pltpu.SemaphoreType.DMA((8,))],
        compiler_params=params(60),
        cost_estimate=takes(4),
        name="attn_grads",
    )(*pieces, grad_mixed, sum_out)


def row_positions(span_order, zl):
    x = lax.axis_index("x")
    c = lax.axis_index("c")
    holders = jnp.stack([((x - dx) % 4 * 2 + zl) * 2 + (c + dc) % 2 for dx, dc in ORDER])
    picked = (holders[:, None] == jnp.arange(16, dtype=jnp.int32)[None, :]).astype(jnp.int32)
    spans = jnp.sum(picked[:, :, None] * span_order.reshape(1, 16, 2), axis=1)
    spans = spans.T.reshape(16, 1)
    return (spans * 64 + jnp.arange(64, dtype=jnp.int32)[None, :]).reshape(ROWS)


def norm_scale(rows):
    return lax.rsqrt(jnp.mean(rows * rows, axis=-1, keepdims=True) + norm_eps)


def norm_back(grad_hat, hat, scale, rest):
    return rest + scale * (grad_hat - hat * jnp.mean(grad_hat * hat, axis=-1, keepdims=True))


def body(
    tokens,
    out_grad,
    seq_lengths,
    span_order,
    attn_in,
    attn_out,
    gate_up,
    down_proj,
    norm_gains,
    first_attn_in,
    second_attn_in,
    first_attn_out,
    second_attn_out,
    first_gate_up,
    second_gate_up,
    first_down_proj,
    second_down_proj,
    first_norm_gains,
    second_norm_gains,
):
    zl = lax.axis_index("zl")
    gains = norm_gains.astype(BF).astype(F32)
    gain_one = gains[0][:, None]
    gain_two = gains[1][:, None]
    low_qkv = attn_in.astype(BF).astype(F32)

    inputs = tokens.astype(F32)
    scale_one = norm_scale(inputs)
    hat_one = inputs * scale_one
    packed = pack(attn_in, gate_up, gains.T)
    ranked = lax.all_to_all(packed, TP, 0, 0, tiled=True).reshape(128, 1920)
    hat_pieces = gather_pieces(tie(hat_one.astype(BF), ranked))
    out_part = lax.ppermute(attn_out.astype(BF), ALL, SPREAD)
    out_part = out_part.reshape(16, 8, 256).transpose(1, 0, 2).reshape(128, 256)
    attn_part = jnp.concatenate([ranked[:, :384], out_part], axis=1)
    attn_all = lax.all_gather(attn_part, REP, axis=0, tiled=True)
    down_rows = jnp.pad(down_proj.astype(BF), ((0, 4), (0, 0)))
    down_tail = [down_rows[16 * part : 16 * part + 16, 1536:] for part in range(3)]
    ff_part = jnp.concatenate(
        [ranked[:, 384:], down_rows[:, :1536], jnp.concatenate(down_tail, axis=1)], axis=0
    )
    grad_pieces = gather_pieces(tie(out_grad, *hat_pieces[1:4]))
    ff_all = lax.all_gather(
        tie(ff_part, attn_all, *hat_pieces[1:]), REP, axis=0, tiled=True
    )

    own_pos = row_positions(span_order, zl)
    other_pos = row_positions(span_order, 1 - zl)
    lengths = seq_lengths[0]
    bound_one = lengths[0]
    bound_two = lengths[0] + lengths[1]
    low_pos = jnp.where(own_pos < bound_one, 0, bound_one)[None, :]
    high_pos = jnp.where(own_pos < bound_two, own_pos, -1)[None, :]
    key_pos = jnp.concatenate([own_pos, other_pos])
    key_pos = jnp.broadcast_to(key_pos[:, None], (KEYS, QB))

    queries, own_kv, w_qkv, w_out = project(hat_pieces, attn_all)
    other_kv = lax.ppermute(own_kv, "zl", [(0, 1), (1, 0)])
    before = attend(queries, own_kv, key_pos[:ROWS], low_pos, high_pos, None)
    att, att_early, lse = attend(
        queries, other_kv, key_pos[ROWS:], low_pos, high_pos, before, *grad_pieces[1:4]
    )
    att_other = dot_nn(att[512:], w_out).astype(BF)
    att_mine = dot_nn(att[:512], w_out)
    to_left, to_right, stays = scatter_second(scatter_first(att_mine, att_other))
    hidden = inputs + total((stays, *scatter_third(to_left, to_right)))

    scale_two = norm_scale(hidden)
    hat_two = hidden * scale_two
    hat_two_pieces = gather_pieces(hat_two.astype(BF))
    hid, grad_gu, back_mine, back_other, ahead_mine, ahead_other = feed_forward(
        hat_two_pieces, grad_pieces, ff_all
    )
    to_left, to_right, stays = scatter_second(scatter_first(back_mine, back_other))
    grad_hat_two = total((stays, *scatter_third(to_left, to_right)))
    grad_hidden = norm_back(grad_hat_two, hat_two, scale_two, out_grad.astype(F32))
    sums = weight_grads(hat_two_pieces, grad_pieces, grad_gu, hid, to_left, to_right)
    sums = sums.reshape(16 * 192, 1536)
    grad_hidden_low = tie(grad_hidden.astype(BF), sums)
    ahead = scatter_first(ahead_mine, tie(ahead_other, grad_hidden_low))
    hidden_pieces = gather_pieces(grad_hidden_low, ahead)
    sums = lax.psum_scatter(tie(sums, grad_hidden_low), REP, scatter_dimension=0, tiled=True)
    grad_att, sum_out = hidden_products(hidden_pieces, att, w_out, ahead)

    grad_q, grad_kv = attend_back(
        queries, grad_att, att_early, other_kv, key_pos[ROWS:], low_pos, high_pos, lse, None, ahead
    )
    arrived = lax.ppermute(grad_kv.astype(BF), "zl", [(0, 1), (1, 0)])
    ahead_left, ahead_right, ahead_stays = scatter_second(ahead)
    grad_q, grad_kv = attend_back(
        queries,
        grad_att,
        att_early,
        own_kv,
        key_pos[:ROWS],
        low_pos,
        high_pos,
        lse,
        grad_q,
        ahead_left,
        ahead_right,
    )
    ahead = scatter_third(ahead_left, ahead_right)
    block_out = (hidden + total((ahead_stays, *ahead))).astype(BF)
    grad_kv = (grad_kv + arrived.astype(F32)).astype(BF)
    grad_kv = grad_kv.reshape(2, 8, 64, 2 * HD).transpose(1, 0, 2, 3).reshape(ROWS, 2 * HD)
    grad_mixed = jnp.concatenate([grad_q, grad_kv], axis=1)
    grad_mixed = tie(grad_mixed, *ahead)
    attn_parts = attn_grads(hat_pieces, grad_mixed, sum_out)
    attn_sums = lax.all_to_all(attn_parts, REP, 0, 0, tiled=True)
    attn_sums = jnp.sum(attn_sums.astype(F32), axis=0).astype(BF)
    last_rows = tie(grad_mixed, attn_parts)
    last_other = dot_nt(last_rows[512:], w_qkv).astype(BF)
    last_mine = dot_nt(last_rows[:512], w_qkv)
    to_left, to_right, stays = scatter_second(scatter_first(last_mine, last_other))
    last_thirds = scatter_third(to_left, to_right)
    got = jnp.concatenate([attn_sums[:, :384], sums[:128]], axis=1).reshape(8, 16, 1920)
    grad_hat_one = total((tie(stays, got), *last_thirds))
    in_grad = norm_back(grad_hat_one, hat_one, scale_one, grad_hidden).astype(BF)
    sum_out = tie(attn_sums[:, 384:], got)
    got = lax.all_to_all(got, TP, 0, 0, tiled=True)
    got_qkv = got[:, :, :384].transpose(1, 0, 2).astype(F32)
    got_kv = got_qkv[:, :, 256:].reshape(16, 4, 2, 2, HD).sum(axis=2)
    got_qkv = jnp.concatenate(
        [
            got_qkv[:, :, :256].reshape(16, 2048),
            got_kv[:, :, 0].reshape(16, 256),
            got_kv[:, :, 1].reshape(16, 256),
        ],
        axis=1,
    )
    sum_out = sum_out.reshape(8, 16, 256).transpose(1, 0, 2).reshape(16, 2048)
    got_out = lax.ppermute(sum_out, ALL, back(SPREAD)).astype(F32)
    tail = [sums[176:192, 512 * part : 512 * part + 512] for part in range(3)]
    got_down = jnp.concatenate([sums[128:176], jnp.concatenate(tail, axis=0)], axis=1)
    got_down = got_down[:44].astype(F32)
    gu_new = update_gate_up(got, gate_up, gain_two, first_gate_up, second_gate_up)
    gain_sums = jnp.stack([jnp.sum(low_qkv * got_qkv, axis=1), gu_new[3][:, 0]], axis=0)
    qkv_new = adam_update(
        attn_in, got_qkv * gain_one, first_attn_in, second_attn_in, step_rates[0], decay_rates[0]
    )
    out_new = adam_update(
        attn_out, got_out, first_attn_out, second_attn_out, step_rates[1], decay_rates[1]
    )
    down_new = adam_update(
        down_proj, got_down, first_down_proj, second_down_proj, step_rates[3], decay_rates[3]
    )
    gains_new = adam_update(
        norm_gains, gain_sums, first_norm_gains, second_norm_gains, step_rates[4], decay_rates[4]
    )
    return (block_out, in_grad, *qkv_new, *out_new, *gu_new[:3], *down_new, *gains_new)


def solution(mesh):
    split = Mesh(mesh.devices.reshape(4, 2, 4, 2, 2), ALL)
    rows = P(ALL, None)
    cols = P(None, ALL)
    group = P(("y", "zh"), None)
    in_specs = (rows, rows, group, P()) + (rows,) * 4 + (cols,) + (rows,) * 8 + (cols,) * 2
    out_specs = (rows,) * 14 + (cols,) * 3
    return jax.shard_map(body, mesh=split, in_specs=in_specs, out_specs=out_specs, check_vma=False)
```

```python
import functools

import jax
import jax.numpy as jnp
from jax import lax
from jax.experimental import pallas as pl
from jax.experimental.pallas import tpu as pltpu
from jax.sharding import Mesh
from jax.sharding import PartitionSpec as P

BF = jnp.bfloat16
F32 = jnp.float32
ALL = ("y", "zh", "x", "zl", "c")
TP = ("x", "c")
REP = ("y", "zh", "zl")

FF = 5632
FP = 768
HD = 64
STEP = 10
ROWS = 1024
KEYS = 2048

norm_eps = 1e-05
beta_one = 0.9
beta_two = 0.95
adam_eps = 1e-08
big_negative = -1e30
step_rates = (0.15, 0.3, 0.06, 0.04, 2.0)
decay_rates = (0.1, 0.1, 0.1, 0.1, 0.0)


def flat_index(f, x, zl, c):
    return ((f * 4 + x) * 2 + zl) * 2 + c


SPREAD = [
    (t * 16 + k, flat_index(k // 2, t // 2, k % 2, t % 2)) for t in range(8) for k in range(16)
]


def back(route):
    return [(b, a) for a, b in route]


def adam_update(master, grad_sum, first_old, second_old, step_rate, decay_rate):
    first_new = beta_one * first_old + (1.0 - beta_one) * grad_sum
    second_new = beta_two * second_old + (1.0 - beta_two) * grad_sum * grad_sum
    first_fix = first_new / (1.0 - beta_one**STEP)
    second_fix = second_new / (1.0 - beta_two**STEP)
    master_new = master - step_rate * (
        first_fix / (jnp.sqrt(second_fix) + adam_eps) + decay_rate * master
    )
    return (first_new, second_new, master_new)


def dot_nn(a, b):
    return lax.dot_general(a, b, (((1,), (0,)), ((), ())), preferred_element_type=F32)


def dot_nt(a, b):
    return lax.dot_general(a, b, (((1,), (1,)), ((), ())), preferred_element_type=F32)


def dot_tn(a, b):
    return lax.dot_general(a, b, (((0,), (0,)), ((), ())), preferred_element_type=F32)


QB = 512


def takes(microseconds):
    return pl.CostEstimate(
        flops=int(microseconds * 1.15e9), bytes_accessed=1 << 20, transcendentals=0
    )


WHOLE = pl.BlockSpec(memory_space=pltpu.VMEM)
ANYWHERE = pl.BlockSpec(memory_space=pl.ANY)


def fixed(shape):
    return pl.BlockSpec(shape, lambda i: (0,) * len(shape), pipeline_mode=pl.Buffered(1))


def params(mib):
    return pltpu.CompilerParams(vmem_limit_bytes=mib * 1024 * 1024)


def natural_rows(block, piece):
    first = block * 64 + 128 * piece
    return pl.ds(pl.multiple_of(first, 64), 64)


def attend_kernel(first, q_ref, kv_ref, kp_ref, lo_ref, hi_ref, *rest):
    turned = rest[-1]

    @pl.when(pl.program_id(0) == 0)
    def _():
        turned[...] = kv_ref[...].T

    def over(count):
        key_pos = kp_ref[:count, :]
        high = hi_ref[...]
        allowed = (key_pos >= lo_ref[...]) & (key_pos <= high)
        keys = kv_ref[:count, :HD]
        for h in range(4):
            cols = slice(h * HD, (h + 1) * HD)
            row = slice(h, h + 1)
            s = jnp.where(allowed, dot_nt(keys, q_ref[:, cols]), big_negative)
            peak = jnp.max(s, axis=0, keepdims=True)
            if not first:
                out_before, peak_before, total_before = rest[:3]
                peak = jnp.maximum(peak, peak_before[row, :])
            p = jnp.exp(s - peak)
            total = jnp.sum(p, axis=0, keepdims=True)
            out = dot_nn(turned[HD:, :count], p.astype(BF))
            if first:
                out_ref, peak_ref, total_ref = rest[-4:-1]
                out_ref[cols, :] = out
                peak_ref[row, :] = peak
                total_ref[row, :] = total
            else:
                natural_ref, o_ref, lse_ref = rest[-4:-1]
                fade = jnp.exp(peak_before[row, :] - peak)
                total = total + fade * total_before[row, :]
                out = out + fade * out_before[cols, :]
                out = out * jnp.where(high >= 0, 1.0 / total, 0.0)
                out = out.T.astype(BF)
                o_ref[:, cols] = out
                for piece in range(8):
                    natural_ref[natural_rows(pl.program_id(0), piece), cols] = out[
                        64 * piece : 64 * piece + 64
                    ]
                lse_ref[row, :] = peak + jnp.log(total)

    pl.when(pl.program_id(0) < 1)(lambda: over(ROWS // 2))
    pl.when(pl.program_id(0) >= 1)(lambda: over(ROWS))


def attend(q, kv, kp, lo, hi, before, *earlier):
    first = before is None
    row = pl.BlockSpec((1, QB), lambda i: (0, i))
    rows = pl.BlockSpec((4, QB), lambda i: (0, i))
    flat = pl.BlockSpec((256, QB), lambda i: (0, i))
    block = pl.BlockSpec((QB, 256), lambda i: (i, 0))
    held = pl.BlockSpec((ROWS, 256), lambda i: (0, 0))
    stat = jax.ShapeDtypeStruct((4, ROWS), F32)
    result = jax.ShapeDtypeStruct((ROWS, 256), BF)
    carried = [] if first else list(before)
    return pl.pallas_call(
        functools.partial(attend_kernel, first),
        grid=(ROWS // QB,),
        in_specs=[block, fixed((ROWS, 2 * HD)), fixed((ROWS, QB)), row, row]
        + [flat, rows, rows][: len(carried)]
        + [ANYWHERE] * len(earlier),
        out_specs=[flat, rows, rows] if first else [held, block, rows],
        out_shape=[jax.ShapeDtypeStruct((256, ROWS), F32), stat, stat]
        if first
        else [result, result, stat],
        scratch_shapes=[pltpu.VMEM((2 * HD, ROWS), BF)],
        compiler_params=params(40),
        cost_estimate=takes(10),
        name="attend",
    )(q, kv, kp, lo, hi, *carried, *earlier)


def attend_back_kernel(first, q_ref, do_ref, o_ref, kv_ref, kp_ref, lo_ref, hi_ref, lse_ref, *rest):
    dq_ref, dkv_ref, turned, values = rest[-4:]

    @pl.when(pl.program_id(0) == 0)
    def _():
        dkv_ref[...] = jnp.zeros_like(dkv_ref)
        turned[...] = kv_ref[...].T
        values[...] = kv_ref[:, HD:]

    def over(count):
        key_pos = kp_ref[:count, :]
        allowed = (key_pos >= lo_ref[...]) & (key_pos <= hi_ref[...])
        keys = kv_ref[:count, :HD]
        delta_all = (do_ref[...].astype(F32) * o_ref[...].astype(F32)).T
        for h in range(4):
            cols = slice(h * HD, (h + 1) * HD)
            qh = q_ref[:, cols]
            doh = do_ref[:, cols]
            delta = jnp.sum(delta_all[cols], axis=0, keepdims=True)
            s = dot_nt(keys, qh)
            p = jnp.where(allowed, jnp.exp(s - lse_ref[h : h + 1, :]), 0.0)
            ds = (p * (dot_nt(values[:count, :], doh) - delta)).astype(BF)
            dkv_ref[:count, :HD] += dot_nn(ds, qh)
            dkv_ref[:count, HD:] += dot_nn(p.astype(BF), doh)
            dq = dot_nn(turned[:HD, :count], ds) * HD**-0.5
            if first:
                dq_ref[cols, :] = dq
            else:
                dq = (dq + rest[0][cols, :]).T.astype(BF)
                for piece in range(8):
                    dq_ref[natural_rows(pl.program_id(0), piece), cols] = dq[
                        64 * piece : 64 * piece + 64
                    ]

    pl.when(pl.program_id(0) < 1)(lambda: over(ROWS // 2))
    pl.when(pl.program_id(0) >= 1)(lambda: over(ROWS))


def attend_back(q, do, o, kv, kp, lo, hi, lse, earlier_dq, *earlier):
    first = earlier_dq is None
    row = pl.BlockSpec((1, QB), lambda i: (0, i))
    block = pl.BlockSpec((QB, 256), lambda i: (i, 0))
    flat = pl.BlockSpec((256, QB), lambda i: (0, i))
    held = lambda cols: pl.BlockSpec((ROWS, cols), lambda i: (0, 0))
    carried = [] if first else [earlier_dq]
    return pl.pallas_call(
        functools.partial(attend_back_kernel, first),
        grid=(ROWS // QB,),
        in_specs=[block, block, block, fixed((ROWS, 2 * HD)), fixed((ROWS, QB)), row, row]
        + [pl.BlockSpec((4, QB), lambda i: (0, i))]
        + [flat] * len(carried)
        + [ANYWHERE] * len(earlier),
        out_specs=[flat if first else held(256), held(2 * HD)],
        out_shape=[
            jax.ShapeDtypeStruct((256, ROWS), F32)
            if first
            else jax.ShapeDtypeStruct((ROWS, 256), BF),
            jax.ShapeDtypeStruct((ROWS, 2 * HD), F32),
        ],
        scratch_shapes=[pltpu.VMEM((2 * HD, ROWS), BF), pltpu.VMEM((ROWS, HD), BF)],
        compiler_params=params(40),
        cost_estimate=takes(10),
        name="attend_back",
    )(q, do, o, kv, kp, lo, hi, lse, *carried, *earlier)


def fetch(pieces, rows, sems):
    copies = [
        pltpu.make_async_copy(piece, rows.at[pl.ds(128 * k, 128), :], sems.at[k])
        for k, piece in enumerate(pieces)
    ]
    for copy in copies:
        copy.start()
    return copies


def project_kernel(*refs):
    pieces, raw_hbm = refs[:8], refs[8]
    q_ref, kv_ref, w_ref, w_out_ref, hat, raw_ref, sems, raw_sem = refs[9:]
    raw_copy = pltpu.make_async_copy(raw_hbm, raw_ref, raw_sem)
    raw_copy.start()
    copies = fetch(pieces, hat, sems)
    raw_copy.wait()
    for f in range(8):
        for zl in range(2):
            r = 2 * f + zl
            for x in range(4):
                row = 256 * f + 64 * x + 32 * zl
                w_ref[row : row + 32, :] = raw_ref[128 * r + 32 * x : 128 * r + 32 * x + 32, :384]
            for k in range(8):
                w_out_ref[16 * r : 16 * r + 16, 256 * k : 256 * k + 256] = raw_ref[
                    128 * r + 16 * k : 128 * r + 16 * k + 16, 384:
                ]
    for copy in copies:
        copy.wait()
    for k in range(2):
        rows = slice(512 * k, 512 * k + 512)
        product = dot_nn(hat[rows, :], w_ref[...]).astype(BF)
        for piece in range(4):
            for late in range(2):
                here = slice(128 * piece + 64 * late, 128 * piece + 64 * late + 64)
                there = 512 * late + 256 * k + 64 * piece
                q_ref[there : there + 64, :] = product[here, :256] * BF(HD**-0.5)
                kv_ref[there : there + 64, :] = product[here, 256:]


def project(pieces, raw):
    shape = lambda *dims: jax.ShapeDtypeStruct(dims, BF)
    return pl.pallas_call(
        project_kernel,
        in_specs=[ANYWHERE] * 9,
        out_specs=[WHOLE] * 4,
        out_shape=[shape(ROWS, 256), shape(ROWS, 128), shape(2048, 384), shape(256, 2048)],
        scratch_shapes=[
            pltpu.VMEM((ROWS, 2048), BF),
            pltpu.VMEM((2048, 640), BF),
            pltpu.SemaphoreType.DMA((8,)),
            pltpu.SemaphoreType.DMA,
        ],
        compiler_params=params(60),
        cost_estimate=takes(5),
        name="project",
    )(*pieces, raw)


def hidden_products_kernel(*refs):
    pieces = refs[:8]
    att_ref, w_ref = refs[8:10]
    grad_att_ref, sum_ref, grad, sems = refs[-4:]
    for copy in fetch(pieces, grad, sems):
        copy.wait()
    grad_att = dot_nt(grad[...], w_ref[...]).astype(BF)
    for piece in range(8):
        for late in range(2):
            here = 128 * piece + 64 * late
            there = 512 * late + 64 * piece
            grad_att_ref[there : there + 64, :] = grad_att[here : here + 64]
    turned = att_ref[...].T
    for k in range(4):
        cols = slice(512 * k, 512 * k + 512)
        sum_ref[:, cols] = dot_nn(turned, grad[:, cols]).astype(BF)


def hidden_products(pieces, att, w_out, *earlier):
    return pl.pallas_call(
        hidden_products_kernel,
        in_specs=[ANYWHERE] * 8 + [WHOLE] * 2 + [ANYWHERE] * len(earlier),
        out_specs=[WHOLE] * 2,
        out_shape=[jax.ShapeDtypeStruct((ROWS, 256), BF), jax.ShapeDtypeStruct((256, 2048), BF)],
        scratch_shapes=[pltpu.VMEM((ROWS, 2048), BF), pltpu.SemaphoreType.DMA((8,))],
        compiler_params=params(40),
        cost_estimate=takes(6),
        name="hidden_products",
    )(*pieces, att, w_out, *earlier)


def feed_forward_kernel(*refs):
    hat_pieces, grad_pieces, ff_ref = refs[:8], refs[8:16], refs[16]
    hid_ref, grad_gu_ref, back_mine, back_other, ahead_mine, ahead_other = refs[17:23]
    w_gu_ref, w_down_ref, hat, grad, w_sems, hat_sems, grad_sems = refs[23:]
    step = pl.program_id(0)

    def copies(first, count):
        return (
            [
                pltpu.make_async_copy(
                    hat_pieces[k], hat.at[pl.ds(128 * k, 128), :], hat_sems.at[k]
                )
                for k in range(first, first + count)
            ],
            [
                pltpu.make_async_copy(
                    grad_pieces[k], grad.at[pl.ds(128 * k, 128), :], grad_sems.at[k]
                )
                for k in range(first, first + count)
            ],
        )

    gu_copies = [
        pltpu.make_async_copy(
            ff_ref.at[:, zl, pl.ds(0, 4)], w_gu_ref.at[:, :, zl], w_sems.at[zl]
        )
        for zl in range(2)
    ]
    down_copies = [
        pltpu.make_async_copy(
            ff_ref.at[:, :, 4], w_down_ref.at[:, :, pl.ds(0, 32), pl.ds(0, 1536)], w_sems.at[2]
        ),
        pltpu.make_async_copy(
            ff_ref.at[:, :, 5, pl.ds(0, 16)],
            w_down_ref.at[:, :, pl.ds(32, 16), pl.ds(0, 1536)],
            w_sems.at[3],
        ),
    ] + [
        pltpu.make_async_copy(
            ff_ref.at[:, :, 5, pl.ds(16, 16), pl.ds(512 * part, 512)],
            w_down_ref.at[:, :, pl.ds(16 * part, 16), pl.ds(1536, 512)],
            w_sems.at[4 + part],
        )
        for part in range(3)
    ]
    mine_hat, mine_grad = copies(0, 4)
    other_hat, other_grad = copies(4, 4)

    @pl.when(step == 0)
    def _():
        for copy in gu_copies + other_hat + down_copies + other_grad + mine_hat + mine_grad:
            copy.start()
        for copy in gu_copies + other_hat:
            copy.wait()

    @pl.when(step == 1)
    def _():
        for copy in mine_hat + mine_grad:
            copy.wait()

    rows = pl.ds(pl.multiple_of((1 - step) * 512, 512), 512)
    w_gu = w_gu_ref[...].reshape(2048, 2 * FP)
    gate_up_val = dot_nn(hat[rows, :], w_gu)
    gate = gate_up_val[:, :FP]
    up = gate_up_val[:, FP:]
    sig = jax.nn.sigmoid(gate)
    silu = gate * sig
    hid_ref[...] = (silu * up).astype(BF)

    @pl.when(step == 0)
    def _():
        for copy in down_copies + other_grad:
            copy.wait()

    w_down = w_down_ref[...].reshape(FP, 2048)
    grad_hid = dot_nt(grad[rows, :], w_down)
    grad_gu_ref[:, :FP] = (grad_hid * up * sig * (1.0 + gate * (1.0 - sig))).astype(BF)
    grad_gu_ref[:, FP:] = (grad_hid * silu).astype(BF)
    for back_ref, ahead_ref, now in ((back_other, ahead_other, 0), (back_mine, ahead_mine, 1)):

        @pl.when(step == now)
        def _():
            for k in range(2):
                cols = slice(1024 * k, 1024 * k + 1024)
                w_cols = w_gu_ref[4 * k : 4 * k + 4].reshape(1024, 2 * FP)
                back_ref[:, cols] = dot_nt(grad_gu_ref[...], w_cols).astype(BF)
                w_cols = w_down_ref[:, :, :, cols].reshape(FP, 1024)
                ahead_ref[:, cols] = dot_nn(hid_ref[...], w_cols).astype(BF)


def feed_forward(hat_pieces, grad_pieces, ff_all):
    block = lambda cols: pl.BlockSpec((512, cols), lambda i: (1 - i, 0))
    held = pl.BlockSpec((512, 2048), lambda i: (0, 0))
    shape = lambda rows, cols: jax.ShapeDtypeStruct((rows, cols), BF)
    half = shape(ROWS // 2, 2048)
    return pl.pallas_call(
        feed_forward_kernel,
        grid=(2,),
        in_specs=[ANYWHERE] * 17,
        out_specs=[block(FP), block(2 * FP)] + [held] * 4,
        out_shape=[shape(ROWS, FP), shape(ROWS, 2 * FP)] + [half] * 4,
        scratch_shapes=[
            pltpu.VMEM((8, 4, 2, 32, 2 * FP), BF),
            pltpu.VMEM((8, 2, 48, 2048), BF),
            pltpu.VMEM((ROWS, 2048), BF),
            pltpu.VMEM((ROWS, 2048), BF),
            pltpu.SemaphoreType.DMA((7,)),
            pltpu.SemaphoreType.DMA((8,)),
            pltpu.SemaphoreType.DMA((8,)),
        ],
        compiler_params=params(60),
        cost_estimate=takes(28),
        name="feed_forward",
    )(*hat_pieces, *grad_pieces, ff_all.reshape(8, 2, 6, 32, 1536))


def weight_grads_kernel(*refs):
    hat_pieces, grad_pieces = refs[:8], refs[8:16]
    grad_gu_ref, hid_ref = refs[16:18]
    out_ref, hid_t, grad, hat = refs[-4:]

    @pl.when(pl.program_id(0) == 0)
    def _():
        hid_t[...] = hid_ref[...].T
        for k in range(8):
            grad[128 * k : 128 * k + 128, :] = grad_pieces[k][...]

    for k in range(8):
        hat[128 * k : 128 * k + 128, :] = hat_pieces[k][...]
    for half in range(2):
        total = dot_tn(hat[:, 256 * half : 256 * half + 256], grad_gu_ref[...])
        total = total.astype(BF).reshape(4, 2, 32, 2 * FP)
        for zl in range(2):
            out_ref[2 * half + zl, :128, :] = total[:, zl].reshape(128, 2 * FP)
    rows = pl.ds(pl.multiple_of(pl.program_id(0) * 192, 64), 192)
    total = dot_nn(hid_t[rows, :], grad[...]).astype(BF).reshape(4, 48, 2048)
    out_ref[:, 128:176, :] = total[:, :, :1536]
    for part in range(3):
        out_ref[:, 176:192, 512 * part : 512 * part + 512] = total[:, 16 * part : 16 * part + 16, 1536:]


def weight_grads(hat_pieces, grad_pieces, grad_gu, hid, *earlier):
    return pl.pallas_call(
        weight_grads_kernel,
        grid=(4,),
        in_specs=[pl.BlockSpec((128, 512), lambda j: (0, j))] * 8
        + [fixed((128, 2048))] * 8
        + [fixed((ROWS, 2 * FP)), fixed((ROWS, FP))]
        + [ANYWHERE] * len(earlier),
        out_specs=pl.BlockSpec((4, 192, 1536), lambda j: (j, 0, 0)),
        out_shape=jax.ShapeDtypeStruct((16, 192, 1536), BF),
        scratch_shapes=[
            pltpu.VMEM((FP, ROWS), BF),
            pltpu.VMEM((ROWS, 2048), BF),
            pltpu.VMEM((ROWS, 512), BF),
        ],
        compiler_params=params(56),
        cost_estimate=takes(16.5),
        name="weight_grads",
    )(*hat_pieces, *grad_pieces, grad_gu, hid, *earlier)


def ff_columns():
    for f in range(8):
        for x in range(4):
            for zl in range(2):
                for c in range(2):
                    for g in range(2):
                        yield (
                            x * 2 + c,
                            g * FP + (f * 2 + zl) * 48,
                            g * FF + flat_index(f, x, zl, c) * 44,
                        )


def pack_kernel(qkv_ref, gate_up_ref, gains_ref, out_ref, scaled_qkv, scaled, packed):
    gains = gains_ref[...]
    scaled_qkv[...] = qkv_ref[...].astype(BF).astype(F32) * gains[:, 0:1]
    scaled[...] = gate_up_ref[...].astype(BF).astype(F32) * gains[:, 1:2]
    packed[...] = jnp.zeros_like(packed)
    for rank in range(8):
        head = 2048 + rank // 2 * HD
        packed[rank, :, :256] = scaled_qkv[:, rank * 256 : rank * 256 + 256]
        packed[rank, :, 256:320] = scaled_qkv[:, head : head + HD]
        packed[rank, :, 320:384] = scaled_qkv[:, head + 256 : head + 256 + HD]
    for rank, there, here in ff_columns():
        packed[rank, :, 384 + there : 384 + there + 44] = scaled[:, here : here + 44]
    out_ref[...] = packed[...].astype(BF)


def pack(qkv, gate_up, gains):
    return pl.pallas_call(
        pack_kernel,
        in_specs=[WHOLE] * 3,
        out_specs=WHOLE,
        out_shape=jax.ShapeDtypeStruct((8, 16, 1920), BF),
        scratch_shapes=[
            pltpu.VMEM((16, 2560), F32),
            pltpu.VMEM((16, 2 * FF), F32),
            pltpu.VMEM((8, 16, 1920), F32),
        ],
        compiler_params=params(24),
        cost_estimate=takes(3),
        name="pack",
    )(qkv, gate_up, gains)


def update_kernel(
    got_ref, master_ref, gain_ref, first_ref, second_ref, new_first, new_second, new_master, gain_sum, packed, sums
):
    packed[...] = got_ref[...].astype(F32)
    for rank, there, here in ff_columns():
        sums[:, here : here + 44] = packed[rank, :, 384 + there : 384 + there + 44]
    master = master_ref[...]
    gain_sum[...] = jnp.sum(
        master.astype(BF).astype(F32) * sums[...], axis=1, keepdims=True
    )
    new_first[...], new_second[...], new_master[...] = adam_update(
        master,
        sums[...] * gain_ref[...],
        first_ref[...],
        second_ref[...],
        step_rates[2],
        decay_rates[2],
    )


def update_gate_up(got, master, gain, first, second):
    shape = jax.ShapeDtypeStruct((16, 2 * FF), F32)
    return pl.pallas_call(
        update_kernel,
        in_specs=[WHOLE] * 5,
        out_specs=[WHOLE] * 4,
        out_shape=[shape, shape, shape, jax.ShapeDtypeStruct((16, 1), F32)],
        scratch_shapes=[pltpu.VMEM((8, 16, 1920), F32), pltpu.VMEM((16, 2 * FF), F32)],
        compiler_params=params(32),
        cost_estimate=takes(4),
        name="update_gate_up",
    )(got, master, gain, first, second)


def shift(block, distance):
    return lax.ppermute(block, "x", [(i, (i + distance) % 4) for i in range(4)])


def swap(block):
    return lax.ppermute(block, "c", [(0, 1), (1, 0)])


ORDER = ((0, 0), (1, 0), (3, 0), (2, 0), (0, 1), (1, 1), (3, 1), (2, 1))


def tie_kernel(*refs):
    pass


def tie(value, *earlier):
    anywhere = pl.BlockSpec(memory_space=pl.ANY)
    return pl.pallas_call(
        tie_kernel,
        in_specs=[anywhere] * (1 + len(earlier)),
        out_specs=anywhere,
        out_shape=jax.ShapeDtypeStruct(value.shape, value.dtype),
        input_output_aliases={0: 0},
        cost_estimate=pl.CostEstimate(flops=0, bytes_accessed=0, transcendentals=0),
        name="tie",
    )(value, *earlier)


def gather_pieces(block, *earlier):
    mine = [block, shift(block, 1), shift(block, -1), shift(block, 2)]
    if earlier:
        mine[1] = tie(mine[1], *earlier)
    return mine + [swap(piece) for piece in mine]


def scatter_first(mine, other):
    return mine.astype(F32) + swap(other).astype(F32)


def scatter_second(mine):
    far = mine[384:].astype(BF)
    by_left = shift(far[:64], -1)
    by_right = shift(far[64:], 1)
    to_left = jnp.concatenate([mine[128:192] + by_left.astype(F32), mine[192:256]], axis=0)
    to_right = jnp.concatenate([mine[256:320], mine[320:384] + by_right.astype(F32)], axis=0)
    return to_left.astype(BF), to_right.astype(BF), mine[:128]


def scatter_third(to_left, to_right):
    return shift(to_left, -1), shift(to_right, 1)


def total(parts):
    first, second, third = parts
    return first.astype(F32) + second.astype(F32) + third.astype(F32)


def attn_grads_kernel(*refs):
    pieces = refs[:8]
    mixed_ref, out_grad_ref, sum_ref, hat, sems = refs[8:]
    copies = fetch(pieces, hat, sems)
    for r in range(16):
        for k in range(8):
            sum_ref[r, 16 * k : 16 * k + 16, 384:] = out_grad_ref[
                16 * r : 16 * r + 16, 256 * k : 256 * k + 256
            ]
    for copy in copies:
        copy.wait()
    for f in range(8):
        total = dot_tn(hat[:, 256 * f : 256 * f + 256], mixed_ref[...])
        total = total.astype(BF).reshape(4, 2, 32, 384)
        for zl in range(2):
            sum_ref[2 * f + zl, :, :384] = total[:, zl].reshape(128, 384)


def attn_grads(pieces, grad_mixed, sum_out):
    return pl.pallas_call(
        attn_grads_kernel,
        in_specs=[ANYWHERE] * 8 + [WHOLE] * 2,
        out_specs=WHOLE,
        out_shape=jax.ShapeDtypeStruct((16, 128, 640), BF),
        scratch_shapes=[pltpu.VMEM((ROWS, 2048), BF), pltpu.SemaphoreType.DMA((8,))],
        compiler_params=params(60),
        cost_estimate=takes(4),
        name="attn_grads",
    )(*pieces, grad_mixed, sum_out)


def row_positions(span_order, zl):
    x = lax.axis_index("x")
    c = lax.axis_index("c")
    holders = jnp.stack([((x - dx) % 4 * 2 + zl) * 2 + (c + dc) % 2 for dx, dc in ORDER])
    picked = (holders[:, None] == jnp.arange(16, dtype=jnp.int32)[None, :]).astype(jnp.int32)
    spans = jnp.sum(picked[:, :, None] * span_order.reshape(1, 16, 2), axis=1)
    spans = spans.T.reshape(16, 1)
    return (spans * 64 + jnp.arange(64, dtype=jnp.int32)[None, :]).reshape(ROWS)


def norm_scale(rows):
    return lax.rsqrt(jnp.mean(rows * rows, axis=-1, keepdims=True) + norm_eps)


def norm_back(grad_hat, hat, scale, rest):
    return rest + scale * (grad_hat - hat * jnp.mean(grad_hat * hat, axis=-1, keepdims=True))


def body(
    tokens,
    out_grad,
    seq_lengths,
    span_order,
    attn_in,
    attn_out,
    gate_up,
    down_proj,
    norm_gains,
    first_attn_in,
    second_attn_in,
    first_attn_out,
    second_attn_out,
    first_gate_up,
    second_gate_up,
    first_down_proj,
    second_down_proj,
    first_norm_gains,
    second_norm_gains,
):
    zl = lax.axis_index("zl")
    gains = norm_gains.astype(BF).astype(F32)
    gain_one = gains[0][:, None]
    gain_two = gains[1][:, None]
    low_qkv = attn_in.astype(BF).astype(F32)

    inputs = tokens.astype(F32)
    scale_one = norm_scale(inputs)
    hat_one = inputs * scale_one
    packed = pack(attn_in, gate_up, gains.T)
    ranked = lax.all_to_all(packed, TP, 0, 0, tiled=True).reshape(128, 1920)
    hat_pieces = gather_pieces(tie(hat_one.astype(BF), ranked))
    out_part = lax.ppermute(attn_out.astype(BF), ALL, SPREAD)
    out_part = out_part.reshape(16, 8, 256).transpose(1, 0, 2).reshape(128, 256)
    attn_part = jnp.concatenate([ranked[:, :384], out_part], axis=1)
    attn_all = lax.all_gather(attn_part, REP, axis=0, tiled=True)
    down_rows = jnp.pad(down_proj.astype(BF), ((0, 4), (0, 0)))
    down_tail = [down_rows[16 * part : 16 * part + 16, 1536:] for part in range(3)]
    ff_part = jnp.concatenate(
        [ranked[:, 384:], down_rows[:, :1536], jnp.concatenate(down_tail, axis=1)], axis=0
    )
    grad_pieces = gather_pieces(tie(out_grad, *hat_pieces[1:4]))
    ff_all = lax.all_gather(
        tie(ff_part, attn_all, *hat_pieces[1:]), REP, axis=0, tiled=True
    )

    own_pos = row_positions(span_order, zl)
    other_pos = row_positions(span_order, 1 - zl)
    lengths = seq_lengths[0]
    bound_one = lengths[0]
    bound_two = lengths[0] + lengths[1]
    low_pos = jnp.where(own_pos < bound_one, 0, bound_one)[None, :]
    high_pos = jnp.where(own_pos < bound_two, own_pos, -1)[None, :]
    key_pos = jnp.concatenate([own_pos, other_pos])
    key_pos = jnp.broadcast_to(key_pos[:, None], (KEYS, QB))

    queries, own_kv, w_qkv, w_out = project(hat_pieces, attn_all)
    other_kv = lax.ppermute(own_kv, "zl", [(0, 1), (1, 0)])
    before = attend(queries, own_kv, key_pos[:ROWS], low_pos, high_pos, None)
    att, att_early, lse = attend(
        queries, other_kv, key_pos[ROWS:], low_pos, high_pos, before, *grad_pieces[1:4]
    )
    att_other = dot_nn(att[512:], w_out).astype(BF)
    att_mine = dot_nn(att[:512], w_out)
    to_left, to_right, stays = scatter_second(scatter_first(att_mine, att_other))
    hidden = inputs + total((stays, *scatter_third(to_left, to_right)))

    scale_two = norm_scale(hidden)
    hat_two = hidden * scale_two
    hat_two_pieces = gather_pieces(hat_two.astype(BF))
    hid, grad_gu, back_mine, back_other, ahead_mine, ahead_other = feed_forward(
        hat_two_pieces, grad_pieces, ff_all
    )
    to_left, to_right, stays = scatter_second(scatter_first(back_mine, back_other))
    grad_hat_two = total((stays, *scatter_third(to_left, to_right)))
    grad_hidden = norm_back(grad_hat_two, hat_two, scale_two, out_grad.astype(F32))
    sums = weight_grads(hat_two_pieces, grad_pieces, grad_gu, hid, to_left, to_right)
    sums = sums.reshape(16 * 192, 1536)
    grad_hidden_low = tie(grad_hidden.astype(BF), sums)
    ahead = scatter_first(ahead_mine, tie(ahead_other, grad_hidden_low))
    hidden_pieces = gather_pieces(grad_hidden_low, ahead)
    sums = lax.psum_scatter(tie(sums, grad_hidden_low), REP, scatter_dimension=0, tiled=True)
    grad_att, sum_out = hidden_products(hidden_pieces, att, w_out, ahead)

    grad_q, grad_kv = attend_back(
        queries, grad_att, att_early, other_kv, key_pos[ROWS:], low_pos, high_pos, lse, None, ahead
    )
    arrived = lax.ppermute(grad_kv.astype(BF), "zl", [(0, 1), (1, 0)])
    ahead_left, ahead_right, ahead_stays = scatter_second(ahead)
    grad_q, grad_kv = attend_back(
        queries,
        grad_att,
        att_early,
        own_kv,
        key_pos[:ROWS],
        low_pos,
        high_pos,
        lse,
        grad_q,
        ahead_left,
        ahead_right,
    )
    ahead = scatter_third(ahead_left, ahead_right)
    block_out = (hidden + total((ahead_stays, *ahead))).astype(BF)
    grad_kv = (grad_kv + arrived.astype(F32)).astype(BF)
    grad_kv = grad_kv.reshape(2, 8, 64, 2 * HD).transpose(1, 0, 2, 3).reshape(ROWS, 2 * HD)
    grad_mixed = jnp.concatenate([grad_q, grad_kv], axis=1)
    grad_mixed = tie(grad_mixed, *ahead)
    attn_parts = attn_grads(hat_pieces, grad_mixed, sum_out)
    attn_sums = lax.all_to_all(attn_parts, REP, 0, 0, tiled=True)
    attn_sums = jnp.sum(attn_sums.astype(F32), axis=0).astype(BF)
    last_rows = tie(grad_mixed, attn_parts)
    last_other = dot_nt(last_rows[512:], w_qkv).astype(BF)
    last_mine = dot_nt(last_rows[:512], w_qkv)
    to_left, to_right, stays = scatter_second(scatter_first(last_mine, last_other))
    last_thirds = scatter_third(to_left, to_right)
    got = jnp.concatenate([attn_sums[:, :384], sums[:128]], axis=1).reshape(8, 16, 1920)
    grad_hat_one = total((tie(stays, got), *last_thirds))
    in_grad = norm_back(grad_hat_one, hat_one, scale_one, grad_hidden).astype(BF)
    sum_out = tie(attn_sums[:, 384:], got)
    got = lax.all_to_all(got, TP, 0, 0, tiled=True)
    got_qkv = got[:, :, :384].transpose(1, 0, 2).astype(F32)
    got_kv = got_qkv[:, :, 256:].reshape(16, 4, 2, 2, HD).sum(axis=2)
    got_qkv = jnp.concatenate(
        [
            got_qkv[:, :, :256].reshape(16, 2048),
            got_kv[:, :, 0].reshape(16, 256),
            got_kv[:, :, 1].reshape(16, 256),
        ],
        axis=1,
    )
    sum_out = sum_out.reshape(8, 16, 256).transpose(1, 0, 2).reshape(16, 2048)
    got_out = lax.ppermute(sum_out, ALL, back(SPREAD)).astype(F32)
    tail = [sums[176:192, 512 * part : 512 * part + 512] for part in range(3)]
    got_down = jnp.concatenate([sums[128:176], jnp.concatenate(tail, axis=0)], axis=1)
    got_down = got_down[:44].astype(F32)
    gu_new = update_gate_up(got, gate_up, gain_two, first_gate_up, second_gate_up)
    gain_sums = jnp.stack([jnp.sum(low_qkv * got_qkv, axis=1), gu_new[3][:, 0]], axis=0)
    qkv_new = adam_update(
        attn_in, got_qkv * gain_one, first_attn_in, second_attn_in, step_rates[0], decay_rates[0]
    )
    out_new = adam_update(
        attn_out, got_out, first_attn_out, second_attn_out, step_rates[1], decay_rates[1]
    )
    down_new = adam_update(
        down_proj, got_down, first_down_proj, second_down_proj, step_rates[3], decay_rates[3]
    )
    gains_new = adam_update(
        norm_gains, gain_sums, first_norm_gains, second_norm_gains, step_rates[4], decay_rates[4]
    )
    return (block_out, in_grad, *qkv_new, *out_new, *gu_new[:3], *down_new, *gains_new)


def solution(mesh):
    split = Mesh(mesh.devices.reshape(4, 2, 4, 2, 2), ALL)
    rows = P(ALL, None)
    cols = P(None, ALL)
    group = P(("y", "zh"), None)
    in_specs = (rows, rows, group, P()) + (rows,) * 4 + (cols,) + (rows,) * 8 + (cols,) * 2
    out_specs = (rows,) * 14 + (cols,) * 3
    return jax.shard_map(body, mesh=split, in_specs=in_specs, out_specs=out_specs, check_vma=False)
```
